32 devices in a mesh: seq: 16 (over z, y, x), chan: 2 (over core).
Axes of the slice: x: 2, y: 2, z: 4, core: 2. Of those that a mesh axis runs over, the one named last changes fastest.
Arguments:
- query_in: bfloat16 [2048, 2048], P('chan', 'seq'), may hold values from -6 to 6
- key_in: bfloat16 [2048, 2048], P('chan', 'seq'), may hold values from -6 to 6
- value_in: bfloat16 [2048, 2048], P('chan', 'seq'), may hold values from -6 to 6
- short_weight: float32 [3, 7, 2048], P(None, None, 'chan'), may hold values from -2 to 2
- residue: float32 [2048, 16], P(('chan', 'seq')), may hold values from -1.5 to 1.5
- log_rate: float32 [2048, 16], P(('chan', 'seq')), may hold values from -13 to -3.2
- grad_out: bfloat16 [2048, 2048], P('chan', 'seq'), may hold values from -6 to 6
Outputs:
- output: bfloat16 [2048, 2048], P('chan', 'seq')
- grad_query: bfloat16 [2048, 2048], P('chan', 'seq')
- grad_key: bfloat16 [2048, 2048], P('chan', 'seq')
- grad_value: bfloat16 [2048, 2048], P('chan', 'seq')
- grad_short: float32 [3, 7, 2048], P(None, None, 'chan')
- grad_residue: float32 [2048, 16], P(('chan', 'seq'))
- grad_log_rate: float32 [2048, 16], P(('chan', 'seq'))
The draws below stay inside these ranges and needn't reach their ends.
All inputs are finite; a program needn't handle non-finite values.
Results may differ from the reference program's by a relative error of at most 0.008.
Values may be sent and summed in bfloat16 or wider, within the bound.
A program may use at most 64 MiB of HBM per device.

```python
import math
import jax
import jax.numpy as jnp
from jax import lax

D = 2048
MODES = 16
LENGTH = 2048


def levels(own_key, extent, pieces, least, top_value):
    level, own = 1.0, jax.random.fold_in(own_key, 6)
    for position, blocks in pieces:
        heights = jnp.exp(jax.random.uniform(jax.random.fold_in(own, position), (blocks,), jnp.float32, least / len(pieces), top_value / len(pieces)))
        level = level * jnp.repeat(heights, extent[position] // blocks).reshape([-1 if axis == position else 1 for axis in range(len(extent))])
    return level


def scatter_about(own_key, shape, spread, bound, split=(), held_as=jnp.bfloat16):
    values = jax.random.normal(own_key, shape, jnp.float32) * spread
    if len(split) > 0:
        values = levels(own_key, shape, split, -0.22, 0.18) * values
    return jnp.clip(values, min=-bound, max=bound).astype(held_as)


def setup_inputs(seed: int = 0) -> dict:
    seeds = jax.random.split(jax.random.key(seed), 8)
    return {
        "query_in": scatter_about(seeds[0], (D, LENGTH), 1.0, 6.0, ((0, 2), (1, 16))),
        "key_in": scatter_about(seeds[1], (D, LENGTH), 1.0, 6.0, ((0, 2), (1, 16))),
        "value_in": scatter_about(seeds[2], (D, LENGTH), 1.0, 6.0, ((0, 2), (1, 16))),
        "short_weight": scatter_about(seeds[3], (3, 7, D), 7 ** -0.5, 2.0, ((2, 2),), jnp.float32),
        "residue": scatter_about(seeds[4], (D, MODES), MODES ** -0.5, 1.5, ((0, 32),), jnp.float32),
        "log_rate": jnp.clip(-13.0 + 9.8 * jax.random.uniform(seeds[5], (D, MODES), jnp.float32) ** levels(seeds[5], (D, MODES), ((0, 32),), -0.2, 0.2), -13.0, -3.2),
        "grad_out": scatter_about(seeds[6], (D, LENGTH), 1.0, 6.0, ((0, 2), (1, 16))),
    }


def causal_taps(signal, taps):
    length = signal.shape[1]
    padded = jnp.pad(signal, ((0, 0), (6, 0)))
    total = jnp.zeros_like(signal)
    for offset in range(7):
        total = total + taps[offset][:, None] * padded[:, 6 - offset:6 - offset + length]
    return total

def causal_taps_back(gradient, taps):
    length = gradient.shape[1]
    padded = jnp.pad(gradient, ((0, 0), (0, 6)))
    total = jnp.zeros_like(gradient)
    for offset in range(7):
        total = total + taps[offset][:, None] * padded[:, offset:offset + length]
    return total

def taps_gradient(gradient, signal):
    length = signal.shape[1]
    padded = jnp.pad(signal, ((0, 0), (6, 0)))
    rows_out = [lax.optimization_barrier(jnp.sum(gradient * padded[:, 6 - offset:6 - offset + length], axis=1)) for offset in range(7)]
    return jnp.stack(rows_out, axis=0)

def modal_filter(residue, log_rate, length):
    decay_rate = jnp.exp(log_rate)
    offsets = jnp.arange(length).astype(residue.dtype)
    filt = jnp.zeros((residue.shape[0], length), residue.dtype)
    for mode_index in range(residue.shape[1]):
        factor = residue[:, mode_index] * jnp.sqrt(2.0 * decay_rate[:, mode_index])
        filt = filt + factor[:, None] * jnp.exp(-decay_rate[:, mode_index][:, None] * offsets)
    return filt

def modal_grads(filt_grad, residue, log_rate):
    decay_rate = jnp.exp(log_rate)
    offsets = jnp.arange(filt_grad.shape[1]).astype(residue.dtype)
    res_terms = []
    log_terms = []
    for mode_index in range(residue.shape[1]):
        rate_col = decay_rate[:, mode_index][:, None]
        basis = jnp.sqrt(2.0 * rate_col) * jnp.exp(-rate_col * offsets)
        weighted = filt_grad * basis
        res_terms.append(lax.optimization_barrier(jnp.sum(weighted, axis=1)))
        log_terms.append(residue[:, mode_index] * lax.optimization_barrier(jnp.sum(weighted * (0.5 - rate_col * offsets), axis=1)))
    return (jnp.stack(res_terms, axis=1), jnp.stack(log_terms, axis=1))

def long_block(items):
    mixed_blk, grad_blk, residue_blk, rate_blk = items
    length = mixed_blk.shape[1]
    fft_len = 2 * length
    filt = modal_filter(residue_blk, rate_blk, length)
    spec_mixed = jnp.fft.rfft(mixed_blk, n=fft_len, axis=1)
    spec_filter = jnp.fft.rfft(filt, n=fft_len, axis=1)
    spec_grad = jnp.fft.rfft(grad_blk, n=fft_len, axis=1)
    long_out = jnp.fft.irfft(spec_mixed * spec_filter, n=fft_len, axis=1)[:, :length]
    long_grad = jnp.fft.irfft(spec_grad * jnp.conj(spec_filter), n=fft_len, axis=1)[:, :length]
    filt_grad = jnp.fft.irfft(spec_grad * jnp.conj(spec_mixed), n=fft_len, axis=1)[:, :length]
    grad_res, grad_log = modal_grads(filt_grad, residue_blk, rate_blk)
    return (long_out.astype(jnp.bfloat16), long_grad.astype(jnp.bfloat16), grad_res, grad_log)

def reference(query_in, key_in, value_in, short_weight, residue, log_rate, grad_out):
    width, length = query_in.shape
    query_wide = query_in.astype(jnp.float32)
    key_wide = key_in.astype(jnp.float32)
    value_wide = value_in.astype(jnp.float32)
    query_hat = causal_taps(query_wide, short_weight[0])
    key_hat = causal_taps(key_wide, short_weight[1])
    value_hat = causal_taps(value_wide, short_weight[2])
    mixed = (key_hat * value_hat).astype(jnp.bfloat16)
    grad_up = grad_out.astype(jnp.float32)
    grad_mixed = (grad_up * query_hat).astype(jnp.bfloat16)
    blocks = 16
    per_block = width // blocks
    long_out, long_grad, grad_res, grad_log = lax.map(long_block, (mixed.astype(jnp.float32).reshape(blocks, per_block, length), grad_mixed.astype(jnp.float32).reshape(blocks, per_block, length), residue.reshape(blocks, per_block, residue.shape[1]), log_rate.reshape(blocks, per_block, residue.shape[1])))
    long_out = long_out.reshape(width, length).astype(jnp.float32)
    long_grad = long_grad.reshape(width, length).astype(jnp.float32)
    scale = 1.0 / math.sqrt(length)
    grad_residue = grad_res.reshape(width, -1) * scale
    grad_log_rate = grad_log.reshape(width, -1) * scale
    output = (query_hat * long_out).astype(jnp.bfloat16)
    grad_q = grad_up * long_out
    grad_k = long_grad * value_hat
    grad_v = long_grad * key_hat
    grad_query = causal_taps_back(grad_q, short_weight[0]).astype(jnp.bfloat16)
    grad_key = causal_taps_back(grad_k, short_weight[1]).astype(jnp.bfloat16)
    grad_value = causal_taps_back(grad_v, short_weight[2]).astype(jnp.bfloat16)
    grad_short = jnp.stack([taps_gradient(grad_q, query_wide), taps_gradient(grad_k, key_wide), taps_gradient(grad_v, value_wide)], axis=0) * scale
    return (output, grad_query, grad_key, grad_value, grad_short, grad_residue, grad_log_rate)
```

```python
import functools
import math

import jax
import jax.numpy as jnp
from jax import lax
from jax.experimental import pallas as pl
from jax.experimental.pallas import tpu as pltpu
from jax.sharding import PartitionSpec as P


def shifted(shard, axis, by):
    count = lax.axis_size(axis)
    pairs = [(i, i + by) for i in range(count) if 0 <= i + by < count]
    return lax.ppermute(shard, axis, pairs)


def dft_table(length, sign):
    counter = jnp.arange(length, dtype=jnp.int32)
    product = counter[:, None] * counter[None, :] % length
    angle = product.astype(jnp.float32) * (sign * 2.0 * math.pi / length)
    return (jnp.cos(angle), jnp.sin(angle))


def complex_dot(real_part, imag_part, table_real, table_imag):
    highest = lax.Precision.HIGHEST
    out_real = jnp.matmul(real_part, table_real, precision=highest) - jnp.matmul(
        imag_part, table_imag, precision=highest
    )
    out_imag = jnp.matmul(real_part, table_imag, precision=highest) + jnp.matmul(
        imag_part, table_real, precision=highest
    )
    return (out_real, out_imag)


def transform(real_part, imag_part, sign):
    length = real_part.shape[-1]
    if length <= 256 or length % 128 != 0:
        table_real, table_imag = dft_table(length, sign)
        return complex_dot(real_part, imag_part, table_real, table_imag)
    outer = 128
    inner = length // outer
    leading = real_part.shape[:-1]
    split_real = jnp.swapaxes(real_part.reshape(leading + (inner, outer)), -1, -2)
    split_imag = jnp.swapaxes(imag_part.reshape(leading + (inner, outer)), -1, -2)
    part_real, part_imag = transform(split_real, split_imag, sign)
    first_index = jnp.arange(outer, dtype=jnp.int32)[:, None]
    second_index = jnp.arange(inner, dtype=jnp.int32)[None, :]
    angle = (first_index * second_index % length).astype(jnp.float32) * (
        sign * 2.0 * math.pi / length
    )
    twist_real = jnp.cos(angle)
    twist_imag = jnp.sin(angle)
    turned_real = part_real * twist_real - part_imag * twist_imag
    turned_imag = part_real * twist_imag + part_imag * twist_real
    table_real, table_imag = dft_table(outer, sign)
    highest = lax.Precision.HIGHEST
    out_real = jnp.einsum(
        "...nk,nl->...lk", turned_real, table_real, precision=highest
    ) - jnp.einsum("...nk,nl->...lk", turned_imag, table_imag, precision=highest)
    out_imag = jnp.einsum(
        "...nk,nl->...lk", turned_real, table_imag, precision=highest
    ) + jnp.einsum("...nk,nl->...lk", turned_imag, table_real, precision=highest)
    return (out_real.reshape(leading + (length,)), out_imag.reshape(leading + (length,)))


def spectrum(signal):
    length = signal.shape[1]
    padded = jnp.pad(signal.astype(jnp.float32), ((0, 0), (0, length)))
    return transform(padded, jnp.zeros_like(padded), -1.0)


def mirrored(values):
    return jnp.roll(jnp.flip(values, -1), 1, -1)


def paired_spectra(first, second):
    length = first.shape[1]
    first_pad = jnp.pad(first, ((0, 0), (0, length)))
    second_pad = jnp.pad(second.astype(jnp.float32), ((0, 0), (0, length)))
    joint_real, joint_imag = transform(first_pad, second_pad, -1.0)
    mirror_real = mirrored(joint_real)
    mirror_imag = mirrored(joint_imag)
    first_spec = (0.5 * (joint_real + mirror_real), 0.5 * (joint_imag - mirror_imag))
    second_spec = (0.5 * (joint_imag + mirror_imag), -0.5 * (joint_real - mirror_real))
    return (first_spec, second_spec)


def to_time(spec_pair, length):
    real_part, imag_part = spec_pair
    back_real, back_imag = transform(real_part, imag_part, 1.0)
    return back_real[:, :length] / real_part.shape[-1]


def paired_time(first_spec, second_spec, length):
    joint_real = first_spec[0] - second_spec[1]
    joint_imag = first_spec[1] + second_spec[0]
    back_real, back_imag = transform(joint_real, joint_imag, 1.0)
    total_len = joint_real.shape[-1]
    return (back_real[:, :length] / total_len, back_imag[:, :length] / total_len)


def spectral_product(first, second, conjugate):
    first_real, first_imag = first
    second_real, second_imag = second
    if conjugate:
        second_imag = -second_imag
    return (
        first_real * second_real - first_imag * second_imag,
        first_real * second_imag + first_imag * second_real,
    )


def modal_filter(residue, log_rate, length):
    decay_rate = jnp.exp(log_rate)
    offsets = jnp.arange(length).astype(jnp.float32)
    filt = jnp.zeros((residue.shape[0], length), jnp.float32)
    for mode_index in range(residue.shape[1]):
        factor = residue[:, mode_index] * jnp.sqrt(2.0 * decay_rate[:, mode_index])
        filt = filt + factor[:, None] * jnp.exp(-decay_rate[:, mode_index][:, None] * offsets)
    return filt


def modal_grads(filt_grad, residue, log_rate):
    decay_rate = jnp.exp(log_rate)
    offsets = jnp.arange(filt_grad.shape[1]).astype(jnp.float32)
    res_terms = []
    log_terms = []
    for mode_index in range(residue.shape[1]):
        rate_col = decay_rate[:, mode_index][:, None]
        basis = jnp.sqrt(2.0 * rate_col) * jnp.exp(-rate_col * offsets)
        weighted = filt_grad * basis
        res_terms.append(jnp.sum(weighted, axis=1))
        log_terms.append(
            residue[:, mode_index] * jnp.sum(weighted * (0.5 - rate_col * offsets), axis=1)
        )
    return (jnp.stack(res_terms, axis=1), jnp.stack(log_terms, axis=1))


def apply_taps(widened, taps, tok_rows):
    total = jnp.zeros((widened.shape[0], tok_rows), jnp.float32)
    for offset in range(7):
        total = total + taps[offset][:, None] * widened[:, 6 - offset : 6 - offset + tok_rows]
    return total


def taps_back(gradient, following, taps):
    tok_rows = gradient.shape[1]
    widened = jnp.concatenate([gradient, following], axis=1)
    total = jnp.zeros_like(gradient)
    for offset in range(7):
        total = total + taps[offset][:, None] * widened[:, offset : offset + tok_rows]
    return total


def taps_gradient(gradient, widened):
    tok_rows = gradient.shape[1]
    rows_out = [
        jnp.sum(gradient * widened[:, 6 - offset : 6 - offset + tok_rows], axis=1)
        for offset in range(7)
    ]
    return jnp.stack(rows_out, axis=0)


def to_channels(stream):
    return lax.all_to_all(stream, "seq", split_axis=0, concat_axis=1, tiled=True)


def to_tokens(stream):
    return lax.all_to_all(stream, "seq", split_axis=1, concat_axis=0, tiled=True)


def local_fft(query_in, key_in, value_in, short_weight, residue, log_rate, grad_out):
    tok_rows = query_in.shape[1]
    length = tok_rows * lax.axis_size("seq")
    scale = 1.0 / math.sqrt(length)
    tails = shifted((query_in[:, -6:], key_in[:, -6:], value_in[:, -6:]), "seq", 1)
    query_wide = jnp.concatenate([tails[0], query_in], axis=1).astype(jnp.float32)
    key_wide = jnp.concatenate([tails[1], key_in], axis=1).astype(jnp.float32)
    value_wide = jnp.concatenate([tails[2], value_in], axis=1).astype(jnp.float32)
    query_hat = apply_taps(query_wide, short_weight[0], tok_rows)
    key_hat = apply_taps(key_wide, short_weight[1], tok_rows)
    value_hat = apply_taps(value_wide, short_weight[2], tok_rows)
    mixed = (key_hat * value_hat).astype(jnp.bfloat16)
    grad_up = grad_out.astype(jnp.float32)
    grad_mixed = (grad_up * query_hat).astype(jnp.bfloat16)
    mixed_cols = to_channels(mixed)
    filt = modal_filter(residue, log_rate, length)
    spec_filter, spec_mixed = paired_spectra(filt, mixed_cols)
    long_out = to_time(spectral_product(spec_mixed, spec_filter, False), length).astype(
        jnp.bfloat16
    )
    conv_out = to_tokens(long_out)
    grad_cols = to_channels(grad_mixed)
    spec_grad = spectrum(grad_cols)
    long_grad, filt_grad = paired_time(
        spectral_product(spec_grad, spec_filter, True),
        spectral_product(spec_grad, spec_mixed, True),
        length,
    )
    conv_grad = to_tokens(long_grad.astype(jnp.bfloat16))
    grad_res, grad_log = modal_grads(filt_grad, residue, log_rate)
    conv_wide = conv_out.astype(jnp.float32)
    conv_grad_wide = conv_grad.astype(jnp.float32)
    output = (query_hat * conv_wide).astype(jnp.bfloat16)
    grad_q = grad_up * conv_wide
    grad_k = conv_grad_wide * value_hat
    grad_v = conv_grad_wide * key_hat
    heads = shifted((grad_q[:, :6], grad_k[:, :6], grad_v[:, :6]), "seq", -1)
    grad_query = taps_back(grad_q, heads[0], short_weight[0]).astype(jnp.bfloat16)
    grad_key = taps_back(grad_k, heads[1], short_weight[1]).astype(jnp.bfloat16)
    grad_value = taps_back(grad_v, heads[2], short_weight[2]).astype(jnp.bfloat16)
    local_terms = jnp.stack(
        [
            taps_gradient(grad_q, query_wide),
            taps_gradient(grad_k, key_wide),
            taps_gradient(grad_v, value_wide),
        ],
        axis=0,
    )
    grad_short = lax.psum(local_terms, "seq") * scale
    return (
        output,
        grad_query,
        grad_key,
        grad_value,
        grad_short,
        grad_res * scale,
        grad_log * scale,
    )


SUB = 8
LANE = 128
HALO = 6
TAPS = 7
GROUP = 8
MESH = pl.DeviceIdType.MESH


def slab(index):
    return pl.ds(pl.multiple_of(index * SUB, SUB), SUB)


def layer_kernel(
    n, modes, tokens, scale,
    query_ref, key_ref, value_ref, grad_ref, weight_ref, param_ref,
    out_ref, gq_ref, gk_ref, gv_ref, short_ref, modal_ref,
    streams, hats, mixed, gmixed, conv, conv_back, prod, cots,
    params, decay, gain, rate,
    fwd_send, fwd_recv, bwd_send, bwd_recv, acc_send, acc_recv,
    carry_send, carry_recv, modal_send, modal_recv,
    short_send, short_recv, total_send, total_recv,
    send_sem, recv_sem, halo_send, halo_recv,
):
    me = lax.axis_index("seq")
    extent = tokens + HALO
    f32 = jnp.float32
    zero = jnp.zeros((SUB, LANE), f32)

    def rounded(value):
        return value.astype(jnp.bfloat16).astype(f32)

    def exchange(phase, k, source, target):
        peer = lax.rem(me + k, n)
        return pltpu.make_async_remote_copy(
            src_ref=source(peer),
            dst_ref=target(me),
            send_sem=send_sem.at[phase, k],
            recv_sem=recv_sem.at[phase, k],
            device_id={"seq": peer},
            device_id_type=MESH,
        )

    def start_all(phase, source, target):
        def step(k, carry):
            exchange(phase, k, source, target).start()
            return carry

        lax.fori_loop(1, n, step, 0)

    def wait_all(phase, source, target):
        def step(k, carry):
            exchange(phase, k, source, target).wait()
            return carry

        lax.fori_loop(1, n, step, 0)

    barrier = pltpu.get_barrier_semaphore()

    def greet(k, carry):
        pl.semaphore_signal(
            barrier, inc=1, device_id={"seq": lax.rem(me + k, n)}, device_id_type=MESH
        )
        return carry

    lax.fori_loop(1, n, greet, 0)

    ins = (query_ref, key_ref, value_ref, grad_ref)
    for s in range(4):
        for b in range(SUB):
            block = ins[s][b * LANE : (b + 1) * LANE, :].astype(f32)
            streams[s, pl.ds(HALO * SUB + b, tokens, stride=SUB), :] = block.T

    pl.semaphore_wait(barrier, n - 1)

    edge = HALO * SUB
    last = tokens * SUB
    to_right = lambda: pltpu.make_async_remote_copy(
        src_ref=streams.at[pl.ds(0, 3), pl.ds(last, edge)],
        dst_ref=streams.at[pl.ds(0, 3), pl.ds(0, edge)],
        send_sem=halo_send.at[0],
        recv_sem=halo_recv.at[0],
        device_id={"seq": lax.rem(me + 1, n)},
        device_id_type=MESH,
    )
    to_left = lambda: pltpu.make_async_remote_copy(
        src_ref=streams.at[:, pl.ds(edge, edge)],
        dst_ref=streams.at[:, pl.ds(edge + last, edge)],
        send_sem=halo_send.at[1],
        recv_sem=halo_recv.at[1],
        device_id={"seq": lax.rem(me + n - 1, n)},
        device_id_type=MESH,
    )

    @pl.when(me < n - 1)
    def _():
        to_right().start()

    @pl.when(me > 0)
    def _():
        to_left().start()

    @pl.when(me == 0)
    def _():
        streams[0:3, 0:edge, :] = jnp.zeros((3, edge, LANE), f32)

    @pl.when(me == n - 1)
    def _():
        streams[:, edge + last : 2 * edge + last, :] = jnp.zeros((4, edge, LANE), f32)

    own_rows = pl.ds(pl.multiple_of(me * modes, modes), modes)
    par_src = lambda peer: param_ref
    par_dst = lambda owner: params.at[pl.ds(pl.multiple_of(owner * modes, modes), modes)]
    start_all(0, par_src, par_dst)
    params[own_rows, :] = param_ref[...]

    taps = [[weight_ref[s * TAPS + j] for j in range(TAPS)] for s in range(3)]

    def filter_token(t):
        vals = []
        for s in range(3):
            total = taps[s][0] * streams[s, slab(t + HALO), :]
            for j in range(1, TAPS):
                total = total + taps[s][j] * streams[s, slab(t + HALO - j), :]
            hats[s, slab(t), :] = total
            vals.append(total)
        mixed[slab(t), :] = rounded(vals[1] * vals[2])
        gmixed[slab(t), :] = rounded(vals[0] * streams[3, slab(t + HALO), :])

    def token_loop(lo, hi, unroll, fn):
        def step(i, carry):
            for u in range(unroll):
                fn(lo + i * unroll + u)
            return carry

        lax.fori_loop(0, (hi - lo) // unroll, step, 0)

    token_loop(HALO, tokens, 2, filter_token)

    @pl.when(me > 0)
    def _():
        to_left().wait_send()
        to_right().wait_recv()

    @pl.when(me < n - 1)
    def _():
        to_right().wait_send()
        to_left().wait_recv()

    token_loop(0, HALO, 2, filter_token)
    token_loop(tokens, extent, 2, filter_token)

    wait_all(0, par_src, par_dst)
    low_half = lax.broadcasted_iota(jnp.int32, (SUB, LANE), 1) < LANE // 2
    for m in range(modes):
        even = params[pl.ds(m, SUB, stride=2 * modes), :]
        odd = params[pl.ds(modes + m, SUB, stride=2 * modes), :]
        log_rate = jnp.where(low_half, even, pltpu.roll(odd, LANE // 2, 1))
        residue = jnp.where(low_half, pltpu.roll(even, LANE // 2, 1), odd)
        r = jnp.exp(log_rate)
        rate[slab(m), :] = r
        decay[slab(m), :] = jnp.exp(-r)
        gain[slab(m), :] = residue * jnp.sqrt(2.0 * r)

    UN = 4
    for first in range(0, modes, GROUP):
        group = range(first, first + GROUP)

        def fwd_step(i, carry, first=first, group=group):
            x, y, ax, ay = [list(c) for c in carry]
            for u in range(UN):
                t = i * UN + u
                value = mixed[slab(t), :]
                cot = gmixed[slab(t), :]
                total = conv[slab(t), :] if first else zero
                for p, m in enumerate(group):
                    a = decay[m * SUB : (m + 1) * SUB, :]
                    y[p] = a * (y[p] + x[p])
                    x[p] = a * x[p] + value
                    total = total + gain[m * SUB : (m + 1) * SUB, :] * x[p]
                    ax[p] = ax[p] + cot * x[p]
                    ay[p] = ay[p] + cot * y[p]
                conv[slab(t), :] = total
            return tuple(tuple(c) for c in (x, y, ax, ay))

        zeros = tuple(zero for _ in group)
        x, y, ax, ay = lax.fori_loop(0, tokens // UN, fwd_step, (zeros,) * 4)
        for p, m in enumerate(group):
            fwd_send[m, 0:SUB, :] = x[p]
            fwd_send[m, SUB : 2 * SUB, :] = y[p]
            acc_send[m, 0:SUB, :] = ax[p]
            acc_send[m, SUB : 2 * SUB, :] = ay[p]
        x = list(x)
        for t in range(tokens, extent):
            value = mixed[t * SUB : (t + 1) * SUB, :]
            total = conv[t * SUB : (t + 1) * SUB, :] if first else zero
            for p, m in enumerate(group):
                x[p] = decay[m * SUB : (m + 1) * SUB, :] * x[p] + value
                total = total + gain[m * SUB : (m + 1) * SUB, :] * x[p]
            conv[t * SUB : (t + 1) * SUB, :] = total

    fwd_src = lambda peer: fwd_send.at[peer]
    fwd_dst = lambda owner: fwd_recv.at[owner]
    start_all(1, fwd_src, fwd_dst)

    for first in range(0, modes, GROUP):
        group = range(first, first + GROUP)

        def bwd_step(i, carry, first=first, group=group):
            z, w = [list(c) for c in carry]
            for u in range(UN):
                t = tokens - 1 - (i * UN + u)
                cot = gmixed[slab(t), :]
                total = conv_back[slab(t), :] if first else zero
                for p, m in enumerate(group):
                    a = decay[m * SUB : (m + 1) * SUB, :]
                    z[p] = a * z[p] + cot
                    w[p] = a * w[p] + z[p]
                    total = total + gain[m * SUB : (m + 1) * SUB, :] * z[p]
                conv_back[slab(t), :] = total
            return tuple(tuple(c) for c in (z, w))

        zeros = tuple(zero for _ in group)
        z, w = lax.fori_loop(0, tokens // UN, bwd_step, (zeros,) * 2)
        for p, m in enumerate(group):
            bwd_send[m, 0:SUB, :] = z[p]
            bwd_send[m, SUB : 2 * SUB, :] = w[p]

    bwd_src = lambda peer: bwd_send.at[peer]
    bwd_dst = lambda owner: bwd_recv.at[owner]
    start_all(2, bwd_src, bwd_dst)
    acc_src = lambda peer: acc_send.at[peer]
    acc_dst = lambda owner: acc_recv.at[owner]
    start_all(3, acc_src, acc_dst)

    fwd_recv[me] = fwd_send[me]
    bwd_recv[me] = bwd_send[me]
    acc_recv[me] = acc_send[me]
    my_rate = rate[slab(me), :]
    my_decay = decay[slab(me), :]
    my_gain = gain[slab(me), :]
    whole = jnp.exp(-float(tokens) * my_rate)
    wait_all(1, fwd_src, fwd_dst)

    def scan_fwd(d, h):
        carry_send[d, 0:SUB, :] = h
        return whole * h + fwd_recv[d, 0:SUB, :]

    lax.fori_loop(0, n, scan_fwd, zero)
    wait_all(2, bwd_src, bwd_dst)

    def scan_bwd(i, z):
        d = n - 1 - i
        carry_send[d, SUB : 2 * SUB, :] = z
        return whole * z + bwd_recv[d, 0:SUB, :]

    lax.fori_loop(0, n, scan_bwd, zero)
    carry_src = lambda peer: carry_send.at[peer]
    carry_dst = lambda owner: carry_recv.at[owner]
    start_all(4, carry_src, carry_dst)
    carry_recv[me] = carry_send[me]

    wait_all(3, acc_src, acc_dst)

    def scan_acc(d, carry):
        hy, acc_x, acc_y = carry
        h = carry_send[d, 0:SUB, :]
        z0 = my_decay * bwd_recv[d, 0:SUB, :]
        z1 = my_decay * bwd_recv[d, SUB : 2 * SUB, :]
        acc_x = acc_x + (acc_recv[d, 0:SUB, :] + h * z0)
        acc_y = acc_y + (acc_recv[d, SUB : 2 * SUB, :] + h * z1 + hy * z0)
        hy = whole * (hy + float(tokens) * h) + fwd_recv[d, SUB : 2 * SUB, :]
        return hy, acc_x, acc_y

    _, acc_x, acc_y = lax.fori_loop(0, n, scan_acc, (zero, zero, zero))
    modal_send[0:SUB, :] = acc_x * jnp.sqrt(2.0 * my_rate) * scale
    modal_send[SUB : 2 * SUB, :] = my_gain * (0.5 * acc_x - my_rate * acc_y) * scale
    modal_src = lambda peer: modal_send
    modal_dst = lambda owner: modal_recv.at[owner]
    start_all(5, modal_src, modal_dst)
    modal_recv[me] = modal_send[...]

    wait_all(4, carry_src, carry_dst)

    def finish_fwd(t, c):
        c = [decay[m * SUB : (m + 1) * SUB, :] * c[m] for m in range(modes)]
        parts = c
        while len(parts) > 1:
            parts = [parts[i] + parts[i + 1] for i in range(0, len(parts), 2)]
        total = rounded(conv[slab(t), :] + parts[0])
        prod[slab(t), :] = hats[0, slab(t), :] * total
        cots[0, slab(t), :] = streams[3, slab(t + HALO), :] * total
        return c

    def fwd_two(i, c):
        c = list(c)
        for u in range(2):
            c = finish_fwd(i * 2 + u, c)
        return tuple(c)

    start = tuple(
        gain[m * SUB : (m + 1) * SUB, :] * carry_recv[m, 0:SUB, :] for m in range(modes)
    )
    lax.fori_loop(0, extent // 2, fwd_two, start)

    def store_back(t, total):
        total = rounded(total)
        cots[1, slab(t), :] = hats[2, slab(t), :] * total
        cots[2, slab(t), :] = hats[1, slab(t), :] * total

    def bwd_two(i, c):
        c = list(c)
        for u in range(2):
            t = tokens - 1 - (i * 2 + u)
            c = [decay[m * SUB : (m + 1) * SUB, :] * c[m] for m in range(modes)]
            parts = c
            while len(parts) > 1:
                parts = [parts[k] + parts[k + 1] for k in range(0, len(parts), 2)]
            store_back(t, conv_back[slab(t), :] + parts[0])
        return tuple(c)

    start = tuple(
        gain[m * SUB : (m + 1) * SUB, :] * carry_recv[m, SUB : 2 * SUB, :]
        for m in range(modes)
    )
    lax.fori_loop(0, tokens // 2, bwd_two, start)

    for h in range(HALO):
        conv_back[(tokens + h) * SUB : (tokens + h + 1) * SUB, :] = zero
    for m in range(modes):
        grow = jnp.exp(rate[m * SUB : (m + 1) * SUB, :])
        z = carry_recv[m, SUB : 2 * SUB, :]
        weight = gain[m * SUB : (m + 1) * SUB, :]
        for h in range(HALO):
            rows = slice((tokens + h) * SUB, (tokens + h + 1) * SUB)
            conv_back[rows, :] = conv_back[rows, :] + weight * z
            z = grow * (z - gmixed[rows, :])
    for h in range(HALO):
        t = tokens + h
        store_back(t, conv_back[t * SUB : (t + 1) * SUB, :])

    def short_step(i, accs):
        accs = list(accs)
        for u in range(2):
            t = i * 2 + u
            for s in range(3):
                cot = cots[s, slab(t), :]
                for j in range(TAPS):
                    at = s * TAPS + j
                    accs[at] = accs[at] + cot * streams[s, slab(t + HALO - j), :]
        return tuple(accs)

    accs = lax.fori_loop(0, tokens // 2, short_step, (zero,) * (3 * TAPS))
    for row in range(2 * n):
        short_send[row // 2, (row % 2) * SUB : (row % 2 + 1) * SUB, :] = (
            accs[row] if row < 3 * TAPS else zero
        )
    short_src = lambda peer: short_send.at[peer]
    short_dst = lambda owner: short_recv.at[owner]
    start_all(6, short_src, short_dst)
    short_recv[me] = short_send[me]

    def taps_step(t):
        for s in range(3):
            total = taps[s][0] * cots[s, slab(t), :]
            for j in range(1, TAPS):
                total = total + taps[s][j] * cots[s, slab(t + j), :]
            hats[s, slab(t), :] = total

    token_loop(0, tokens, 2, taps_step)

    wait_all(6, short_src, short_dst)
    total = short_recv[0]
    for d in range(1, n):
        total = total + short_recv[d]
    total_send[...] = total * scale
    total_src = lambda peer: total_send
    total_dst = lambda owner: total_recv.at[owner]
    start_all(7, total_src, total_dst)
    total_recv[me] = total_send[...]

    for b in range(SUB):
        rows = slice(b * LANE, (b + 1) * LANE)
        out_ref[rows, :] = prod[pl.ds(b, tokens, stride=SUB), :].T.astype(jnp.bfloat16)
    for s, ref in enumerate((gq_ref, gk_ref, gv_ref)):
        for b in range(SUB):
            rows = slice(b * LANE, (b + 1) * LANE)
            ref[rows, :] = hats[s, pl.ds(b, tokens, stride=SUB), :].T.astype(jnp.bfloat16)

    wait_all(5, modal_src, modal_dst)
    modal_ref[...] = modal_recv[...]
    wait_all(7, total_src, total_dst)
    short_ref[...] = total_recv[...]


def local(query_in, key_in, value_in, short_weight, residue, log_rate, grad_out):
    n = lax.axis_size("seq")
    width, tokens = query_in.shape
    own, modes = residue.shape
    fits = width == SUB * LANE and tokens == LANE and modes == n == 2 * SUB
    if not (fits and own == LANE // 2):
        return local_fft(
            query_in, key_in, value_in, short_weight, residue, log_rate, grad_out
        )
    scale = 1.0 / math.sqrt(tokens * n)
    f32 = jnp.float32
    rows = (tokens + HALO) * SUB
    weight = short_weight.reshape(3 * TAPS, SUB, LANE)
    param = jnp.concatenate([log_rate.T, residue.T], axis=1)
    vmem = pl.BlockSpec(memory_space=pltpu.VMEM)
    stage = pltpu.VMEM((n, 2 * SUB, LANE), f32)
    flat = pltpu.VMEM((rows, LANE), f32)
    small = pltpu.VMEM((modes * SUB, LANE), f32)
    shape = jax.ShapeDtypeStruct((width, tokens), jnp.bfloat16)
    table = jax.ShapeDtypeStruct((n, 2 * SUB, LANE), f32)
    out, gq, gk, gv, short, modal = pl.pallas_call(
        functools.partial(layer_kernel, n, modes, tokens, scale),
        out_shape=(shape, shape, shape, shape, table, table),
        in_specs=[vmem] * 6,
        out_specs=(vmem,) * 6,
        scratch_shapes=[
            pltpu.VMEM((4, rows + HALO * SUB, LANE), f32),
            pltpu.VMEM((3, rows, LANE), f32),
            flat, flat, flat, flat, flat,
            pltpu.VMEM((3, rows, LANE), f32),
            pltpu.VMEM((n * modes, LANE), f32),
            small, small, small,
            stage, stage, stage, stage, stage, stage,
            stage, stage, pltpu.VMEM((2 * SUB, LANE), f32), stage,
            stage, stage, pltpu.VMEM((2 * SUB, LANE), f32), stage,
            pltpu.SemaphoreType.DMA((8, n)),
            pltpu.SemaphoreType.DMA((8, n)),
            pltpu.SemaphoreType.DMA((2,)),
            pltpu.SemaphoreType.DMA((2,)),
        ],
        compiler_params=pltpu.CompilerParams(
            collective_id=0, has_side_effects=True, vmem_limit_bytes=40 * 2**20
        ),
    )(query_in, key_in, value_in, grad_out, weight, param)
    short = short.reshape(2 * n, width)[: 3 * TAPS].reshape(3, TAPS, width)
    modal = modal.reshape(modes, 2, width)
    mine = lax.dynamic_slice_in_dim(modal, lax.axis_index("seq") * own, own, 2)
    return (out, gq, gk, gv, short, mine[:, 0].T, mine[:, 1].T)


def solution(mesh):
    return jax.shard_map(
        local,
        mesh=mesh,
        in_specs=(
            P("chan", "seq"),
            P("chan", "seq"),
            P("chan", "seq"),
            P(None, None, "chan"),
            P(("chan", "seq"), None),
            P(("chan", "seq"), None),
            P("chan", "seq"),
        ),
        out_specs=(
            P("chan", "seq"),
            P("chan", "seq"),
            P("chan", "seq"),
            P("chan", "seq"),
            P(None, None, "chan"),
            P(("chan", "seq"), None),
            P(("chan", "seq"), None),
        ),
        check_vma=False,
    )
```

```python
import functools
import math

import jax
import jax.numpy as jnp
from jax import lax
from jax.experimental import pallas as pl
from jax.experimental.pallas import tpu as pltpu
from jax.sharding import PartitionSpec as P


def shifted(shard, axis, by):
    count = lax.axis_size(axis)
    pairs = [(i, i + by) for i in range(count) if 0 <= i + by < count]
    return lax.ppermute(shard, axis, pairs)


def dft_table(length, sign):
    counter = jnp.arange(length, dtype=jnp.int32)
    product = counter[:, None] * counter[None, :] % length
    angle = product.astype(jnp.float32) * (sign * 2.0 * math.pi / length)
    return (jnp.cos(angle), jnp.sin(angle))


def complex_dot(real_part, imag_part, table_real, table_imag):
    highest = lax.Precision.HIGHEST
    out_real = jnp.matmul(real_part, table_real, precision=highest) - jnp.matmul(
        imag_part, table_imag, precision=highest
    )
    out_imag = jnp.matmul(real_part, table_imag, precision=highest) + jnp.matmul(
        imag_part, table_real, precision=highest
    )
    return (out_real, out_imag)


def transform(real_part, imag_part, sign):
    length = real_part.shape[-1]
    if length <= 256 or length % 128 != 0:
        table_real, table_imag = dft_table(length, sign)
        return complex_dot(real_part, imag_part, table_real, table_imag)
    outer = 128
    inner = length // outer
    leading = real_part.shape[:-1]
    split_real = jnp.swapaxes(real_part.reshape(leading + (inner, outer)), -1, -2)
    split_imag = jnp.swapaxes(imag_part.reshape(leading + (inner, outer)), -1, -2)
    part_real, part_imag = transform(split_real, split_imag, sign)
    first_index = jnp.arange(outer, dtype=jnp.int32)[:, None]
    second_index = jnp.arange(inner, dtype=jnp.int32)[None, :]
    angle = (first_index * second_index % length).astype(jnp.float32) * (
        sign * 2.0 * math.pi / length
    )
    twist_real = jnp.cos(angle)
    twist_imag = jnp.sin(angle)
    turned_real = part_real * twist_real - part_imag * twist_imag
    turned_imag = part_real * twist_imag + part_imag * twist_real
    table_real, table_imag = dft_table(outer, sign)
    highest = lax.Precision.HIGHEST
    out_real = jnp.einsum(
        "...nk,nl->...lk", turned_real, table_real, precision=highest
    ) - jnp.einsum("...nk,nl->...lk", turned_imag, table_imag, precision=highest)
    out_imag = jnp.einsum(
        "...nk,nl->...lk", turned_real, table_imag, precision=highest
    ) + jnp.einsum("...nk,nl->...lk", turned_imag, table_real, precision=highest)
    return (out_real.reshape(leading + (length,)), out_imag.reshape(leading + (length,)))


def spectrum(signal):
    length = signal.shape[1]
    padded = jnp.pad(signal.astype(jnp.float32), ((0, 0), (0, length)))
    return transform(padded, jnp.zeros_like(padded), -1.0)


def mirrored(values):
    return jnp.roll(jnp.flip(values, -1), 1, -1)


def paired_spectra(first, second):
    length = first.shape[1]
    first_pad = jnp.pad(first, ((0, 0), (0, length)))
    second_pad = jnp.pad(second.astype(jnp.float32), ((0, 0), (0, length)))
    joint_real, joint_imag = transform(first_pad, second_pad, -1.0)
    mirror_real = mirrored(joint_real)
    mirror_imag = mirrored(joint_imag)
    first_spec = (0.5 * (joint_real + mirror_real), 0.5 * (joint_imag - mirror_imag))
    second_spec = (0.5 * (joint_imag + mirror_imag), -0.5 * (joint_real - mirror_real))
    return (first_spec, second_spec)


def to_time(spec_pair, length):
    real_part, imag_part = spec_pair
    back_real, back_imag = transform(real_part, imag_part, 1.0)
    return back_real[:, :length] / real_part.shape[-1]


def paired_time(first_spec, second_spec, length):
    joint_real = first_spec[0] - second_spec[1]
    joint_imag = first_spec[1] + second_spec[0]
    back_real, back_imag = transform(joint_real, joint_imag, 1.0)
    total_len = joint_real.shape[-1]
    return (back_real[:, :length] / total_len, back_imag[:, :length] / total_len)


def spectral_product(first, second, conjugate):
    first_real, first_imag = first
    second_real, second_imag = second
    if conjugate:
        second_imag = -second_imag
    return (
        first_real * second_real - first_imag * second_imag,
        first_real * second_imag + first_imag * second_real,
    )


def modal_filter(residue, log_rate, length):
    decay_rate = jnp.exp(log_rate)
    offsets = jnp.arange(length).astype(jnp.float32)
    filt = jnp.zeros((residue.shape[0], length), jnp.float32)
    for mode_index in range(residue.shape[1]):
        factor = residue[:, mode_index] * jnp.sqrt(2.0 * decay_rate[:, mode_index])
        filt = filt + factor[:, None] * jnp.exp(-decay_rate[:, mode_index][:, None] * offsets)
    return filt


def modal_grads(filt_grad, residue, log_rate):
    decay_rate = jnp.exp(log_rate)
    offsets = jnp.arange(filt_grad.shape[1]).astype(jnp.float32)
    res_terms = []
    log_terms = []
    for mode_index in range(residue.shape[1]):
        rate_col = decay_rate[:, mode_index][:, None]
        basis = jnp.sqrt(2.0 * rate_col) * jnp.exp(-rate_col * offsets)
        weighted = filt_grad * basis
        res_terms.append(jnp.sum(weighted, axis=1))
        log_terms.append(
            residue[:, mode_index] * jnp.sum(weighted * (0.5 - rate_col * offsets), axis=1)
        )
    return (jnp.stack(res_terms, axis=1), jnp.stack(log_terms, axis=1))


def apply_taps(widened, taps, tok_rows):
    total = jnp.zeros((widened.shape[0], tok_rows), jnp.float32)
    for offset in range(7):
        total = total + taps[offset][:, None] * widened[:, 6 - offset : 6 - offset + tok_rows]
    return total


def taps_back(gradient, following, taps):
    tok_rows = gradient.shape[1]
    widened = jnp.concatenate([gradient, following], axis=1)
    total = jnp.zeros_like(gradient)
    for offset in range(7):
        total = total + taps[offset][:, None] * widened[:, offset : offset + tok_rows]
    return total


def taps_gradient(gradient, widened):
    tok_rows = gradient.shape[1]
    rows_out = [
        jnp.sum(gradient * widened[:, 6 - offset : 6 - offset + tok_rows], axis=1)
        for offset in range(7)
    ]
    return jnp.stack(rows_out, axis=0)


def to_channels(stream):
    return lax.all_to_all(stream, "seq", split_axis=0, concat_axis=1, tiled=True)


def to_tokens(stream):
    return lax.all_to_all(stream, "seq", split_axis=1, concat_axis=0, tiled=True)


def local_fft(query_in, key_in, value_in, short_weight, residue, log_rate, grad_out):
    tok_rows = query_in.shape[1]
    length = tok_rows * lax.axis_size("seq")
    scale = 1.0 / math.sqrt(length)
    tails = shifted((query_in[:, -6:], key_in[:, -6:], value_in[:, -6:]), "seq", 1)
    query_wide = jnp.concatenate([tails[0], query_in], axis=1).astype(jnp.float32)
    key_wide = jnp.concatenate([tails[1], key_in], axis=1).astype(jnp.float32)
    value_wide = jnp.concatenate([tails[2], value_in], axis=1).astype(jnp.float32)
    query_hat = apply_taps(query_wide, short_weight[0], tok_rows)
    key_hat = apply_taps(key_wide, short_weight[1], tok_rows)
    value_hat = apply_taps(value_wide, short_weight[2], tok_rows)
    mixed = (key_hat * value_hat).astype(jnp.bfloat16)
    grad_up = grad_out.astype(jnp.float32)
    grad_mixed = (grad_up * query_hat).astype(jnp.bfloat16)
    mixed_cols = to_channels(mixed)
    filt = modal_filter(residue, log_rate, length)
    spec_filter, spec_mixed = paired_spectra(filt, mixed_cols)
    long_out = to_time(spectral_product(spec_mixed, spec_filter, False), length).astype(
        jnp.bfloat16
    )
    conv_out = to_tokens(long_out)
    grad_cols = to_channels(grad_mixed)
    spec_grad = spectrum(grad_cols)
    long_grad, filt_grad = paired_time(
        spectral_product(spec_grad, spec_filter, True),
        spectral_product(spec_grad, spec_mixed, True),
        length,
    )
    conv_grad = to_tokens(long_grad.astype(jnp.bfloat16))
    grad_res, grad_log = modal_grads(filt_grad, residue, log_rate)
    conv_wide = conv_out.astype(jnp.float32)
    conv_grad_wide = conv_grad.astype(jnp.float32)
    output = (query_hat * conv_wide).astype(jnp.bfloat16)
    grad_q = grad_up * conv_wide
    grad_k = conv_grad_wide * value_hat
    grad_v = conv_grad_wide * key_hat
    heads = shifted((grad_q[:, :6], grad_k[:, :6], grad_v[:, :6]), "seq", -1)
    grad_query = taps_back(grad_q, heads[0], short_weight[0]).astype(jnp.bfloat16)
    grad_key = taps_back(grad_k, heads[1], short_weight[1]).astype(jnp.bfloat16)
    grad_value = taps_back(grad_v, heads[2], short_weight[2]).astype(jnp.bfloat16)
    local_terms = jnp.stack(
        [
            taps_gradient(grad_q, query_wide),
            taps_gradient(grad_k, key_wide),
            taps_gradient(grad_v, value_wide),
        ],
        axis=0,
    )
    grad_short = lax.psum(local_terms, "seq") * scale
    return (
        output,
        grad_query,
        grad_key,
        grad_value,
        grad_short,
        grad_res * scale,
        grad_log * scale,
    )


SUB = 8
LANE = 128
HALO = 6
TAPS = 7
GROUP = 8
MESH = pl.DeviceIdType.MESH


def slab(index):
    return pl.ds(pl.multiple_of(index * SUB, SUB), SUB)


def layer_kernel(
    n, modes, tokens, scale,
    query_ref, key_ref, value_ref, grad_ref, weight_ref, param_ref,
    out_ref, gq_ref, gk_ref, gv_ref, short_ref, res_ref, log_ref,
    inputs, streams, hats, mixed, gmixed, conv, conv_back, prod, cots,
    weights, params, decay, gain, rate,
    edge_send, edge_recv, acc_send, acc_recv, carry_send, carry_recv,
    modal_send, modal_recv, short_send, short_recv, total_send, total_recv,
    load_sem, send_sem, recv_sem, halo_send, halo_recv,
):
    me = lax.axis_index("seq")
    extent = tokens + HALO
    rows_all = 3 * TAPS
    owners = (rows_all + 1) // 2
    f32 = jnp.float32
    zero = jnp.zeros((SUB, LANE), f32)

    def rounded(value):
        return value.astype(jnp.bfloat16).astype(f32)

    def tree(parts):
        while len(parts) > 1:
            parts = [parts[i] + parts[i + 1] for i in range(0, len(parts), 2)]
        return parts[0]

    def per_mode(ref):
        return [ref[m * SUB : (m + 1) * SUB, :] for m in range(modes)]

    loads = [
        pltpu.make_async_copy(ref, inputs.at[s], load_sem.at[s])
        for s, ref in enumerate((query_ref, key_ref, value_ref, grad_ref))
    ]
    for load in loads:
        load.start()

    barrier = pltpu.get_barrier_semaphore()
    peers = [lax.rem(me + k, n) for k in range(1, n)]
    for peer in peers:
        pl.semaphore_signal(
            barrier, inc=1, device_id={"seq": peer}, device_id_type=MESH
        )

    def send(phase, peer, source, target):
        pltpu.make_async_remote_copy(
            src_ref=source,
            dst_ref=target,
            send_sem=send_sem.at[phase],
            recv_sem=recv_sem.at[phase],
            device_id={"seq": peer},
            device_id_type=MESH,
        ).start()

    def sent(phase, like):
        pltpu.make_async_copy(like, like, send_sem.at[phase]).wait()

    def arrived(phase, like):
        pltpu.make_async_copy(like, like, recv_sem.at[phase]).wait()

    others = pl.ds(0, n - 1)

    for s in range(3):
        for b in range(SUB):
            weights[pl.ds(s * TAPS * SUB + b, TAPS, stride=SUB), :] = weight_ref[
                s, :, b * LANE : (b + 1) * LANE
            ]

    for s in range(4):
        loads[s].wait()
        for b in range(SUB):
            block = inputs[s, b * LANE : (b + 1) * LANE, :].astype(f32)
            streams[s, pl.ds(HALO * SUB + b, tokens, stride=SUB), :] = block.T

    pl.semaphore_wait(barrier, n - 1)

    edge = HALO * SUB
    last = tokens * SUB
    to_right = lambda: pltpu.make_async_remote_copy(
        src_ref=streams.at[pl.ds(0, 3), pl.ds(last, edge)],
        dst_ref=streams.at[pl.ds(0, 3), pl.ds(0, edge)],
        send_sem=halo_send.at[0],
        recv_sem=halo_recv.at[0],
        device_id={"seq": lax.rem(me + 1, n)},
        device_id_type=MESH,
    )
    to_left = lambda: pltpu.make_async_remote_copy(
        src_ref=streams.at[:, pl.ds(edge, edge)],
        dst_ref=streams.at[:, pl.ds(edge + last, edge)],
        send_sem=halo_send.at[1],
        recv_sem=halo_recv.at[1],
        device_id={"seq": lax.rem(me + n - 1, n)},
        device_id_type=MESH,
    )

    @pl.when(me < n - 1)
    def _():
        to_right().start()

    @pl.when(me > 0)
    def _():
        to_left().start()

    @pl.when(me == 0)
    def _():
        streams[0:3, 0:edge, :] = jnp.zeros((3, edge, LANE), f32)

    @pl.when(me == n - 1)
    def _():
        streams[:, edge + last : 2 * edge + last, :] = jnp.zeros((4, edge, LANE), f32)

    for peer in peers:
        send(0, peer, param_ref, params.at[me])
    params[me] = param_ref[...]

    taps = [
        [weights[(s * TAPS + j) * SUB : (s * TAPS + j + 1) * SUB, :] for j in range(TAPS)]
        for s in range(3)
    ]

    def filter_token(t):
        vals = []
        for s in range(3):
            total = taps[s][0] * streams[s, slab(t + HALO), :]
            for j in range(1, TAPS):
                total = total + taps[s][j] * streams[s, slab(t + HALO - j), :]
            hats[s, slab(t), :] = total
            vals.append(total)
        mixed[slab(t), :] = rounded(vals[1] * vals[2])
        gmixed[slab(t), :] = rounded(vals[0] * streams[3, slab(t + HALO), :])

    def token_loop(lo, hi, unroll, fn):
        def step(i, carry):
            for u in range(unroll):
                fn(lo + i * unroll + u)
            return carry

        lax.fori_loop(0, (hi - lo) // unroll, step, 0)

    token_loop(HALO, tokens, 2, filter_token)

    @pl.when(me > 0)
    def _():
        to_left().wait_send()
        to_right().wait_recv()

    @pl.when(me < n - 1)
    def _():
        to_right().wait_send()
        to_left().wait_recv()

    token_loop(0, HALO, 2, filter_token)
    token_loop(tokens, extent, 2, filter_token)

    arrived(0, params.at[others])
    low_half = lax.broadcasted_iota(jnp.int32, (SUB, LANE), 1) < LANE // 2
    for m in range(modes):
        even = jnp.concatenate([params[2 * b, m : m + 1, :] for b in range(SUB)], axis=0)
        odd = jnp.concatenate([params[2 * b + 1, m : m + 1, :] for b in range(SUB)], axis=0)
        log_rate = jnp.where(low_half, even, pltpu.roll(odd, LANE // 2, 1))
        residue = jnp.where(low_half, pltpu.roll(even, LANE // 2, 1), odd)
        r = jnp.exp(log_rate)
        rate[slab(m), :] = r
        decay[slab(m), :] = jnp.exp(-r)
        gain[slab(m), :] = residue * jnp.sqrt(2.0 * r)

    UN = 4
    decays = per_mode(decay)

    def edge_step(i, carry):
        x, z = [list(c) for c in carry]
        for u in range(UN):
            t = i * UN + u
            value = mixed[slab(t), :]
            cot = gmixed[slab(tokens - 1 - t), :]
            for m in range(modes):
                x[m] = decays[m] * x[m] + value
                z[m] = decays[m] * z[m] + cot
        return tuple(x), tuple(z)

    x, z = lax.fori_loop(0, tokens // UN, edge_step, ((zero,) * modes,) * 2)
    for m in range(modes):
        edge_send[m, 0:SUB, :] = x[m]
        edge_send[m, SUB : 2 * SUB, :] = z[m]
    for peer in peers:
        send(1, peer, edge_send.at[peer], edge_recv.at[me])
    edge_recv[me] = edge_send[me]

    for first in range(0, modes, GROUP):
        group = range(first, first + GROUP)

        def fwd_step(i, carry, first=first, group=group):
            x, y, ax, ay = [list(c) for c in carry]
            for u in range(UN):
                t = i * UN + u
                value = mixed[slab(t), :]
                cot = gmixed[slab(t), :]
                parts = []
                for p, m in enumerate(group):
                    a = decay[m * SUB : (m + 1) * SUB, :]
                    y[p] = a * (y[p] + x[p])
                    x[p] = a * x[p] + value
                    parts.append(gain[m * SUB : (m + 1) * SUB, :] * x[p])
                    ax[p] = ax[p] + cot * x[p]
                    ay[p] = ay[p] + cot * y[p]
                total = tree(parts)
                conv[slab(t), :] = conv[slab(t), :] + total if first else total
            return tuple(tuple(c) for c in (x, y, ax, ay))

        zeros = tuple(zero for _ in group)
        x, y, ax, ay = lax.fori_loop(0, tokens // UN, fwd_step, (zeros,) * 4)
        for p, m in enumerate(group):
            acc_send[m, 0:SUB, :] = y[p]
            acc_send[m, 2 * SUB : 3 * SUB, :] = ax[p]
            acc_send[m, 3 * SUB : 4 * SUB, :] = ay[p]
        x = list(x)
        for t in range(tokens, extent):
            value = mixed[t * SUB : (t + 1) * SUB, :]
            total = conv[t * SUB : (t + 1) * SUB, :] if first else zero
            for p, m in enumerate(group):
                x[p] = decay[m * SUB : (m + 1) * SUB, :] * x[p] + value
                total = total + gain[m * SUB : (m + 1) * SUB, :] * x[p]
            conv[t * SUB : (t + 1) * SUB, :] = total

    my_rate = rate[slab(me), :]
    my_decay = decay[slab(me), :]
    my_gain = gain[slab(me), :]
    whole = jnp.exp(-float(tokens) * my_rate)
    arrived(1, edge_recv.at[others])
    h, z = zero, zero
    for d in range(n):
        back = n - 1 - d
        carry_send[d, 0:SUB, :] = h
        carry_send[back, SUB : 2 * SUB, :] = z
        h = whole * h + edge_recv[d, 0:SUB, :]
        z = whole * z + edge_recv[back, SUB : 2 * SUB, :]
    for peer in peers:
        send(2, peer, carry_send.at[peer], carry_recv.at[me])
    carry_recv[me] = carry_send[me]

    for first in range(0, modes, GROUP):
        group = range(first, first + GROUP)

        def bwd_step(i, carry, first=first, group=group):
            z, w = [list(c) for c in carry]
            for u in range(UN):
                t = tokens - 1 - (i * UN + u)
                cot = gmixed[slab(t), :]
                parts = []
                for p, m in enumerate(group):
                    a = decay[m * SUB : (m + 1) * SUB, :]
                    z[p] = a * z[p] + cot
                    w[p] = a * w[p] + z[p]
                    parts.append(gain[m * SUB : (m + 1) * SUB, :] * z[p])
                total = tree(parts)
                conv_back[slab(t), :] = conv_back[slab(t), :] + total if first else total
            return tuple(tuple(c) for c in (z, w))

        zeros = tuple(zero for _ in group)
        z, w = lax.fori_loop(0, tokens // UN, bwd_step, (zeros,) * 2)
        for p, m in enumerate(group):
            acc_send[m, SUB : 2 * SUB, :] = w[p]

    for peer in peers:
        send(3, peer, acc_send.at[peer], acc_recv.at[me])
    acc_recv[me] = acc_send[me]

    arrived(2, carry_recv.at[others])
    gains = per_mode(gain)

    def fwd_two(i, c):
        c = list(c)
        for u in range(2):
            t = i * 2 + u
            c = [decays[m] * c[m] for m in range(modes)]
            total = rounded(conv[slab(t), :] + tree(c))
            prod[slab(t), :] = hats[0, slab(t), :] * total
            cots[0, slab(t), :] = streams[3, slab(t + HALO), :] * total
        return tuple(c)

    start = tuple(gains[m] * carry_recv[m, 0:SUB, :] for m in range(modes))
    lax.fori_loop(0, extent // 2, fwd_two, start)

    def store_back(t, total):
        total = rounded(total)
        cots[1, slab(t), :] = hats[2, slab(t), :] * total
        cots[2, slab(t), :] = hats[1, slab(t), :] * total

    def bwd_two(i, c):
        c = list(c)
        for u in range(2):
            t = tokens - 1 - (i * 2 + u)
            c = [decays[m] * c[m] for m in range(modes)]
            store_back(t, conv_back[slab(t), :] + tree(c))
        return tuple(c)

    start = tuple(gains[m] * carry_recv[m, SUB : 2 * SUB, :] for m in range(modes))
    lax.fori_loop(0, tokens // 2, bwd_two, start)

    ahead = [zero] * HALO
    for m in range(modes):
        grow = jnp.exp(rate[m * SUB : (m + 1) * SUB, :])
        z = carry_recv[m, SUB : 2 * SUB, :]
        for h in range(HALO):
            ahead[h] = ahead[h] + gains[m] * z
            z = grow * (z - gmixed[(tokens + h) * SUB : (tokens + h + 1) * SUB, :])
    for h in range(HALO):
        store_back(tokens + h, ahead[h])

    def short_step(i, accs):
        accs = list(accs)
        for u in range(2):
            t = i * 2 + u
            for s in range(3):
                cot = cots[s, slab(t), :]
                for j in range(TAPS):
                    at = s * TAPS + j
                    accs[at] = accs[at] + cot * streams[s, slab(t + HALO - j), :]
        return tuple(accs)

    accs = lax.fori_loop(0, tokens // 2, short_step, (zero,) * rows_all)
    for row in range(2 * owners):
        short_send[row // 2, (row % 2) * SUB : (row % 2 + 1) * SUB, :] = (
            accs[row] if row < rows_all else zero
        )
    for peer in peers:

        @pl.when(peer < owners)
        def _(peer=peer):
            send(5, peer, short_send.at[peer], short_recv.at[me])

    @pl.when(me < owners)
    def _():
        short_recv[me] = short_send[me]

    arrived(3, acc_recv.at[others])
    hy, acc_x, acc_y = zero, zero, zero
    for d in range(n):
        h = carry_send[d, 0:SUB, :]
        z0 = my_decay * edge_recv[d, SUB : 2 * SUB, :]
        z1 = my_decay * acc_recv[d, SUB : 2 * SUB, :]
        acc_x = acc_x + (acc_recv[d, 2 * SUB : 3 * SUB, :] + h * z0)
        acc_y = acc_y + (acc_recv[d, 3 * SUB : 4 * SUB, :] + h * z1 + hy * z0)
        hy = whole * (hy + float(tokens) * h) + acc_recv[d, 0:SUB, :]
    grad_res = acc_x * jnp.sqrt(2.0 * my_rate) * scale
    grad_log = my_gain * (0.5 * acc_x - my_rate * acc_y) * scale
    for b in range(SUB):
        modal_send[b, 0:1, :] = grad_res[b : b + 1, :]
        modal_send[b, 1:2, :] = grad_log[b : b + 1, :]
    for peer in peers:
        send(4, peer, modal_send.at[lax.div(peer, 2)], modal_recv.at[me])
    modal_recv[me] = modal_send[lax.div(me, 2)]

    def taps_step(t):
        for s in range(3):
            total = taps[s][0] * cots[s, slab(t), :]
            for j in range(1, TAPS):
                total = total + taps[s][j] * cots[s, slab(t + j), :]
            hats[s, slab(t), :] = total

    token_loop(0, tokens, 2, taps_step)

    @pl.when(me < owners)
    def _():
        arrived(5, short_recv.at[others])
        total = short_recv[0]
        for d in range(1, n):
            total = total + short_recv[d]
        total_send[...] = total * scale
        for peer in peers:
            send(6, peer, total_send, total_recv.at[me])
        total_recv[me] = total_send[...]

    for s, ref in enumerate((out_ref, gq_ref, gk_ref, gv_ref)):
        for b in range(SUB):
            rows = pl.ds(b, tokens, stride=SUB)
            block = hats[s - 1, rows, :] if s else prod[rows, :]
            ref[b * LANE : (b + 1) * LANE, :] = block.T.astype(jnp.bfloat16)

    arrived(4, modal_recv.at[others])
    odd_owner = lax.rem(me, 2) == 1
    for at, ref in ((0, res_ref), (1, log_ref)):
        table = jnp.concatenate([modal_recv[m, at : at + 1, :] for m in range(modes)], axis=0)
        table = jnp.where(odd_owner, pltpu.roll(table, LANE // 2, 1), table)
        ref[...] = table[:, : LANE // 2]

    @pl.when(me < owners)
    def _():
        arrived(6, total_recv.at[pl.ds(0, owners - 1)])
        sent(5, short_recv.at[pl.ds(0, owners - 1)])
        sent(6, short_recv.at[others])

    @pl.when(me >= owners)
    def _():
        arrived(6, total_recv)
        sent(5, short_recv.at[pl.ds(0, owners)])

    for s in range(3):
        for b in range(SUB):
            for j in range(TAPS):
                row = s * TAPS + j
                at = (row % 2) * SUB + b
                short_ref[s, j : j + 1, b * LANE : (b + 1) * LANE] = total_recv[
                    row // 2, at : at + 1, :
                ]

    sent(0, params.at[others])
    sent(1, edge_recv.at[others])
    sent(2, carry_recv.at[others])
    sent(3, acc_recv.at[others])
    sent(4, modal_recv.at[others])


def hand_over(*refs):
    sems = refs[-1]
    count = (len(refs) - 1) // 2
    copies = [
        pltpu.make_async_copy(refs[i], refs[count + i], sems.at[i]) for i in range(count)
    ]
    for copy in copies:
        copy.start()
    for copy in copies:
        copy.wait()


def local(query_in, key_in, value_in, short_weight, residue, log_rate, grad_out):
    n = lax.axis_size("seq")
    width, tokens = query_in.shape
    own, modes = residue.shape
    fits = width == SUB * LANE and tokens == LANE and modes == n == 2 * SUB
    if not (fits and own == LANE // 2):
        return local_fft(
            query_in, key_in, value_in, short_weight, residue, log_rate, grad_out
        )
    scale = 1.0 / math.sqrt(tokens * n)
    f32 = jnp.float32
    rows = (tokens + HALO) * SUB
    owners = (3 * TAPS + 1) // 2
    param = jnp.concatenate([log_rate.T, residue.T], axis=1)
    vmem = pl.BlockSpec(memory_space=pltpu.VMEM)
    hbm = pl.BlockSpec(memory_space=pltpu.MemorySpace.HBM)
    pair = pltpu.VMEM((n, 2 * SUB, LANE), f32)
    quad = pltpu.VMEM((n, 4 * SUB, LANE), f32)
    flat = pltpu.VMEM((rows, LANE), f32)
    triple = pltpu.VMEM((3, rows, LANE), f32)
    small = pltpu.VMEM((modes * SUB, LANE), f32)
    shape = jax.ShapeDtypeStruct((width, tokens), jnp.bfloat16)
    modal = jax.ShapeDtypeStruct((modes, own), f32)
    results = pl.pallas_call(
        functools.partial(layer_kernel, n, modes, tokens, scale),
        out_shape=(
            shape, shape, shape, shape,
            jax.ShapeDtypeStruct(short_weight.shape, f32), modal, modal,
        ),
        in_specs=[hbm] * 4 + [vmem] * 2,
        out_specs=(vmem,) * 7,
        scratch_shapes=[
            pltpu.VMEM((4, width, tokens), jnp.bfloat16),
            pltpu.VMEM((4, rows + HALO * SUB, LANE), f32),
            triple, flat, flat, flat, flat, flat, triple,
            pltpu.VMEM((3 * TAPS * SUB, LANE), f32),
            pltpu.VMEM((n, modes, LANE), f32),
            small, small, small,
            pair, pair, quad, quad, pair, pair,
            pltpu.VMEM((SUB, 2, LANE), f32),
            pltpu.VMEM((n, 2, LANE), f32),
            pltpu.VMEM((owners, 2 * SUB, LANE), f32),
            pair,
            pltpu.VMEM((2 * SUB, LANE), f32),
            pltpu.VMEM((owners, 2 * SUB, LANE), f32),
            pltpu.SemaphoreType.DMA((4,)),
            pltpu.SemaphoreType.DMA((7,)),
            pltpu.SemaphoreType.DMA((7,)),
            pltpu.SemaphoreType.DMA((2,)),
            pltpu.SemaphoreType.DMA((2,)),
        ],
        compiler_params=pltpu.CompilerParams(
            collective_id=0, has_side_effects=True, vmem_limit_bytes=56 * 2**20
        ),
    )(query_in, key_in, value_in, grad_out, short_weight, param)
    count = len(results)
    results = pl.pallas_call(
        hand_over,
        out_shape=[jax.ShapeDtypeStruct(r.shape, r.dtype) for r in results],
        in_specs=[hbm] * count,
        out_specs=[hbm] * count,
        scratch_shapes=[pltpu.SemaphoreType.DMA((count,))],
        compiler_params=pltpu.CompilerParams(vmem_limit_bytes=60 * 2**20),
    )(*results)
    return (*results[:5], results[5].T, results[6].T)


def solution(mesh):
    return jax.shard_map(
        local,
        mesh=mesh,
        in_specs=(
            P("chan", "seq"),
            P("chan", "seq"),
            P("chan", "seq"),
            P(None, None, "chan"),
            P(("chan", "seq"), None),
            P(("chan", "seq"), None),
            P("chan", "seq"),
        ),
        out_specs=(
            P("chan", "seq"),
            P("chan", "seq"),
            P("chan", "seq"),
            P("chan", "seq"),
            P(None, None, "chan"),
            P(("chan", "seq"), None),
            P(("chan", "seq"), None),
        ),
        check_vma=False,
    )
```

```python
import functools
import math

import jax
import jax.numpy as jnp
from jax import lax
from jax.experimental import pallas as pl
from jax.experimental.pallas import tpu as pltpu
from jax.sharding import PartitionSpec as P


def shifted(shard, axis, by):
    count = lax.axis_size(axis)
    pairs = [(i, i + by) for i in range(count) if 0 <= i + by < count]
    return lax.ppermute(shard, axis, pairs)


def dft_table(length, sign):
    counter = jnp.arange(length, dtype=jnp.int32)
    product = counter[:, None] * counter[None, :] % length
    angle = product.astype(jnp.float32) * (sign * 2.0 * math.pi / length)
    return (jnp.cos(angle), jnp.sin(angle))


def complex_dot(real_part, imag_part, table_real, table_imag):
    highest = lax.Precision.HIGHEST
    out_real = jnp.matmul(real_part, table_real, precision=highest) - jnp.matmul(
        imag_part, table_imag, precision=highest
    )
    out_imag = jnp.matmul(real_part, table_imag, precision=highest) + jnp.matmul(
        imag_part, table_real, precision=highest
    )
    return (out_real, out_imag)


def transform(real_part, imag_part, sign):
    length = real_part.shape[-1]
    if length <= 256 or length % 128 != 0:
        table_real, table_imag = dft_table(length, sign)
        return complex_dot(real_part, imag_part, table_real, table_imag)
    outer = 128
    inner = length // outer
    leading = real_part.shape[:-1]
    split_real = jnp.swapaxes(real_part.reshape(leading + (inner, outer)), -1, -2)
    split_imag = jnp.swapaxes(imag_part.reshape(leading + (inner, outer)), -1, -2)
    part_real, part_imag = transform(split_real, split_imag, sign)
    first_index = jnp.arange(outer, dtype=jnp.int32)[:, None]
    second_index = jnp.arange(inner, dtype=jnp.int32)[None, :]
    angle = (first_index * second_index % length).astype(jnp.float32) * (
        sign * 2.0 * math.pi / length
    )
    twist_real = jnp.cos(angle)
    twist_imag = jnp.sin(angle)
    turned_real = part_real * twist_real - part_imag * twist_imag
    turned_imag = part_real * twist_imag + part_imag * twist_real
    table_real, table_imag = dft_table(outer, sign)
    highest = lax.Precision.HIGHEST
    out_real = jnp.einsum(
        "...nk,nl->...lk", turned_real, table_real, precision=highest
    ) - jnp.einsum("...nk,nl->...lk", turned_imag, table_imag, precision=highest)
    out_imag = jnp.einsum(
        "...nk,nl->...lk", turned_real, table_imag, precision=highest
    ) + jnp.einsum("...nk,nl->...lk", turned_imag, table_real, precision=highest)
    return (out_real.reshape(leading + (length,)), out_imag.reshape(leading + (length,)))


def spectrum(signal):
    length = signal.shape[1]
    padded = jnp.pad(signal.astype(jnp.float32), ((0, 0), (0, length)))
    return transform(padded, jnp.zeros_like(padded), -1.0)


def mirrored(values):
    return jnp.roll(jnp.flip(values, -1), 1, -1)


def paired_spectra(first, second):
    length = first.shape[1]
    first_pad = jnp.pad(first, ((0, 0), (0, length)))
    second_pad = jnp.pad(second.astype(jnp.float32), ((0, 0), (0, length)))
    joint_real, joint_imag = transform(first_pad, second_pad, -1.0)
    mirror_real = mirrored(joint_real)
    mirror_imag = mirrored(joint_imag)
    first_spec = (0.5 * (joint_real + mirror_real), 0.5 * (joint_imag - mirror_imag))
    second_spec = (0.5 * (joint_imag + mirror_imag), -0.5 * (joint_real - mirror_real))
    return (first_spec, second_spec)


def to_time(spec_pair, length):
    real_part, imag_part = spec_pair
    back_real, back_imag = transform(real_part, imag_part, 1.0)
    return back_real[:, :length] / real_part.shape[-1]


def paired_time(first_spec, second_spec, length):
    joint_real = first_spec[0] - second_spec[1]
    joint_imag = first_spec[1] + second_spec[0]
    back_real, back_imag = transform(joint_real, joint_imag, 1.0)
    total_len = joint_real.shape[-1]
    return (back_real[:, :length] / total_len, back_imag[:, :length] / total_len)


def spectral_product(first, second, conjugate):
    first_real, first_imag = first
    second_real, second_imag = second
    if conjugate:
        second_imag = -second_imag
    return (
        first_real * second_real - first_imag * second_imag,
        first_real * second_imag + first_imag * second_real,
    )


def modal_filter(residue, log_rate, length):
    decay_rate = jnp.exp(log_rate)
    offsets = jnp.arange(length).astype(jnp.float32)
    filt = jnp.zeros((residue.shape[0], length), jnp.float32)
    for mode_index in range(residue.shape[1]):
        factor = residue[:, mode_index] * jnp.sqrt(2.0 * decay_rate[:, mode_index])
        filt = filt + factor[:, None] * jnp.exp(-decay_rate[:, mode_index][:, None] * offsets)
    return filt


def modal_grads(filt_grad, residue, log_rate):
    decay_rate = jnp.exp(log_rate)
    offsets = jnp.arange(filt_grad.shape[1]).astype(jnp.float32)
    res_terms = []
    log_terms = []
    for mode_index in range(residue.shape[1]):
        rate_col = decay_rate[:, mode_index][:, None]
        basis = jnp.sqrt(2.0 * rate_col) * jnp.exp(-rate_col * offsets)
        weighted = filt_grad * basis
        res_terms.append(jnp.sum(weighted, axis=1))
        log_terms.append(
            residue[:, mode_index] * jnp.sum(weighted * (0.5 - rate_col * offsets), axis=1)
        )
    return (jnp.stack(res_terms, axis=1), jnp.stack(log_terms, axis=1))


def apply_taps(widened, taps, tok_rows):
    total = jnp.zeros((widened.shape[0], tok_rows), jnp.float32)
    for offset in range(7):
        total = total + taps[offset][:, None] * widened[:, 6 - offset : 6 - offset + tok_rows]
    return total


def taps_back(gradient, following, taps):
    tok_rows = gradient.shape[1]
    widened = jnp.concatenate([gradient, following], axis=1)
    total = jnp.zeros_like(gradient)
    for offset in range(7):
        total = total + taps[offset][:, None] * widened[:, offset : offset + tok_rows]
    return total


def taps_gradient(gradient, widened):
    tok_rows = gradient.shape[1]
    rows_out = [
        jnp.sum(gradient * widened[:, 6 - offset : 6 - offset + tok_rows], axis=1)
        for offset in range(7)
    ]
    return jnp.stack(rows_out, axis=0)


def to_channels(stream):
    return lax.all_to_all(stream, "seq", split_axis=0, concat_axis=1, tiled=True)


def to_tokens(stream):
    return lax.all_to_all(stream, "seq", split_axis=1, concat_axis=0, tiled=True)


def local_fft(query_in, key_in, value_in, short_weight, residue, log_rate, grad_out):
    tok_rows = query_in.shape[1]
    length = tok_rows * lax.axis_size("seq")
    scale = 1.0 / math.sqrt(length)
    tails = shifted((query_in[:, -6:], key_in[:, -6:], value_in[:, -6:]), "seq", 1)
    query_wide = jnp.concatenate([tails[0], query_in], axis=1).astype(jnp.float32)
    key_wide = jnp.concatenate([tails[1], key_in], axis=1).astype(jnp.float32)
    value_wide = jnp.concatenate([tails[2], value_in], axis=1).astype(jnp.float32)
    query_hat = apply_taps(query_wide, short_weight[0], tok_rows)
    key_hat = apply_taps(key_wide, short_weight[1], tok_rows)
    value_hat = apply_taps(value_wide, short_weight[2], tok_rows)
    mixed = (key_hat * value_hat).astype(jnp.bfloat16)
    grad_up = grad_out.astype(jnp.float32)
    grad_mixed = (grad_up * query_hat).astype(jnp.bfloat16)
    mixed_cols = to_channels(mixed)
    filt = modal_filter(residue, log_rate, length)
    spec_filter, spec_mixed = paired_spectra(filt, mixed_cols)
    long_out = to_time(spectral_product(spec_mixed, spec_filter, False), length).astype(
        jnp.bfloat16
    )
    conv_out = to_tokens(long_out)
    grad_cols = to_channels(grad_mixed)
    spec_grad = spectrum(grad_cols)
    long_grad, filt_grad = paired_time(
        spectral_product(spec_grad, spec_filter, True),
        spectral_product(spec_grad, spec_mixed, True),
        length,
    )
    conv_grad = to_tokens(long_grad.astype(jnp.bfloat16))
    grad_res, grad_log = modal_grads(filt_grad, residue, log_rate)
    conv_wide = conv_out.astype(jnp.float32)
    conv_grad_wide = conv_grad.astype(jnp.float32)
    output = (query_hat * conv_wide).astype(jnp.bfloat16)
    grad_q = grad_up * conv_wide
    grad_k = conv_grad_wide * value_hat
    grad_v = conv_grad_wide * key_hat
    heads = shifted((grad_q[:, :6], grad_k[:, :6], grad_v[:, :6]), "seq", -1)
    grad_query = taps_back(grad_q, heads[0], short_weight[0]).astype(jnp.bfloat16)
    grad_key = taps_back(grad_k, heads[1], short_weight[1]).astype(jnp.bfloat16)
    grad_value = taps_back(grad_v, heads[2], short_weight[2]).astype(jnp.bfloat16)
    local_terms = jnp.stack(
        [
            taps_gradient(grad_q, query_wide),
            taps_gradient(grad_k, key_wide),
            taps_gradient(grad_v, value_wide),
        ],
        axis=0,
    )
    grad_short = lax.psum(local_terms, "seq") * scale
    return (
        output,
        grad_query,
        grad_key,
        grad_value,
        grad_short,
        grad_res * scale,
        grad_log * scale,
    )


SUB = 8
LANE = 128
HALO = 6
TAPS = 7
GROUP = 8
MESH = pl.DeviceIdType.MESH


def slab(index):
    return pl.ds(pl.multiple_of(index * SUB, SUB), SUB)


def layer_kernel(
    n, modes, tokens, scale,
    query_ref, key_ref, value_ref, grad_ref, weight_ref, param_ref,
    out_ref, gq_ref, gk_ref, gv_ref, short_ref, res_ref, log_ref,
    inputs, results, streams, hats, mixed, gmixed, conv, conv_back, prod, cots,
    weights, params, decay, gain, rate,
    edge_send, edge_recv, acc_hold, acc_send, acc_recv,
    carry_hold, carry_send, carry_recv, modal_send, modal_recv, short_send, short_recv, total_send, total_recv,
    load_sem, store_sem, send_sem, recv_sem, halo_send, halo_recv,
):
    me = lax.axis_index("seq")
    extent = tokens + HALO
    rows_all = 3 * TAPS
    owners = (rows_all + 1) // 2
    f32 = jnp.float32
    zero = jnp.zeros((SUB, LANE), f32)

    def rounded(value):
        return value.astype(jnp.bfloat16).astype(f32)

    def tree(parts):
        while len(parts) > 1:
            parts = [parts[i] + parts[i + 1] for i in range(0, len(parts), 2)]
        return parts[0]

    def per_mode(ref):
        return [ref[m * SUB : (m + 1) * SUB, :] for m in range(modes)]

    loads = [
        pltpu.make_async_copy(ref, inputs.at[s], load_sem.at[s])
        for s, ref in enumerate((query_ref, key_ref, value_ref, grad_ref))
    ]
    for load in loads:
        load.start()

    barrier = pltpu.get_barrier_semaphore()
    peers = [lax.rem(me + k, n) for k in range(1, n)]
    for peer in peers:
        pl.semaphore_signal(
            barrier, inc=1, device_id={"seq": peer}, device_id_type=MESH
        )

    def send(phase, peer, source, target):
        pltpu.make_async_remote_copy(
            src_ref=source,
            dst_ref=target,
            send_sem=send_sem.at[phase],
            recv_sem=recv_sem.at[phase],
            device_id={"seq": peer},
            device_id_type=MESH,
        ).start()

    def sent(phase, like):
        pltpu.make_async_copy(like, like, send_sem.at[phase]).wait()

    def arrived(phase, like):
        pltpu.make_async_copy(like, like, recv_sem.at[phase]).wait()

    others = pl.ds(0, n - 1)

    for s in range(3):
        for b in range(SUB):
            weights[pl.ds(s * TAPS * SUB + b, TAPS, stride=SUB), :] = weight_ref[
                s, :, b * LANE : (b + 1) * LANE
            ]

    eye = (
        lax.broadcasted_iota(jnp.int32, (LANE, LANE), 0)
        == lax.broadcasted_iota(jnp.int32, (LANE, LANE), 1)
    ).astype(jnp.bfloat16)

    def turned(block):
        return lax.dot_general(
            eye, block, (((1,), (1,)), ((), ())), preferred_element_type=f32
        )

    for s in range(4):
        loads[s].wait()
        for b in range(0, SUB, 2):
            block = turned(inputs[s, b * LANE : (b + 2) * LANE, :])
            for half in range(2):
                streams[s, pl.ds(HALO * SUB + b + half, tokens, stride=SUB), :] = block[
                    :, half * LANE : (half + 1) * LANE
                ]
        if s == 1:
            pl.semaphore_wait(barrier, n - 1)
            for peer in peers:
                send(0, peer, param_ref, params.at[me])
            params[me] = param_ref[...]

    edge = HALO * SUB
    last = tokens * SUB
    to_right = lambda: pltpu.make_async_remote_copy(
        src_ref=streams.at[pl.ds(0, 3), pl.ds(last, edge)],
        dst_ref=streams.at[pl.ds(0, 3), pl.ds(0, edge)],
        send_sem=halo_send.at[0],
        recv_sem=halo_recv.at[0],
        device_id={"seq": lax.rem(me + 1, n)},
        device_id_type=MESH,
    )
    to_left = lambda: pltpu.make_async_remote_copy(
        src_ref=streams.at[:, pl.ds(edge, edge)],
        dst_ref=streams.at[:, pl.ds(edge + last, edge)],
        send_sem=halo_send.at[1],
        recv_sem=halo_recv.at[1],
        device_id={"seq": lax.rem(me + n - 1, n)},
        device_id_type=MESH,
    )

    @pl.when(me < n - 1)
    def _():
        to_right().start()

    @pl.when(me > 0)
    def _():
        to_left().start()

    @pl.when(me == 0)
    def _():
        streams[0:3, 0:edge, :] = jnp.zeros((3, edge, LANE), f32)

    @pl.when(me == n - 1)
    def _():
        streams[:, edge + last : 2 * edge + last, :] = jnp.zeros((4, edge, LANE), f32)

    taps = [
        [weights[(s * TAPS + j) * SUB : (s * TAPS + j + 1) * SUB, :] for j in range(TAPS)]
        for s in range(3)
    ]

    def filter_token(t):
        vals = []
        for s in range(3):
            total = taps[s][0] * streams[s, slab(t + HALO), :]
            for j in range(1, TAPS):
                total = total + taps[s][j] * streams[s, slab(t + HALO - j), :]
            hats[s, slab(t), :] = total
            vals.append(total)
        mixed[slab(t), :] = rounded(vals[1] * vals[2])
        gmixed[slab(t), :] = rounded(vals[0] * streams[3, slab(t + HALO), :])

    def token_loop(lo, hi, unroll, fn):
        def step(i, carry):
            for u in range(unroll):
                fn(lo + i * unroll + u)
            return carry

        lax.fori_loop(0, (hi - lo) // unroll, step, 0)

    token_loop(HALO, tokens, 2, filter_token)

    @pl.when(me > 0)
    def _():
        to_left().wait_send()
        to_right().wait_recv()

    @pl.when(me < n - 1)
    def _():
        to_right().wait_send()
        to_left().wait_recv()

    token_loop(0, HALO, 2, filter_token)
    token_loop(tokens, extent, 2, filter_token)

    arrived(0, params.at[others])
    low_half = lax.broadcasted_iota(jnp.int32, (SUB, LANE), 1) < LANE // 2
    for m in range(modes):
        even = jnp.concatenate([params[2 * b, m : m + 1, :] for b in range(SUB)], axis=0)
        odd = jnp.concatenate([params[2 * b + 1, m : m + 1, :] for b in range(SUB)], axis=0)
        log_rate = jnp.where(low_half, even, pltpu.roll(odd, LANE // 2, 1))
        residue = jnp.where(low_half, pltpu.roll(even, LANE // 2, 1), odd)
        r = jnp.exp(log_rate)
        rate[slab(m), :] = r
        decay[slab(m), :] = jnp.exp(-r)
        gain[slab(m), :] = residue * jnp.sqrt(2.0 * r)

    UN = 4
    decays = per_mode(decay)

    def edge_step(i, carry):
        x, z = [list(c) for c in carry]
        for u in range(UN):
            t = i * UN + u
            value = mixed[slab(t), :]
            cot = gmixed[slab(tokens - 1 - t), :]
            for m in range(modes):
                x[m] = decays[m] * x[m] + value
                z[m] = decays[m] * z[m] + cot
        return tuple(x), tuple(z)

    x, z = lax.fori_loop(0, tokens // UN, edge_step, ((zero,) * modes,) * 2)
    for m in range(modes):
        edge_send[m] = jnp.concatenate([x[m], z[m]], axis=0).astype(jnp.bfloat16)
    for peer in peers:
        send(1, peer, edge_send.at[peer], edge_recv.at[me])
    edge_recv[me] = edge_send[me]

    for first in range(0, modes, GROUP):
        group = range(first, first + GROUP)

        def fwd_step(i, carry, first=first, group=group):
            x, y, ax, ay = [list(c) for c in carry]
            for u in range(UN):
                t = i * UN + u
                value = mixed[slab(t), :]
                cot = gmixed[slab(t), :]
                parts = []
                for p, m in enumerate(group):
                    a = decay[m * SUB : (m + 1) * SUB, :]
                    y[p] = a * (y[p] + x[p])
                    x[p] = a * x[p] + value
                    parts.append(gain[m * SUB : (m + 1) * SUB, :] * x[p])
                    ax[p] = ax[p] + cot * x[p]
                    ay[p] = ay[p] + cot * y[p]
                total = tree(parts)
                conv[slab(t), :] = conv[slab(t), :] + total if first else total
            return tuple(tuple(c) for c in (x, y, ax, ay))

        zeros = tuple(zero for _ in group)
        x, y, ax, ay = lax.fori_loop(0, tokens // UN, fwd_step, (zeros,) * 4)
        for p, m in enumerate(group):
            acc_hold[m, 0:SUB, :] = y[p]
            acc_hold[m, 2 * SUB : 3 * SUB, :] = ax[p]
            acc_hold[m, 3 * SUB : 4 * SUB, :] = ay[p]
        x = list(x)
        for t in range(tokens, extent):
            value = mixed[t * SUB : (t + 1) * SUB, :]
            total = conv[t * SUB : (t + 1) * SUB, :] if first else zero
            for p, m in enumerate(group):
                x[p] = decay[m * SUB : (m + 1) * SUB, :] * x[p] + value
                total = total + gain[m * SUB : (m + 1) * SUB, :] * x[p]
            conv[t * SUB : (t + 1) * SUB, :] = total

    my_rate = rate[slab(me), :]
    my_decay = decay[slab(me), :]
    my_gain = gain[slab(me), :]
    whole = jnp.exp(-float(tokens) * my_rate)
    arrived(1, edge_recv.at[others])
    h, z = zero, zero
    for d in range(n):
        back = n - 1 - d
        carry_hold[d, 0:SUB, :] = h
        carry_hold[back, SUB : 2 * SUB, :] = z
        h = whole * h + edge_recv[d].astype(f32)[0:SUB]
        z = whole * z + edge_recv[back].astype(f32)[SUB : 2 * SUB]
    for d in range(n):
        carry_send[d] = carry_hold[d].astype(jnp.bfloat16)
    for peer in peers:
        send(2, peer, carry_send.at[peer], carry_recv.at[me])
    carry_recv[me] = carry_send[me]

    for first in range(0, modes, GROUP):
        group = range(first, first + GROUP)

        def bwd_step(i, carry, first=first, group=group):
            z, w = [list(c) for c in carry]
            for u in range(UN):
                t = tokens - 1 - (i * UN + u)
                cot = gmixed[slab(t), :]
                parts = []
                for p, m in enumerate(group):
                    a = decay[m * SUB : (m + 1) * SUB, :]
                    z[p] = a * z[p] + cot
                    w[p] = a * w[p] + z[p]
                    parts.append(gain[m * SUB : (m + 1) * SUB, :] * z[p])
                total = tree(parts)
                conv_back[slab(t), :] = conv_back[slab(t), :] + total if first else total
            return tuple(tuple(c) for c in (z, w))

        zeros = tuple(zero for _ in group)
        z, w = lax.fori_loop(0, tokens // UN, bwd_step, (zeros,) * 2)
        for p, m in enumerate(group):
            acc_hold[m, SUB : 2 * SUB, :] = w[p]

    for m in range(modes):
        acc_send[m] = acc_hold[m].astype(jnp.bfloat16)
    for peer in peers:
        send(3, peer, acc_send.at[peer], acc_recv.at[me])
    acc_recv[me] = acc_send[me]

    arrived(2, carry_recv.at[others])
    gains = per_mode(gain)
    carried = [carry_recv[m].astype(f32) for m in range(modes)]

    def fwd_two(i, c):
        c = list(c)
        for u in range(2):
            t = i * 2 + u
            c = [decays[m] * c[m] for m in range(modes)]
            total = rounded(conv[slab(t), :] + tree(c))
            prod[slab(t), :] = hats[0, slab(t), :] * total
            cots[0, slab(t), :] = streams[3, slab(t + HALO), :] * total
        return tuple(c)

    start = tuple(gains[m] * carried[m][0:SUB] for m in range(modes))
    lax.fori_loop(0, extent // 2, fwd_two, start)

    def store_back(t, total):
        total = rounded(total)
        cots[1, slab(t), :] = hats[2, slab(t), :] * total
        cots[2, slab(t), :] = hats[1, slab(t), :] * total

    def bwd_two(i, c):
        c = list(c)
        for u in range(2):
            t = tokens - 1 - (i * 2 + u)
            c = [decays[m] * c[m] for m in range(modes)]
            store_back(t, conv_back[slab(t), :] + tree(c))
        return tuple(c)

    start = tuple(gains[m] * carried[m][SUB : 2 * SUB] for m in range(modes))
    lax.fori_loop(0, tokens // 2, bwd_two, start)

    ahead = [zero] * HALO
    for m in range(modes):
        grow = jnp.exp(rate[m * SUB : (m + 1) * SUB, :])
        z = carry_recv[m].astype(f32)[SUB : 2 * SUB]
        for h in range(HALO):
            ahead[h] = ahead[h] + gains[m] * z
            z = grow * (z - gmixed[(tokens + h) * SUB : (tokens + h + 1) * SUB, :])
    for h in range(HALO):
        store_back(tokens + h, ahead[h])

    def short_step(i, accs):
        accs = list(accs)
        for u in range(2):
            t = i * 2 + u
            for s in range(3):
                cot = cots[s, slab(t), :]
                for j in range(TAPS):
                    at = s * TAPS + j
                    accs[at] = accs[at] + cot * streams[s, slab(t + HALO - j), :]
        return tuple(accs)

    accs = lax.fori_loop(0, tokens // 2, short_step, (zero,) * rows_all)
    accs = list(accs) + [zero] * (2 * owners - rows_all)
    for o in range(owners):
        both = jnp.concatenate(accs[2 * o : 2 * o + 2], axis=0)
        short_send[o] = both.astype(jnp.bfloat16)
    for peer in peers:

        @pl.when(peer < owners)
        def _(peer=peer):
            send(5, peer, short_send.at[peer], short_recv.at[me])

    @pl.when(me < owners)
    def _():
        short_recv[me] = short_send[me]

    arrived(3, acc_recv.at[others])
    hy, acc_x, acc_y = zero, zero, zero
    for d in range(n):
        h = carry_hold[d, 0:SUB, :]
        terms = acc_recv[d].astype(f32)
        z0 = my_decay * edge_recv[d].astype(f32)[SUB : 2 * SUB]
        z1 = my_decay * terms[SUB : 2 * SUB]
        acc_x = acc_x + (terms[2 * SUB : 3 * SUB] + h * z0)
        acc_y = acc_y + (terms[3 * SUB : 4 * SUB] + h * z1 + hy * z0)
        hy = whole * (hy + float(tokens) * h) + terms[0:SUB]
    grad_res = acc_x * jnp.sqrt(2.0 * my_rate) * scale
    grad_log = my_gain * (0.5 * acc_x - my_rate * acc_y) * scale
    for b in range(SUB):
        modal_send[b, 0:1, :] = grad_res[b : b + 1, :]
        modal_send[b, 1:2, :] = grad_log[b : b + 1, :]
    for peer in peers:
        send(4, peer, modal_send.at[lax.div(peer, 2)], modal_recv.at[me])
    modal_recv[me] = modal_send[lax.div(me, 2)]

    def taps_step(t):
        for s in range(3):
            total = taps[s][0] * cots[s, slab(t), :]
            for j in range(1, TAPS):
                total = total + taps[s][j] * cots[s, slab(t + j), :]
            hats[s, slab(t), :] = total

    token_loop(0, tokens, 2, taps_step)

    @pl.when(me < owners)
    def _():
        arrived(5, short_recv.at[others])
        total = short_recv[0].astype(f32)
        for d in range(1, n):
            total = total + short_recv[d].astype(f32)
        total_send[...] = total * scale
        for peer in peers:
            send(6, peer, total_send, total_recv.at[me])
        total_recv[me] = total_send[...]

    stores = []
    outs = (out_ref, gq_ref, gk_ref, gv_ref)
    for first in (0, 2):
        for b in range(SUB):
            rows = pl.ds(b, tokens, stride=SUB)
            one = hats[first - 1, rows, :] if first else prod[rows, :]
            block = jnp.concatenate([one, hats[first, rows, :]], axis=0)
            block = turned(block.astype(jnp.bfloat16)).astype(jnp.bfloat16)
            for half in range(2):
                results[first + half, b * LANE : (b + 1) * LANE, :] = block[
                    :, half * LANE : (half + 1) * LANE
                ]
        for s in (first, first + 1):
            stores.append(pltpu.make_async_copy(results.at[s], outs[s], store_sem.at[s]))
            stores[-1].start()

    arrived(4, modal_recv.at[others])
    odd_owner = lax.rem(me, 2) == 1
    for at, ref in ((0, res_ref), (1, log_ref)):
        table = jnp.concatenate([modal_recv[m, at : at + 1, :] for m in range(modes)], axis=0)
        table = jnp.where(odd_owner, pltpu.roll(table, LANE // 2, 1), table)
        ref[...] = table[:, : LANE // 2]

    @pl.when(me < owners)
    def _():
        arrived(6, total_recv.at[pl.ds(0, owners - 1)])
        sent(5, short_recv.at[pl.ds(0, owners - 1)])
        sent(6, carry_hold.at[others])

    @pl.when(me >= owners)
    def _():
        arrived(6, total_recv)
        sent(5, short_recv.at[pl.ds(0, owners)])

    for s in range(3):
        for b in range(SUB):
            for j in range(TAPS):
                row = s * TAPS + j
                at = (row % 2) * SUB + b
                short_ref[s, j : j + 1, b * LANE : (b + 1) * LANE] = total_recv[
                    row // 2, at : at + 1, :
                ]

    for store in stores:
        store.wait()
    sent(0, params.at[others])
    sent(1, edge_recv.at[others])
    sent(2, carry_recv.at[others])
    sent(3, acc_recv.at[others])
    sent(4, modal_recv.at[others])


def hand_over(count, *refs):
    sources, targets, held = refs[:count], refs[count : 2 * count], refs[2 * count : -2]
    load_sem, store_sem = refs[-2:]
    loads = [
        pltpu.make_async_copy(sources[i], held[i], load_sem.at[i]) for i in range(count)
    ]
    stores = [
        pltpu.make_async_copy(held[i], targets[i], store_sem.at[i]) for i in range(count)
    ]
    for load in loads:
        load.start()
    for load, store in zip(loads, stores):
        load.wait()
        store.start()
    for store in stores:
        store.wait()


def local(query_in, key_in, value_in, short_weight, residue, log_rate, grad_out):
    n = lax.axis_size("seq")
    width, tokens = query_in.shape
    own, modes = residue.shape
    fits = width == SUB * LANE and tokens == LANE and modes == n == 2 * SUB
    if not (fits and own == LANE // 2):
        return local_fft(
            query_in, key_in, value_in, short_weight, residue, log_rate, grad_out
        )
    scale = 1.0 / math.sqrt(tokens * n)
    f32 = jnp.float32
    rows = (tokens + HALO) * SUB
    owners = (3 * TAPS + 1) // 2
    param = jnp.concatenate([log_rate.T, residue.T], axis=1)
    vmem = pl.BlockSpec(memory_space=pltpu.VMEM)
    hbm = pl.BlockSpec(memory_space=pltpu.MemorySpace.HBM)
    pair = pltpu.VMEM((n, 2 * SUB, LANE), f32)
    quad = pltpu.VMEM((n, 4 * SUB, LANE), f32)
    half_pair = pltpu.VMEM((n, 2 * SUB, LANE), jnp.bfloat16)
    half_quad = pltpu.VMEM((n, 4 * SUB, LANE), jnp.bfloat16)
    flat = pltpu.VMEM((rows, LANE), f32)
    triple = pltpu.VMEM((3, rows, LANE), f32)
    small = pltpu.VMEM((modes * SUB, LANE), f32)
    shape = jax.ShapeDtypeStruct((width, tokens), jnp.bfloat16)
    modal = jax.ShapeDtypeStruct((modes, own), f32)
    results = pl.pallas_call(
        functools.partial(layer_kernel, n, modes, tokens, scale),
        out_shape=(
            shape, shape, shape, shape,
            jax.ShapeDtypeStruct(short_weight.shape, f32), modal, modal,
        ),
        in_specs=[hbm] * 4 + [vmem] * 2,
        out_specs=(hbm,) * 4 + (vmem,) * 3,
        scratch_shapes=[
            pltpu.VMEM((4, width, tokens), jnp.bfloat16),
            pltpu.VMEM((4, width, tokens), jnp.bfloat16),
            pltpu.VMEM((4, rows + HALO * SUB, LANE), f32),
            triple, flat, flat, flat, flat, flat, triple,
            pltpu.VMEM((3 * TAPS * SUB, LANE), f32),
            pltpu.VMEM((n, modes, LANE), f32),
            small, small, small,
            half_pair, half_pair, quad, half_quad, half_quad,
            pair, half_pair, half_pair,
            pltpu.VMEM((SUB, 2, LANE), f32),
            pltpu.VMEM((n, 2, LANE), f32),
            pltpu.VMEM((owners, 2 * SUB, LANE), jnp.bfloat16),
            half_pair,
            pltpu.VMEM((2 * SUB, LANE), f32),
            pltpu.VMEM((owners, 2 * SUB, LANE), f32),
            pltpu.SemaphoreType.DMA((4,)),
            pltpu.SemaphoreType.DMA((4,)),
            pltpu.SemaphoreType.DMA((7,)),
            pltpu.SemaphoreType.DMA((7,)),
            pltpu.SemaphoreType.DMA((2,)),
            pltpu.SemaphoreType.DMA((2,)),
        ],
        compiler_params=pltpu.CompilerParams(
            collective_id=0, has_side_effects=True, vmem_limit_bytes=56 * 2**20
        ),
    )(query_in, key_in, value_in, grad_out, short_weight, param)
    count = len(results)
    results = pl.pallas_call(
        functools.partial(hand_over, count),
        out_shape=[jax.ShapeDtypeStruct(r.shape, r.dtype) for r in results],
        in_specs=[hbm] * count,
        out_specs=[hbm] * count,
        scratch_shapes=[pltpu.VMEM(r.shape, r.dtype) for r in results]
        + [pltpu.SemaphoreType.DMA((count,))] * 2,
        compiler_params=pltpu.CompilerParams(vmem_limit_bytes=60 * 2**20),
    )(*results)
    return (*results[:5], results[5].T, results[6].T)


def solution(mesh):
    return jax.shard_map(
        local,
        mesh=mesh,
        in_specs=(
            P("chan", "seq"),
            P("chan", "seq"),
            P("chan", "seq"),
            P(None, None, "chan"),
            P(("chan", "seq"), None),
            P(("chan", "seq"), None),
            P("chan", "seq"),
        ),
        out_specs=(
            P("chan", "seq"),
            P("chan", "seq"),
            P("chan", "seq"),
            P("chan", "seq"),
            P(None, None, "chan"),
            P(("chan", "seq"), None),
            P(("chan", "seq"), None),
        ),
        check_vma=False,
    )
```

```python
import functools
import math

import jax
import jax.numpy as jnp
from jax import lax
from jax.experimental import pallas as pl
from jax.experimental.pallas import tpu as pltpu
from jax.sharding import PartitionSpec as P


def shifted(shard, axis, by):
    count = lax.axis_size(axis)
    pairs = [(i, i + by) for i in range(count) if 0 <= i + by < count]
    return lax.ppermute(shard, axis, pairs)


def dft_table(length, sign):
    counter = jnp.arange(length, dtype=jnp.int32)
    product = counter[:, None] * counter[None, :] % length
    angle = product.astype(jnp.float32) * (sign * 2.0 * math.pi / length)
    return (jnp.cos(angle), jnp.sin(angle))


def complex_dot(real_part, imag_part, table_real, table_imag):
    highest = lax.Precision.HIGHEST
    out_real = jnp.matmul(real_part, table_real, precision=highest) - jnp.matmul(
        imag_part, table_imag, precision=highest
    )
    out_imag = jnp.matmul(real_part, table_imag, precision=highest) + jnp.matmul(
        imag_part, table_real, precision=highest
    )
    return (out_real, out_imag)


def transform(real_part, imag_part, sign):
    length = real_part.shape[-1]
    if length <= 256 or length % 128 != 0:
        table_real, table_imag = dft_table(length, sign)
        return complex_dot(real_part, imag_part, table_real, table_imag)
    outer = 128
    inner = length // outer
    leading = real_part.shape[:-1]
    split_real = jnp.swapaxes(real_part.reshape(leading + (inner, outer)), -1, -2)
    split_imag = jnp.swapaxes(imag_part.reshape(leading + (inner, outer)), -1, -2)
    part_real, part_imag = transform(split_real, split_imag, sign)
    first_index = jnp.arange(outer, dtype=jnp.int32)[:, None]
    second_index = jnp.arange(inner, dtype=jnp.int32)[None, :]
    angle = (first_index * second_index % length).astype(jnp.float32) * (
        sign * 2.0 * math.pi / length
    )
    twist_real = jnp.cos(angle)
    twist_imag = jnp.sin(angle)
    turned_real = part_real * twist_real - part_imag * twist_imag
    turned_imag = part_real * twist_imag + part_imag * twist_real
    table_real, table_imag = dft_table(outer, sign)
    highest = lax.Precision.HIGHEST
    out_real = jnp.einsum(
        "...nk,nl->...lk", turned_real, table_real, precision=highest
    ) - jnp.einsum("...nk,nl->...lk", turned_imag, table_imag, precision=highest)
    out_imag = jnp.einsum(
        "...nk,nl->...lk", turned_real, table_imag, precision=highest
    ) + jnp.einsum("...nk,nl->...lk", turned_imag, table_real, precision=highest)
    return (out_real.reshape(leading + (length,)), out_imag.reshape(leading + (length,)))


def spectrum(signal):
    length = signal.shape[1]
    padded = jnp.pad(signal.astype(jnp.float32), ((0, 0), (0, length)))
    return transform(padded, jnp.zeros_like(padded), -1.0)


def mirrored(values):
    return jnp.roll(jnp.flip(values, -1), 1, -1)


def paired_spectra(first, second):
    length = first.shape[1]
    first_pad = jnp.pad(first, ((0, 0), (0, length)))
    second_pad = jnp.pad(second.astype(jnp.float32), ((0, 0), (0, length)))
    joint_real, joint_imag = transform(first_pad, second_pad, -1.0)
    mirror_real = mirrored(joint_real)
    mirror_imag = mirrored(joint_imag)
    first_spec = (0.5 * (joint_real + mirror_real), 0.5 * (joint_imag - mirror_imag))
    second_spec = (0.5 * (joint_imag + mirror_imag), -0.5 * (joint_real - mirror_real))
    return (first_spec, second_spec)


def to_time(spec_pair, length):
    real_part, imag_part = spec_pair
    back_real, back_imag = transform(real_part, imag_part, 1.0)
    return back_real[:, :length] / real_part.shape[-1]


def paired_time(first_spec, second_spec, length):
    joint_real = first_spec[0] - second_spec[1]
    joint_imag = first_spec[1] + second_spec[0]
    back_real, back_imag = transform(joint_real, joint_imag, 1.0)
    total_len = joint_real.shape[-1]
    return (back_real[:, :length] / total_len, back_imag[:, :length] / total_len)


def spectral_product(first, second, conjugate):
    first_real, first_imag = first
    second_real, second_imag = second
    if conjugate:
        second_imag = -second_imag
    return (
        first_real * second_real - first_imag * second_imag,
        first_real * second_imag + first_imag * second_real,
    )


def modal_filter(residue, log_rate, length):
    decay_rate = jnp.exp(log_rate)
    offsets = jnp.arange(length).astype(jnp.float32)
    filt = jnp.zeros((residue.shape[0], length), jnp.float32)
    for mode_index in range(residue.shape[1]):
        factor = residue[:, mode_index] * jnp.sqrt(2.0 * decay_rate[:, mode_index])
        filt = filt + factor[:, None] * jnp.exp(-decay_rate[:, mode_index][:, None] * offsets)
    return filt


def modal_grads(filt_grad, residue, log_rate):
    decay_rate = jnp.exp(log_rate)
    offsets = jnp.arange(filt_grad.shape[1]).astype(jnp.float32)
    res_terms = []
    log_terms = []
    for mode_index in range(residue.shape[1]):
        rate_col = decay_rate[:, mode_index][:, None]
        basis = jnp.sqrt(2.0 * rate_col) * jnp.exp(-rate_col * offsets)
        weighted = filt_grad * basis
        res_terms.append(jnp.sum(weighted, axis=1))
        log_terms.append(
            residue[:, mode_index] * jnp.sum(weighted * (0.5 - rate_col * offsets), axis=1)
        )
    return (jnp.stack(res_terms, axis=1), jnp.stack(log_terms, axis=1))


def apply_taps(widened, taps, tok_rows):
    total = jnp.zeros((widened.shape[0], tok_rows), jnp.float32)
    for offset in range(7):
        total = total + taps[offset][:, None] * widened[:, 6 - offset : 6 - offset + tok_rows]
    return total


def taps_back(gradient, following, taps):
    tok_rows = gradient.shape[1]
    widened = jnp.concatenate([gradient, following], axis=1)
    total = jnp.zeros_like(gradient)
    for offset in range(7):
        total = total + taps[offset][:, None] * widened[:, offset : offset + tok_rows]
    return total


def taps_gradient(gradient, widened):
    tok_rows = gradient.shape[1]
    rows_out = [
        jnp.sum(gradient * widened[:, 6 - offset : 6 - offset + tok_rows], axis=1)
        for offset in range(7)
    ]
    return jnp.stack(rows_out, axis=0)


def to_channels(stream):
    return lax.all_to_all(stream, "seq", split_axis=0, concat_axis=1, tiled=True)


def to_tokens(stream):
    return lax.all_to_all(stream, "seq", split_axis=1, concat_axis=0, tiled=True)


def local_fft(query_in, key_in, value_in, short_weight, residue, log_rate, grad_out):
    tok_rows = query_in.shape[1]
    length = tok_rows * lax.axis_size("seq")
    scale = 1.0 / math.sqrt(length)
    tails = shifted((query_in[:, -6:], key_in[:, -6:], value_in[:, -6:]), "seq", 1)
    query_wide = jnp.concatenate([tails[0], query_in], axis=1).astype(jnp.float32)
    key_wide = jnp.concatenate([tails[1], key_in], axis=1).astype(jnp.float32)
    value_wide = jnp.concatenate([tails[2], value_in], axis=1).astype(jnp.float32)
    query_hat = apply_taps(query_wide, short_weight[0], tok_rows)
    key_hat = apply_taps(key_wide, short_weight[1], tok_rows)
    value_hat = apply_taps(value_wide, short_weight[2], tok_rows)
    mixed = (key_hat * value_hat).astype(jnp.bfloat16)
    grad_up = grad_out.astype(jnp.float32)
    grad_mixed = (grad_up * query_hat).astype(jnp.bfloat16)
    mixed_cols = to_channels(mixed)
    filt = modal_filter(residue, log_rate, length)
    spec_filter, spec_mixed = paired_spectra(filt, mixed_cols)
    long_out = to_time(spectral_product(spec_mixed, spec_filter, False), length).astype(
        jnp.bfloat16
    )
    conv_out = to_tokens(long_out)
    grad_cols = to_channels(grad_mixed)
    spec_grad = spectrum(grad_cols)
    long_grad, filt_grad = paired_time(
        spectral_product(spec_grad, spec_filter, True),
        spectral_product(spec_grad, spec_mixed, True),
        length,
    )
    conv_grad = to_tokens(long_grad.astype(jnp.bfloat16))
    grad_res, grad_log = modal_grads(filt_grad, residue, log_rate)
    conv_wide = conv_out.astype(jnp.float32)
    conv_grad_wide = conv_grad.astype(jnp.float32)
    output = (query_hat * conv_wide).astype(jnp.bfloat16)
    grad_q = grad_up * conv_wide
    grad_k = conv_grad_wide * value_hat
    grad_v = conv_grad_wide * key_hat
    heads = shifted((grad_q[:, :6], grad_k[:, :6], grad_v[:, :6]), "seq", -1)
    grad_query = taps_back(grad_q, heads[0], short_weight[0]).astype(jnp.bfloat16)
    grad_key = taps_back(grad_k, heads[1], short_weight[1]).astype(jnp.bfloat16)
    grad_value = taps_back(grad_v, heads[2], short_weight[2]).astype(jnp.bfloat16)
    local_terms = jnp.stack(
        [
            taps_gradient(grad_q, query_wide),
            taps_gradient(grad_k, key_wide),
            taps_gradient(grad_v, value_wide),
        ],
        axis=0,
    )
    grad_short = lax.psum(local_terms, "seq") * scale
    return (
        output,
        grad_query,
        grad_key,
        grad_value,
        grad_short,
        grad_res * scale,
        grad_log * scale,
    )


SUB = 8
LANE = 128
HALO = 6
TAPS = 7
GROUP = 8
MESH = pl.DeviceIdType.MESH


def slab(index):
    return pl.ds(pl.multiple_of(index * SUB, SUB), SUB)


def layer_kernel(
    n, modes, tokens, scale,
    query_ref, key_ref, value_ref, grad_ref, weight_ref, rate_ref, residue_ref,
    out_ref, gq_ref, gk_ref, gv_ref, short_ref, res_ref, log_ref,
    inputs, results, tails, heads, tails_in, heads_in, param_ref, streams, hats, mixed, gmixed, conv, conv_back, prod, cots,
    weights, params, decay, gain, rate,
    edge_send, edge_recv, acc_hold, acc_send, acc_recv,
    carry_hold, carry_send, carry_recv, modal_send, modal_recv, short_send, short_recv, total_send, total_recv,
    load_sem, store_sem, send_sem, recv_sem, halo_send, halo_recv,
):
    me = lax.axis_index("seq")
    extent = tokens + HALO
    rows_all = 3 * TAPS
    owners = (rows_all + 1) // 2
    f32 = jnp.float32
    zero = jnp.zeros((SUB, LANE), f32)

    def rounded(value):
        return value.astype(jnp.bfloat16).astype(f32)

    def tree(parts):
        while len(parts) > 1:
            parts = [parts[i] + parts[i + 1] for i in range(0, len(parts), 2)]
        return parts[0]

    def per_mode(ref):
        return [ref[m * SUB : (m + 1) * SUB, :] for m in range(modes)]

    half_width = SUB * LANE // 2
    loads = []
    for s, ref in enumerate((query_ref, key_ref, value_ref, grad_ref)):
        for half in range(2):
            part = pl.ds(half * half_width, half_width)
            loads.append(
                pltpu.make_async_copy(
                    ref.at[part], inputs.at[s, part], load_sem.at[2 * s + half]
                )
            )
            loads[-1].start()

    barrier = pltpu.get_barrier_semaphore()
    peers = [lax.rem(me + k, n) for k in range(1, n)]
    for peer in peers:
        pl.semaphore_signal(
            barrier, inc=1, device_id={"seq": peer}, device_id_type=MESH
        )

    def send(phase, peer, source, target):
        pltpu.make_async_remote_copy(
            src_ref=source,
            dst_ref=target,
            send_sem=send_sem.at[phase],
            recv_sem=recv_sem.at[phase],
            device_id={"seq": peer},
            device_id_type=MESH,
        ).start()

    def sent(phase, like):
        pltpu.make_async_copy(like, like, send_sem.at[phase]).wait()

    def arrived(phase, like):
        pltpu.make_async_copy(like, like, recv_sem.at[phase]).wait()

    others = pl.ds(0, n - 1)
    param_ref[...] = jnp.concatenate([rate_ref[...], residue_ref[...]], axis=1)

    for s in range(3):
        for b in range(SUB):
            weights[pl.ds(s * TAPS * SUB + b, TAPS, stride=SUB), :] = weight_ref[
                s, :, b * LANE : (b + 1) * LANE
            ]

    eye = (
        lax.broadcasted_iota(jnp.int32, (LANE, LANE), 0)
        == lax.broadcasted_iota(jnp.int32, (LANE, LANE), 1)
    ).astype(jnp.bfloat16)

    def turned(block):
        return lax.dot_general(
            eye, block, (((1,), (1,)), ((), ())), preferred_element_type=f32
        )

    for s in range(4):
        for b in range(0, SUB, 2):
            if b % (SUB // 2) == 0:
                loads[2 * s + b // (SUB // 2)].wait()
            block = turned(inputs[s, b * LANE : (b + 2) * LANE, :])
            for half in range(2):
                streams[s, pl.ds(HALO * SUB + b + half, tokens, stride=SUB), :] = block[
                    :, half * LANE : (half + 1) * LANE
                ]
        if s == 1:
            pl.semaphore_wait(barrier, n - 1)
            for peer in peers:
                send(0, peer, param_ref, params.at[me])
            params[me] = param_ref[...]

    edge = HALO * SUB
    last = tokens * SUB
    to_right = lambda: pltpu.make_async_remote_copy(
        src_ref=tails,
        dst_ref=tails_in,
        send_sem=halo_send.at[0],
        recv_sem=halo_recv.at[0],
        device_id={"seq": lax.rem(me + 1, n)},
        device_id_type=MESH,
    )
    to_left = lambda: pltpu.make_async_remote_copy(
        src_ref=heads,
        dst_ref=heads_in,
        send_sem=halo_send.at[1],
        recv_sem=halo_recv.at[1],
        device_id={"seq": lax.rem(me + n - 1, n)},
        device_id_type=MESH,
    )
    for s in range(3):
        tails[s] = streams[s, last : last + edge, :].astype(jnp.bfloat16)
    for s in range(4):
        heads[s] = streams[s, edge : 2 * edge, :].astype(jnp.bfloat16)

    @pl.when(me < n - 1)
    def _():
        to_right().start()

    @pl.when(me > 0)
    def _():
        to_left().start()

    taps = [
        [weights[(s * TAPS + j) * SUB : (s * TAPS + j + 1) * SUB, :] for j in range(TAPS)]
        for s in range(3)
    ]

    def filter_token(t):
        vals = []
        for s in range(3):
            total = taps[s][0] * streams[s, slab(t + HALO), :]
            for j in range(1, TAPS):
                total = total + taps[s][j] * streams[s, slab(t + HALO - j), :]
            hats[s, slab(t), :] = total
            vals.append(total)
        mixed[slab(t), :] = rounded(vals[1] * vals[2])
        gmixed[slab(t), :] = rounded(vals[0] * streams[3, slab(t + HALO), :])

    def token_loop(lo, hi, unroll, fn):
        def step(i, carry):
            for u in range(unroll):
                fn(lo + i * unroll + u)
            return carry

        lax.fori_loop(0, (hi - lo) // unroll, step, 0)

    token_loop(HALO, tokens, 2, filter_token)

    arrived(0, params.at[others])
    low_half = lax.broadcasted_iota(jnp.int32, (SUB, LANE), 1) < LANE // 2
    for m in range(modes):
        even = jnp.concatenate([params[2 * b, m : m + 1, :] for b in range(SUB)], axis=0)
        odd = jnp.concatenate([params[2 * b + 1, m : m + 1, :] for b in range(SUB)], axis=0)
        log_rate = jnp.where(low_half, even, pltpu.roll(odd, LANE // 2, 1))
        residue = jnp.where(low_half, pltpu.roll(even, LANE // 2, 1), odd)
        r = jnp.exp(log_rate)
        rate[slab(m), :] = r
        decay[slab(m), :] = jnp.exp(-r)
        gain[slab(m), :] = residue * jnp.sqrt(2.0 * r)

    UN = 4
    decays = per_mode(decay)

    def edge_step(i, carry):
        x, z = [list(c) for c in carry]
        for u in range(2):
            t = i * 2 + u
            value = mixed[slab(t + HALO), :]
            cot = gmixed[slab(tokens - 1 - t), :]
            for m in range(modes):
                x[m] = decays[m] * x[m] + value
                z[m] = decays[m] * z[m] + cot
        return tuple(x), tuple(z)

    inner = tokens - HALO
    x, z = lax.fori_loop(0, inner // 2, edge_step, ((zero,) * modes,) * 2)
    @pl.when(me > 0)
    def _():
        to_left().wait_send()
        to_right().wait_recv()
        for s in range(3):
            streams[s, 0:edge, :] = tails_in[s].astype(f32)

    @pl.when(me == 0)
    def _():
        streams[0:3, 0:edge, :] = jnp.zeros((3, edge, LANE), f32)

    @pl.when(me < n - 1)
    def _():
        to_right().wait_send()
        to_left().wait_recv()
        for s in range(4):
            streams[s, edge + last : 2 * edge + last, :] = heads_in[s].astype(f32)

    @pl.when(me == n - 1)
    def _():
        streams[:, edge + last : 2 * edge + last, :] = jnp.zeros((4, edge, LANE), f32)

    token_loop(0, HALO, 2, filter_token)
    token_loop(tokens, extent, 2, filter_token)

    x, z = list(x), list(z)
    for m in range(modes):
        early = zero
        for t in range(HALO):
            back = HALO - 1 - t
            early = decays[m] * early + mixed[t * SUB : (t + 1) * SUB, :]
            z[m] = decays[m] * z[m] + gmixed[back * SUB : (back + 1) * SUB, :]
        x[m] = x[m] + jnp.exp(-float(inner) * rate[m * SUB : (m + 1) * SUB, :]) * early
    for m in range(modes):
        edge_send[m] = jnp.concatenate([x[m], z[m]], axis=0).astype(jnp.bfloat16)
    for peer in peers:
        send(1, peer, edge_send.at[peer], edge_recv.at[me])
    edge_recv[me] = edge_send[me]

    for first in range(0, modes, GROUP):
        group = range(first, first + GROUP)

        def fwd_step(i, carry, first=first, group=group):
            x, y, ax, ay = [list(c) for c in carry]
            for u in range(UN):
                t = i * UN + u
                value = mixed[slab(t), :]
                cot = gmixed[slab(t), :]
                parts = []
                for p, m in enumerate(group):
                    a = decay[m * SUB : (m + 1) * SUB, :]
                    y[p] = a * (y[p] + x[p])
                    x[p] = a * x[p] + value
                    parts.append(gain[m * SUB : (m + 1) * SUB, :] * x[p])
                    ax[p] = ax[p] + cot * x[p]
                    ay[p] = ay[p] + cot * y[p]
                total = tree(parts)
                conv[slab(t), :] = conv[slab(t), :] + total if first else total
            return tuple(tuple(c) for c in (x, y, ax, ay))

        zeros = tuple(zero for _ in group)
        x, y, ax, ay = lax.fori_loop(0, tokens // UN, fwd_step, (zeros,) * 4)
        for p, m in enumerate(group):
            acc_hold[m, 0:SUB, :] = y[p]
            acc_hold[m, 2 * SUB : 3 * SUB, :] = ax[p]
            acc_hold[m, 3 * SUB : 4 * SUB, :] = ay[p]
        x = list(x)
        for t in range(tokens, extent):
            value = mixed[t * SUB : (t + 1) * SUB, :]
            total = conv[t * SUB : (t + 1) * SUB, :] if first else zero
            for p, m in enumerate(group):
                x[p] = decay[m * SUB : (m + 1) * SUB, :] * x[p] + value
                total = total + gain[m * SUB : (m + 1) * SUB, :] * x[p]
            conv[t * SUB : (t + 1) * SUB, :] = total

    my_rate = rate[slab(me), :]
    my_decay = decay[slab(me), :]
    my_gain = gain[slab(me), :]
    whole = jnp.exp(-float(tokens) * my_rate)
    arrived(1, edge_recv.at[others])
    h, z = zero, zero
    for d in range(n):
        back = n - 1 - d
        carry_hold[d, 0:SUB, :] = h
        carry_hold[back, SUB : 2 * SUB, :] = z
        h = whole * h + edge_recv[d].astype(f32)[0:SUB]
        z = whole * z + edge_recv[back].astype(f32)[SUB : 2 * SUB]
    for d in range(n):
        carry_send[d] = carry_hold[d].astype(jnp.bfloat16)
    for peer in peers:
        send(2, peer, carry_send.at[peer], carry_recv.at[me])
    carry_recv[me] = carry_send[me]

    for first in range(0, modes, GROUP):
        group = range(first, first + GROUP)

        def bwd_step(i, carry, first=first, group=group):
            z, w = [list(c) for c in carry]
            for u in range(UN):
                t = tokens - 1 - (i * UN + u)
                cot = gmixed[slab(t), :]
                parts = []
                for p, m in enumerate(group):
                    a = decay[m * SUB : (m + 1) * SUB, :]
                    z[p] = a * z[p] + cot
                    w[p] = a * w[p] + z[p]
                    parts.append(gain[m * SUB : (m + 1) * SUB, :] * z[p])
                total = tree(parts)
                conv_back[slab(t), :] = conv_back[slab(t), :] + total if first else total
            return tuple(tuple(c) for c in (z, w))

        zeros = tuple(zero for _ in group)
        z, w = lax.fori_loop(0, tokens // UN, bwd_step, (zeros,) * 2)
        for p, m in enumerate(group):
            acc_hold[m, SUB : 2 * SUB, :] = w[p]

    for m in range(modes):
        acc_send[m] = acc_hold[m].astype(jnp.bfloat16)
    for peer in peers:
        send(3, peer, acc_send.at[peer], acc_recv.at[me])
    acc_recv[me] = acc_send[me]

    arrived(2, carry_recv.at[others])
    gains = per_mode(gain)
    carried = [carry_recv[m].astype(f32) for m in range(modes)]

    def fwd_two(i, c):
        c = list(c)
        for u in range(2):
            t = i * 2 + u
            c = [decays[m] * c[m] for m in range(modes)]
            total = rounded(conv[slab(t), :] + tree(c))
            prod[slab(t), :] = hats[0, slab(t), :] * total
            cots[0, slab(t), :] = streams[3, slab(t + HALO), :] * total
        return tuple(c)

    start = tuple(gains[m] * carried[m][0:SUB] for m in range(modes))
    lax.fori_loop(0, extent // 2, fwd_two, start)

    def store_back(t, total):
        total = rounded(total)
        cots[1, slab(t), :] = hats[2, slab(t), :] * total
        cots[2, slab(t), :] = hats[1, slab(t), :] * total

    def bwd_two(i, c):
        c = list(c)
        for u in range(2):
            t = tokens - 1 - (i * 2 + u)
            c = [decays[m] * c[m] for m in range(modes)]
            store_back(t, conv_back[slab(t), :] + tree(c))
        return tuple(c)

    start = tuple(gains[m] * carried[m][SUB : 2 * SUB] for m in range(modes))
    lax.fori_loop(0, tokens // 2, bwd_two, start)

    ahead = [zero] * HALO
    for m in range(modes):
        grow = jnp.exp(rate[m * SUB : (m + 1) * SUB, :])
        z = carry_recv[m].astype(f32)[SUB : 2 * SUB]
        for h in range(HALO):
            ahead[h] = ahead[h] + gains[m] * z
            z = grow * (z - gmixed[(tokens + h) * SUB : (tokens + h + 1) * SUB, :])
    for h in range(HALO):
        store_back(tokens + h, ahead[h])

    def short_step(i, accs):
        accs = list(accs)
        for u in range(2):
            t = i * 2 + u
            for s in range(3):
                cot = cots[s, slab(t), :]
                for j in range(TAPS):
                    at = s * TAPS + j
                    accs[at] = accs[at] + cot * streams[s, slab(t + HALO - j), :]
        return tuple(accs)

    accs = lax.fori_loop(0, tokens // 2, short_step, (zero,) * rows_all)
    accs = list(accs) + [zero] * (2 * owners - rows_all)
    for o in range(owners):
        both = jnp.concatenate(accs[2 * o : 2 * o + 2], axis=0)
        short_send[o] = both.astype(jnp.bfloat16)
    for peer in peers:

        @pl.when(peer < owners)
        def _(peer=peer):
            send(5, peer, short_send.at[peer], short_recv.at[me])

    @pl.when(me < owners)
    def _():
        short_recv[me] = short_send[me]

    arrived(3, acc_recv.at[others])
    hy, acc_x, acc_y = zero, zero, zero
    for d in range(n):
        h = carry_hold[d, 0:SUB, :]
        terms = acc_recv[d].astype(f32)
        z0 = my_decay * edge_recv[d].astype(f32)[SUB : 2 * SUB]
        z1 = my_decay * terms[SUB : 2 * SUB]
        acc_x = acc_x + (terms[2 * SUB : 3 * SUB] + h * z0)
        acc_y = acc_y + (terms[3 * SUB : 4 * SUB] + h * z1 + hy * z0)
        hy = whole * (hy + float(tokens) * h) + terms[0:SUB]
    grad_res = acc_x * jnp.sqrt(2.0 * my_rate) * scale
    grad_log = my_gain * (0.5 * acc_x - my_rate * acc_y) * scale
    for b in range(SUB):
        modal_send[b, 0:1, :] = grad_res[b : b + 1, :]
        modal_send[b, 1:2, :] = grad_log[b : b + 1, :]
    for peer in peers:
        send(4, peer, modal_send.at[lax.div(peer, 2)], modal_recv.at[me])
    modal_recv[me] = modal_send[lax.div(me, 2)]

    def taps_step(t):
        for s in range(3):
            total = taps[s][0] * cots[s, slab(t), :]
            for j in range(1, TAPS):
                total = total + taps[s][j] * cots[s, slab(t + j), :]
            hats[s, slab(t), :] = total

    token_loop(0, tokens, 2, taps_step)

    @pl.when(me < owners)
    def _():
        arrived(5, short_recv.at[others])
        total = short_recv[0].astype(f32)
        for d in range(1, n):
            total = total + short_recv[d].astype(f32)
        total_send[...] = (total * scale).astype(jnp.bfloat16)
        for peer in peers:
            send(6, peer, total_send, total_recv.at[me])
        total_recv[me] = total_send[...]

    stores = []
    outs = (out_ref, gq_ref, gk_ref, gv_ref)
    for first in (0, 2):
        for b in range(SUB):
            rows = pl.ds(b, tokens, stride=SUB)
            one = hats[first - 1, rows, :] if first else prod[rows, :]
            block = jnp.concatenate([one, hats[first, rows, :]], axis=0)
            block = turned(block.astype(jnp.bfloat16)).astype(jnp.bfloat16)
            for half in range(2):
                results[first + half, b * LANE : (b + 1) * LANE, :] = block[
                    :, half * LANE : (half + 1) * LANE
                ]
        for s in (first, first + 1):
            stores.append(pltpu.make_async_copy(results.at[s], outs[s], store_sem.at[s]))
            stores[-1].start()

    arrived(4, modal_recv.at[others])
    odd_owner = lax.rem(me, 2) == 1
    for at, ref in ((0, res_ref), (1, log_ref)):
        table = jnp.concatenate([modal_recv[m, at : at + 1, :] for m in range(modes)], axis=0)
        table = jnp.where(odd_owner, pltpu.roll(table, LANE // 2, 1), table)
        ref[...] = table[:, : LANE // 2]

    @pl.when(me < owners)
    def _():
        arrived(6, total_recv.at[pl.ds(0, owners - 1)])
        sent(5, short_recv.at[pl.ds(0, owners - 1)])
        sent(6, short_recv.at[others])

    @pl.when(me >= owners)
    def _():
        arrived(6, total_recv)
        sent(5, short_recv.at[pl.ds(0, owners)])

    for o in range(owners):
        both = total_recv[o].astype(f32)
        for row in range(2 * o, min(2 * o + 2, rows_all)):
            s, j = row // TAPS, row % TAPS
            for b in range(SUB):
                at = (row % 2) * SUB + b
                short_ref[s, j : j + 1, b * LANE : (b + 1) * LANE] = both[at : at + 1]

    for store in stores:
        store.wait()
    sent(0, params.at[others])
    sent(1, edge_recv.at[others])
    sent(2, carry_recv.at[others])
    sent(3, acc_recv.at[others])
    sent(4, modal_recv.at[others])


def hand_over(count, *refs):
    sources, targets, held = refs[:count], refs[count : 2 * count], refs[2 * count : -2]
    load_sem, store_sem = refs[-2:]
    loads = [
        pltpu.make_async_copy(sources[i], held[i], load_sem.at[i]) for i in range(count)
    ]
    stores = [
        pltpu.make_async_copy(held[i], targets[i], store_sem.at[i]) for i in range(count)
    ]
    for load in loads:
        load.start()
    for load, store in zip(loads, stores):
        load.wait()
        store.start()
    for store in stores:
        store.wait()


def local(query_in, key_in, value_in, short_weight, residue, log_rate, grad_out):
    n = lax.axis_size("seq")
    width, tokens = query_in.shape
    own, modes = residue.shape
    fits = width == SUB * LANE and tokens == LANE and modes == n == 2 * SUB
    if not (fits and own == LANE // 2):
        return local_fft(
            query_in, key_in, value_in, short_weight, residue, log_rate, grad_out
        )
    scale = 1.0 / math.sqrt(tokens * n)
    f32 = jnp.float32
    rows = (tokens + HALO) * SUB
    owners = (3 * TAPS + 1) // 2
    vmem = pl.BlockSpec(memory_space=pltpu.VMEM)
    hbm = pl.BlockSpec(memory_space=pltpu.MemorySpace.HBM)
    pair = pltpu.VMEM((n, 2 * SUB, LANE), f32)
    quad = pltpu.VMEM((n, 4 * SUB, LANE), f32)
    half_pair = pltpu.VMEM((n, 2 * SUB, LANE), jnp.bfloat16)
    half_quad = pltpu.VMEM((n, 4 * SUB, LANE), jnp.bfloat16)
    tail = pltpu.VMEM((3, HALO * SUB, LANE), jnp.bfloat16)
    head = pltpu.VMEM((4, HALO * SUB, LANE), jnp.bfloat16)
    flat = pltpu.VMEM((rows, LANE), f32)
    triple = pltpu.VMEM((3, rows, LANE), f32)
    small = pltpu.VMEM((modes * SUB, LANE), f32)
    shape = jax.ShapeDtypeStruct((width, tokens), jnp.bfloat16)
    modal = jax.ShapeDtypeStruct((modes, own), f32)
    results = pl.pallas_call(
        functools.partial(layer_kernel, n, modes, tokens, scale),
        out_shape=(
            shape, shape, shape, shape,
            jax.ShapeDtypeStruct(short_weight.shape, f32), modal, modal,
        ),
        in_specs=[hbm] * 4 + [vmem] * 3,
        out_specs=(hbm,) * 4 + (vmem,) * 3,
        scratch_shapes=[
            pltpu.VMEM((4, width, tokens), jnp.bfloat16),
            pltpu.VMEM((4, width, tokens), jnp.bfloat16),
            tail, head, tail, head,
            pltpu.VMEM((modes, LANE), f32),
            pltpu.VMEM((4, rows + HALO * SUB, LANE), f32),
            triple, flat, flat, flat, flat, flat, triple,
            pltpu.VMEM((3 * TAPS * SUB, LANE), f32),
            pltpu.VMEM((n, modes, LANE), f32),
            small, small, small,
            half_pair, half_pair, quad, half_quad, half_quad,
            pair, half_pair, half_pair,
            pltpu.VMEM((SUB, 2, LANE), f32),
            pltpu.VMEM((n, 2, LANE), f32),
            pltpu.VMEM((owners, 2 * SUB, LANE), jnp.bfloat16),
            half_pair,
            pltpu.VMEM((2 * SUB, LANE), jnp.bfloat16),
            pltpu.VMEM((owners, 2 * SUB, LANE), jnp.bfloat16),
            pltpu.SemaphoreType.DMA((8,)),
            pltpu.SemaphoreType.DMA((4,)),
            pltpu.SemaphoreType.DMA((7,)),
            pltpu.SemaphoreType.DMA((7,)),
            pltpu.SemaphoreType.DMA((2,)),
            pltpu.SemaphoreType.DMA((2,)),
        ],
        compiler_params=pltpu.CompilerParams(
            collective_id=0, has_side_effects=True, vmem_limit_bytes=56 * 2**20
        ),
    )(query_in, key_in, value_in, grad_out, short_weight, log_rate.T, residue.T)
    count = len(results)
    results = pl.pallas_call(
        functools.partial(hand_over, count),
        out_shape=[jax.ShapeDtypeStruct(r.shape, r.dtype) for r in results],
        in_specs=[hbm] * count,
        out_specs=[hbm] * count,
        scratch_shapes=[pltpu.VMEM(r.shape, r.dtype) for r in results]
        + [pltpu.SemaphoreType.DMA((count,))] * 2,
        compiler_params=pltpu.CompilerParams(vmem_limit_bytes=60 * 2**20),
    )(*results)
    return (*results[:5], results[5].T, results[6].T)


def solution(mesh):
    return jax.shard_map(
        local,
        mesh=mesh,
        in_specs=(
            P("chan", "seq"),
            P("chan", "seq"),
            P("chan", "seq"),
            P(None, None, "chan"),
            P(("chan", "seq"), None),
            P(("chan", "seq"), None),
            P("chan", "seq"),
        ),
        out_specs=(
            P("chan", "seq"),
            P("chan", "seq"),
            P("chan", "seq"),
            P("chan", "seq"),
            P(None, None, "chan"),
            P(("chan", "seq"), None),
            P(("chan", "seq"), None),
        ),
        check_vma=False,
    )
```

```python
import functools
import math

import jax
import jax.numpy as jnp
from jax import lax
from jax.experimental import pallas as pl
from jax.experimental.pallas import tpu as pltpu
from jax.sharding import PartitionSpec as P


def shifted(shard, axis, by):
    count = lax.axis_size(axis)
    pairs = [(i, i + by) for i in range(count) if 0 <= i + by < count]
    return lax.ppermute(shard, axis, pairs)


def dft_table(length, sign):
    counter = jnp.arange(length, dtype=jnp.int32)
    product = counter[:, None] * counter[None, :] % length
    angle = product.astype(jnp.float32) * (sign * 2.0 * math.pi / length)
    return (jnp.cos(angle), jnp.sin(angle))


def complex_dot(real_part, imag_part, table_real, table_imag):
    highest = lax.Precision.HIGHEST
    out_real = jnp.matmul(real_part, table_real, precision=highest) - jnp.matmul(
        imag_part, table_imag, precision=highest
    )
    out_imag = jnp.matmul(real_part, table_imag, precision=highest) + jnp.matmul(
        imag_part, table_real, precision=highest
    )
    return (out_real, out_imag)


def transform(real_part, imag_part, sign):
    length = real_part.shape[-1]
    if length <= 256 or length % 128 != 0:
        table_real, table_imag = dft_table(length, sign)
        return complex_dot(real_part, imag_part, table_real, table_imag)
    outer = 128
    inner = length // outer
    leading = real_part.shape[:-1]
    split_real = jnp.swapaxes(real_part.reshape(leading + (inner, outer)), -1, -2)
    split_imag = jnp.swapaxes(imag_part.reshape(leading + (inner, outer)), -1, -2)
    part_real, part_imag = transform(split_real, split_imag, sign)
    first_index = jnp.arange(outer, dtype=jnp.int32)[:, None]
    second_index = jnp.arange(inner, dtype=jnp.int32)[None, :]
    angle = (first_index * second_index % length).astype(jnp.float32) * (
        sign * 2.0 * math.pi / length
    )
    twist_real = jnp.cos(angle)
    twist_imag = jnp.sin(angle)
    turned_real = part_real * twist_real - part_imag * twist_imag
    turned_imag = part_real * twist_imag + part_imag * twist_real
    table_real, table_imag = dft_table(outer, sign)
    highest = lax.Precision.HIGHEST
    out_real = jnp.einsum(
        "...nk,nl->...lk", turned_real, table_real, precision=highest
    ) - jnp.einsum("...nk,nl->...lk", turned_imag, table_imag, precision=highest)
    out_imag = jnp.einsum(
        "...nk,nl->...lk", turned_real, table_imag, precision=highest
    ) + jnp.einsum("...nk,nl->...lk", turned_imag, table_real, precision=highest)
    return (out_real.reshape(leading + (length,)), out_imag.reshape(leading + (length,)))


def spectrum(signal):
    length = signal.shape[1]
    padded = jnp.pad(signal.astype(jnp.float32), ((0, 0), (0, length)))
    return transform(padded, jnp.zeros_like(padded), -1.0)


def mirrored(values):
    return jnp.roll(jnp.flip(values, -1), 1, -1)


def paired_spectra(first, second):
    length = first.shape[1]
    first_pad = jnp.pad(first, ((0, 0), (0, length)))
    second_pad = jnp.pad(second.astype(jnp.float32), ((0, 0), (0, length)))
    joint_real, joint_imag = transform(first_pad, second_pad, -1.0)
    mirror_real = mirrored(joint_real)
    mirror_imag = mirrored(joint_imag)
    first_spec = (0.5 * (joint_real + mirror_real), 0.5 * (joint_imag - mirror_imag))
    second_spec = (0.5 * (joint_imag + mirror_imag), -0.5 * (joint_real - mirror_real))
    return (first_spec, second_spec)


def to_time(spec_pair, length):
    real_part, imag_part = spec_pair
    back_real, back_imag = transform(real_part, imag_part, 1.0)
    return back_real[:, :length] / real_part.shape[-1]


def paired_time(first_spec, second_spec, length):
    joint_real = first_spec[0] - second_spec[1]
    joint_imag = first_spec[1] + second_spec[0]
    back_real, back_imag = transform(joint_real, joint_imag, 1.0)
    total_len = joint_real.shape[-1]
    return (back_real[:, :length] / total_len, back_imag[:, :length] / total_len)


def spectral_product(first, second, conjugate):
    first_real, first_imag = first
    second_real, second_imag = second
    if conjugate:
        second_imag = -second_imag
    return (
        first_real * second_real - first_imag * second_imag,
        first_real * second_imag + first_imag * second_real,
    )


def modal_filter(residue, log_rate, length):
    decay_rate = jnp.exp(log_rate)
    offsets = jnp.arange(length).astype(jnp.float32)
    filt = jnp.zeros((residue.shape[0], length), jnp.float32)
    for mode_index in range(residue.shape[1]):
        factor = residue[:, mode_index] * jnp.sqrt(2.0 * decay_rate[:, mode_index])
        filt = filt + factor[:, None] * jnp.exp(-decay_rate[:, mode_index][:, None] * offsets)
    return filt


def modal_grads(filt_grad, residue, log_rate):
    decay_rate = jnp.exp(log_rate)
    offsets = jnp.arange(filt_grad.shape[1]).astype(jnp.float32)
    res_terms = []
    log_terms = []
    for mode_index in range(residue.shape[1]):
        rate_col = decay_rate[:, mode_index][:, None]
        basis = jnp.sqrt(2.0 * rate_col) * jnp.exp(-rate_col * offsets)
        weighted = filt_grad * basis
        res_terms.append(jnp.sum(weighted, axis=1))
        log_terms.append(
            residue[:, mode_index] * jnp.sum(weighted * (0.5 - rate_col * offsets), axis=1)
        )
    return (jnp.stack(res_terms, axis=1), jnp.stack(log_terms, axis=1))


def apply_taps(widened, taps, tok_rows):
    total = jnp.zeros((widened.shape[0], tok_rows), jnp.float32)
    for offset in range(7):
        total = total + taps[offset][:, None] * widened[:, 6 - offset : 6 - offset + tok_rows]
    return total


def taps_back(gradient, following, taps):
    tok_rows = gradient.shape[1]
    widened = jnp.concatenate([gradient, following], axis=1)
    total = jnp.zeros_like(gradient)
    for offset in range(7):
        total = total + taps[offset][:, None] * widened[:, offset : offset + tok_rows]
    return total


def taps_gradient(gradient, widened):
    tok_rows = gradient.shape[1]
    rows_out = [
        jnp.sum(gradient * widened[:, 6 - offset : 6 - offset + tok_rows], axis=1)
        for offset in range(7)
    ]
    return jnp.stack(rows_out, axis=0)


def to_channels(stream):
    return lax.all_to_all(stream, "seq", split_axis=0, concat_axis=1, tiled=True)


def to_tokens(stream):
    return lax.all_to_all(stream, "seq", split_axis=1, concat_axis=0, tiled=True)


def local_fft(query_in, key_in, value_in, short_weight, residue, log_rate, grad_out):
    tok_rows = query_in.shape[1]
    length = tok_rows * lax.axis_size("seq")
    scale = 1.0 / math.sqrt(length)
    tails = shifted((query_in[:, -6:], key_in[:, -6:], value_in[:, -6:]), "seq", 1)
    query_wide = jnp.concatenate([tails[0], query_in], axis=1).astype(jnp.float32)
    key_wide = jnp.concatenate([tails[1], key_in], axis=1).astype(jnp.float32)
    value_wide = jnp.concatenate([tails[2], value_in], axis=1).astype(jnp.float32)
    query_hat = apply_taps(query_wide, short_weight[0], tok_rows)
    key_hat = apply_taps(key_wide, short_weight[1], tok_rows)
    value_hat = apply_taps(value_wide, short_weight[2], tok_rows)
    mixed = (key_hat * value_hat).astype(jnp.bfloat16)
    grad_up = grad_out.astype(jnp.float32)
    grad_mixed = (grad_up * query_hat).astype(jnp.bfloat16)
    mixed_cols = to_channels(mixed)
    filt = modal_filter(residue, log_rate, length)
    spec_filter, spec_mixed = paired_spectra(filt, mixed_cols)
    long_out = to_time(spectral_product(spec_mixed, spec_filter, False), length).astype(
        jnp.bfloat16
    )
    conv_out = to_tokens(long_out)
    grad_cols = to_channels(grad_mixed)
    spec_grad = spectrum(grad_cols)
    long_grad, filt_grad = paired_time(
        spectral_product(spec_grad, spec_filter, True),
        spectral_product(spec_grad, spec_mixed, True),
        length,
    )
    conv_grad = to_tokens(long_grad.astype(jnp.bfloat16))
    grad_res, grad_log = modal_grads(filt_grad, residue, log_rate)
    conv_wide = conv_out.astype(jnp.float32)
    conv_grad_wide = conv_grad.astype(jnp.float32)
    output = (query_hat * conv_wide).astype(jnp.bfloat16)
    grad_q = grad_up * conv_wide
    grad_k = conv_grad_wide * value_hat
    grad_v = conv_grad_wide * key_hat
    heads = shifted((grad_q[:, :6], grad_k[:, :6], grad_v[:, :6]), "seq", -1)
    grad_query = taps_back(grad_q, heads[0], short_weight[0]).astype(jnp.bfloat16)
    grad_key = taps_back(grad_k, heads[1], short_weight[1]).astype(jnp.bfloat16)
    grad_value = taps_back(grad_v, heads[2], short_weight[2]).astype(jnp.bfloat16)
    local_terms = jnp.stack(
        [
            taps_gradient(grad_q, query_wide),
            taps_gradient(grad_k, key_wide),
            taps_gradient(grad_v, value_wide),
        ],
        axis=0,
    )
    grad_short = lax.psum(local_terms, "seq") * scale
    return (
        output,
        grad_query,
        grad_key,
        grad_value,
        grad_short,
        grad_res * scale,
        grad_log * scale,
    )


SUB = 8
LANE = 128
HALO = 6
TAPS = 7
GROUP = 8
MESH = pl.DeviceIdType.MESH


def slab(index):
    return pl.ds(pl.multiple_of(index * SUB, SUB), SUB)


def layer_kernel(
    n, modes, tokens, scale,
    query_ref, key_ref, value_ref, grad_ref, weight_ref, rate_ref, residue_ref,
    out_ref, gq_ref, gk_ref, gv_ref, short_ref, res_ref, log_ref,
    inputs, results, tails, heads, tails_in, heads_in, param_ref, streams, hats, mixed, gmixed, conv, conv_back, prod, cots,
    weights, params, decay, gain, rate,
    edge_send, edge_recv, acc_hold, acc_send, acc_recv,
    carry_hold, carry_send, carry_recv, modal_send, modal_recv, short_send, short_recv, total_send, total_recv, totals,
    load_sem, store_sem, send_sem, recv_sem, halo_send, halo_recv,
):
    me = lax.axis_index("seq")
    extent = tokens + HALO
    rows_all = 3 * TAPS
    owners = (rows_all + 1) // 2
    f32 = jnp.float32
    zero = jnp.zeros((SUB, LANE), f32)

    def rounded(value):
        return value.astype(jnp.bfloat16).astype(f32)

    def tree(parts):
        while len(parts) > 1:
            parts = [parts[i] + parts[i + 1] for i in range(0, len(parts), 2)]
        return parts[0]

    def per_mode(ref):
        return [ref[m * SUB : (m + 1) * SUB, :] for m in range(modes)]

    half_width = SUB * LANE // 2
    loads = []
    for s, ref in enumerate((query_ref, key_ref, value_ref, grad_ref)):
        for half in range(2):
            part = pl.ds(half * half_width, half_width)
            loads.append(
                pltpu.make_async_copy(
                    ref.at[part], inputs.at[s, part], load_sem.at[2 * s + half]
                )
            )
            loads[-1].start()

    barrier = pltpu.get_barrier_semaphore()
    offsets = sorted(range(1, n), key=lambda k: abs(2 * k - n))
    peers = [lax.rem(me + k, n) for k in offsets]
    for peer in peers:
        pl.semaphore_signal(
            barrier, inc=1, device_id={"seq": peer}, device_id_type=MESH
        )

    def send(phase, peer, source, target):
        pltpu.make_async_remote_copy(
            src_ref=source,
            dst_ref=target,
            send_sem=send_sem.at[phase],
            recv_sem=recv_sem.at[phase],
            device_id={"seq": peer},
            device_id_type=MESH,
        ).start()

    def sent(phase, like):
        pltpu.make_async_copy(like, like, send_sem.at[phase]).wait()

    def arrived(phase, like):
        pltpu.make_async_copy(like, like, recv_sem.at[phase]).wait()

    others = pl.ds(0, n - 1)
    param_ref[...] = jnp.concatenate([rate_ref[...], residue_ref[...]], axis=1)

    for s in range(3):
        for b in range(SUB):
            weights[pl.ds(s * TAPS * SUB + b, TAPS, stride=SUB), :] = weight_ref[
                s, :, b * LANE : (b + 1) * LANE
            ]

    eye = (
        lax.broadcasted_iota(jnp.int32, (LANE, LANE), 0)
        == lax.broadcasted_iota(jnp.int32, (LANE, LANE), 1)
    ).astype(jnp.bfloat16)

    def turned(block):
        return lax.dot_general(
            eye, block, (((1,), (1,)), ((), ())), preferred_element_type=f32
        )

    own_rows = pl.ds(pl.multiple_of(me * modes, modes), modes)
    for s in range(4):
        for b in range(0, SUB, 2):
            if b % (SUB // 2) == 0:
                loads[2 * s + b // (SUB // 2)].wait()
            block = turned(inputs[s, b * LANE : (b + 2) * LANE, :])
            for half in range(2):
                streams[s, pl.ds(HALO * SUB + b + half, tokens, stride=SUB), :] = block[
                    :, half * LANE : (half + 1) * LANE
                ]
        if s == 1:
            pl.semaphore_wait(barrier, n - 1)
            for peer in peers:
                send(0, peer, param_ref, params.at[own_rows])
            params[own_rows, :] = param_ref[...]

    edge = HALO * SUB
    last = tokens * SUB
    to_right = lambda: pltpu.make_async_remote_copy(
        src_ref=tails,
        dst_ref=tails_in,
        send_sem=halo_send.at[0],
        recv_sem=halo_recv.at[0],
        device_id={"seq": lax.rem(me + 1, n)},
        device_id_type=MESH,
    )
    to_left = lambda: pltpu.make_async_remote_copy(
        src_ref=heads,
        dst_ref=heads_in,
        send_sem=halo_send.at[1],
        recv_sem=halo_recv.at[1],
        device_id={"seq": lax.rem(me + n - 1, n)},
        device_id_type=MESH,
    )
    for s in range(3):
        tails[s] = streams[s, last : last + edge, :].astype(jnp.bfloat16)
    for s in range(4):
        heads[s] = streams[s, edge : 2 * edge, :].astype(jnp.bfloat16)

    @pl.when(me < n - 1)
    def _():
        to_right().start()

    @pl.when(me > 0)
    def _():
        to_left().start()

    taps = [
        [weights[(s * TAPS + j) * SUB : (s * TAPS + j + 1) * SUB, :] for j in range(TAPS)]
        for s in range(3)
    ]

    def filter_token(t):
        vals = []
        for s in range(3):
            total = taps[s][0] * streams[s, slab(t + HALO), :]
            for j in range(1, TAPS):
                total = total + taps[s][j] * streams[s, slab(t + HALO - j), :]
            hats[s, slab(t), :] = total
            vals.append(total)
        mixed[slab(t), :] = rounded(vals[1] * vals[2])
        gmixed[slab(t), :] = rounded(vals[0] * streams[3, slab(t + HALO), :])

    def token_loop(lo, hi, unroll, fn):
        def step(i, carry):
            for u in range(unroll):
                fn(lo + i * unroll + u)
            return carry

        lax.fori_loop(0, (hi - lo) // unroll, step, 0)

    token_loop(HALO, tokens, 2, filter_token)

    arrived(0, params.at[pl.ds(0, (n - 1) * modes)])
    low_half = lax.broadcasted_iota(jnp.int32, (SUB, LANE), 1) < LANE // 2
    for m in range(modes):
        even = params[pl.ds(m, SUB, stride=2 * modes), :]
        odd = params[pl.ds(modes + m, SUB, stride=2 * modes), :]
        log_rate = jnp.where(low_half, even, pltpu.roll(odd, LANE // 2, 1))
        residue = jnp.where(low_half, pltpu.roll(even, LANE // 2, 1), odd)
        r = jnp.exp(log_rate)
        rate[slab(m), :] = r
        decay[slab(m), :] = jnp.exp(-r)
        gain[slab(m), :] = residue * jnp.sqrt(2.0 * r)

    UN = 4
    decays = per_mode(decay)

    def edge_step(i, carry):
        x, z = [list(c) for c in carry]
        for u in range(2):
            t = i * 2 + u
            value = mixed[slab(t + HALO), :]
            cot = gmixed[slab(tokens - 1 - t), :]
            for m in range(modes):
                x[m] = decays[m] * x[m] + value
                z[m] = decays[m] * z[m] + cot
        return tuple(x), tuple(z)

    inner = tokens - HALO
    x, z = lax.fori_loop(0, inner // 2, edge_step, ((zero,) * modes,) * 2)
    @pl.when(me > 0)
    def _():
        to_left().wait_send()
        to_right().wait_recv()
        for s in range(3):
            streams[s, 0:edge, :] = tails_in[s].astype(f32)

    @pl.when(me == 0)
    def _():
        streams[0:3, 0:edge, :] = jnp.zeros((3, edge, LANE), f32)

    @pl.when(me < n - 1)
    def _():
        to_right().wait_send()
        to_left().wait_recv()
        for s in range(4):
            streams[s, edge + last : 2 * edge + last, :] = heads_in[s].astype(f32)

    @pl.when(me == n - 1)
    def _():
        streams[:, edge + last : 2 * edge + last, :] = jnp.zeros((4, edge, LANE), f32)

    token_loop(0, HALO, 2, filter_token)
    token_loop(tokens, extent, 2, filter_token)

    x, z = list(x), list(z)
    for m in range(modes):
        early = zero
        for t in range(HALO):
            back = HALO - 1 - t
            early = decays[m] * early + mixed[t * SUB : (t + 1) * SUB, :]
            z[m] = decays[m] * z[m] + gmixed[back * SUB : (back + 1) * SUB, :]
        x[m] = x[m] + jnp.exp(-float(inner) * rate[m * SUB : (m + 1) * SUB, :]) * early
    for m in range(modes):
        edge_send[m] = jnp.concatenate([x[m], z[m]], axis=0).astype(jnp.bfloat16)
    for peer in peers:
        send(1, peer, edge_send.at[peer], edge_recv.at[me])
    edge_recv[me] = edge_send[me]

    for first in range(0, modes, GROUP):
        group = range(first, first + GROUP)

        def fwd_step(i, carry, first=first, group=group):
            x, y, ax, ay = [list(c) for c in carry]
            for u in range(UN):
                t = i * UN + u
                value = mixed[slab(t), :]
                cot = gmixed[slab(t), :]
                parts = []
                for p, m in enumerate(group):
                    a = decay[m * SUB : (m + 1) * SUB, :]
                    y[p] = a * (y[p] + x[p])
                    x[p] = a * x[p] + value
                    parts.append(gain[m * SUB : (m + 1) * SUB, :] * x[p])
                    ax[p] = ax[p] + cot * x[p]
                    ay[p] = ay[p] + cot * y[p]
                total = tree(parts)
                conv[slab(t), :] = conv[slab(t), :] + total if first else total
            return tuple(tuple(c) for c in (x, y, ax, ay))

        zeros = tuple(zero for _ in group)
        x, y, ax, ay = lax.fori_loop(0, tokens // UN, fwd_step, (zeros,) * 4)
        for p, m in enumerate(group):
            acc_hold[m, 0:SUB, :] = y[p]
            acc_hold[m, 2 * SUB : 3 * SUB, :] = ax[p]
            acc_hold[m, 3 * SUB : 4 * SUB, :] = ay[p]
        x = list(x)
        for t in range(tokens, extent):
            value = mixed[t * SUB : (t + 1) * SUB, :]
            total = conv[t * SUB : (t + 1) * SUB, :] if first else zero
            for p, m in enumerate(group):
                x[p] = decay[m * SUB : (m + 1) * SUB, :] * x[p] + value
                total = total + gain[m * SUB : (m + 1) * SUB, :] * x[p]
            conv[t * SUB : (t + 1) * SUB, :] = total

    my_rate = rate[slab(me), :]
    my_decay = decay[slab(me), :]
    my_gain = gain[slab(me), :]
    whole = jnp.exp(-float(tokens) * my_rate)
    arrived(1, edge_recv.at[others])
    h, z = zero, zero
    for d in range(n):
        back = n - 1 - d
        carry_hold[d, 0:SUB, :] = h
        carry_hold[back, SUB : 2 * SUB, :] = z
        h = whole * h + edge_recv[d].astype(f32)[0:SUB]
        z = whole * z + edge_recv[back].astype(f32)[SUB : 2 * SUB]
    for d in range(n):
        carry_send[d] = carry_hold[d].astype(jnp.bfloat16)
    for peer in peers:
        send(2, peer, carry_send.at[peer], carry_recv.at[me])
    carry_recv[me] = carry_send[me]

    for first in range(0, modes, GROUP):
        group = range(first, first + GROUP)

        def bwd_step(i, carry, first=first, group=group):
            z, w = [list(c) for c in carry]
            for u in range(UN):
                t = tokens - 1 - (i * UN + u)
                cot = gmixed[slab(t), :]
                parts = []
                for p, m in enumerate(group):
                    a = decay[m * SUB : (m + 1) * SUB, :]
                    z[p] = a * z[p] + cot
                    w[p] = a * w[p] + z[p]
                    parts.append(gain[m * SUB : (m + 1) * SUB, :] * z[p])
                total = tree(parts)
                conv_back[slab(t), :] = conv_back[slab(t), :] + total if first else total
            return tuple(tuple(c) for c in (z, w))

        zeros = tuple(zero for _ in group)
        z, w = lax.fori_loop(0, tokens // UN, bwd_step, (zeros,) * 2)
        for p, m in enumerate(group):
            acc_hold[m, SUB : 2 * SUB, :] = w[p]

    for m in range(modes):
        acc_send[m] = acc_hold[m].astype(jnp.bfloat16)
    for peer in peers:
        send(3, peer, acc_send.at[peer], acc_recv.at[me])
    acc_recv[me] = acc_send[me]

    arrived(2, carry_recv.at[others])
    gains = per_mode(gain)
    carried = [carry_recv[m].astype(f32) for m in range(modes)]

    def fwd_two(i, c):
        c = list(c)
        for u in range(2):
            t = i * 2 + u
            c = [decays[m] * c[m] for m in range(modes)]
            total = rounded(conv[slab(t), :] + tree(c))
            prod[slab(t), :] = hats[0, slab(t), :] * total
            cots[0, slab(t), :] = streams[3, slab(t + HALO), :] * total
        return tuple(c)

    start = tuple(gains[m] * carried[m][0:SUB] for m in range(modes))
    lax.fori_loop(0, extent // 2, fwd_two, start)

    def store_back(t, total):
        total = rounded(total)
        cots[1, slab(t), :] = hats[2, slab(t), :] * total
        cots[2, slab(t), :] = hats[1, slab(t), :] * total

    def bwd_two(i, c):
        c = list(c)
        for u in range(2):
            t = tokens - 1 - (i * 2 + u)
            c = [decays[m] * c[m] for m in range(modes)]
            store_back(t, conv_back[slab(t), :] + tree(c))
        return tuple(c)

    start = tuple(gains[m] * carried[m][SUB : 2 * SUB] for m in range(modes))
    lax.fori_loop(0, tokens // 2, bwd_two, start)

    ahead = [zero] * HALO
    for m in range(modes):
        grow = jnp.exp(rate[m * SUB : (m + 1) * SUB, :])
        z = carry_recv[m].astype(f32)[SUB : 2 * SUB]
        for h in range(HALO):
            ahead[h] = ahead[h] + gains[m] * z
            z = grow * (z - gmixed[(tokens + h) * SUB : (tokens + h + 1) * SUB, :])
    for h in range(HALO):
        store_back(tokens + h, ahead[h])

    def short_step(i, accs):
        accs = list(accs)
        for u in range(2):
            t = i * 2 + u
            for s in range(3):
                cot = cots[s, slab(t), :]
                for j in range(TAPS):
                    at = s * TAPS + j
                    accs[at] = accs[at] + cot * streams[s, slab(t + HALO - j), :]
        return tuple(accs)

    accs = lax.fori_loop(0, tokens // 2, short_step, (zero,) * rows_all)
    accs = list(accs) + [zero] * (2 * owners - rows_all)
    for o in range(owners):
        both = jnp.concatenate(accs[2 * o : 2 * o + 2], axis=0)
        short_send[o] = both.astype(jnp.bfloat16)
    for peer in peers:

        @pl.when(peer < owners)
        def _(peer=peer):
            send(5, peer, short_send.at[peer], short_recv.at[me])

    @pl.when(me < owners)
    def _():
        short_recv[me] = short_send[me]

    arrived(3, acc_recv.at[others])
    hy, acc_x, acc_y = zero, zero, zero
    for d in range(n):
        h = carry_hold[d, 0:SUB, :]
        terms = acc_recv[d].astype(f32)
        z0 = my_decay * edge_recv[d].astype(f32)[SUB : 2 * SUB]
        z1 = my_decay * terms[SUB : 2 * SUB]
        acc_x = acc_x + (terms[2 * SUB : 3 * SUB] + h * z0)
        acc_y = acc_y + (terms[3 * SUB : 4 * SUB] + h * z1 + hy * z0)
        hy = whole * (hy + float(tokens) * h) + terms[0:SUB]
    grad_res = acc_x * jnp.sqrt(2.0 * my_rate) * scale
    grad_log = my_gain * (0.5 * acc_x - my_rate * acc_y) * scale
    for b in range(SUB):
        modal_send[b, 0:1, :] = grad_res[b : b + 1, :]
        modal_send[b, 1:2, :] = grad_log[b : b + 1, :]
    for peer in peers:
        send(4, peer, modal_send.at[lax.div(peer, 2)], modal_recv.at[me])
    modal_recv[me] = modal_send[lax.div(me, 2)]

    def taps_step(t):
        for s in range(3):
            total = taps[s][0] * cots[s, slab(t), :]
            for j in range(1, TAPS):
                total = total + taps[s][j] * cots[s, slab(t + j), :]
            hats[s, slab(t), :] = total

    token_loop(0, tokens, 2, taps_step)

    @pl.when(me < owners)
    def _():
        arrived(5, short_recv.at[others])
        total = short_recv[0].astype(f32)
        for d in range(1, n):
            total = total + short_recv[d].astype(f32)
        total_send[...] = (total * scale).astype(jnp.bfloat16)
        for peer in peers:
            send(6, peer, total_send, total_recv.at[me])
        total_recv[me] = total_send[...]

    stores = []
    outs = (out_ref, gq_ref, gk_ref, gv_ref)
    for first in (0, 2):
        for b in range(SUB):
            rows = pl.ds(b, tokens, stride=SUB)
            one = hats[first - 1, rows, :] if first else prod[rows, :]
            block = jnp.concatenate([one, hats[first, rows, :]], axis=0)
            block = turned(block.astype(jnp.bfloat16)).astype(jnp.bfloat16)
            for half in range(2):
                results[first + half, b * LANE : (b + 1) * LANE, :] = block[
                    :, half * LANE : (half + 1) * LANE
                ]
        for s in (first, first + 1):
            stores.append(pltpu.make_async_copy(results.at[s], outs[s], store_sem.at[s]))
            stores[-1].start()

    arrived(4, modal_recv.at[others])
    odd_owner = lax.rem(me, 2) == 1
    for at, ref in ((0, res_ref), (1, log_ref)):
        table = jnp.concatenate([modal_recv[m, at : at + 1, :] for m in range(modes)], axis=0)
        table = jnp.where(odd_owner, pltpu.roll(table, LANE // 2, 1), table)
        ref[...] = table[:, : LANE // 2]

    @pl.when(me < owners)
    def _():
        arrived(6, total_recv.at[pl.ds(0, owners - 1)])
        sent(5, short_recv.at[pl.ds(0, owners - 1)])
        sent(6, short_recv.at[others])

    @pl.when(me >= owners)
    def _():
        arrived(6, total_recv)
        sent(5, short_recv.at[pl.ds(0, owners)])

    for o in range(owners):
        totals[2 * o * SUB : 2 * (o + 1) * SUB, :] = total_recv[o].astype(f32)
    for s in range(3):
        for b in range(SUB):
            short_ref[s, :, b * LANE : (b + 1) * LANE] = totals[
                pl.ds(s * TAPS * SUB + b, TAPS, stride=SUB), :
            ]

    for store in stores:
        store.wait()
    sent(0, params.at[pl.ds(0, (n - 1) * modes)])
    sent(1, edge_recv.at[others])
    sent(2, carry_recv.at[others])
    sent(3, acc_recv.at[others])
    sent(4, modal_recv.at[others])


def hand_over(count, *refs):
    sources, targets, held = refs[:count], refs[count : 2 * count], refs[2 * count : -2]
    load_sem, store_sem = refs[-2:]
    pieces = []
    for i in range(count):
        lead = sources[i].shape[0]
        cuts = 4 if lead % 64 == 0 else 1
        for c in range(cuts):
            pieces.append((i, pl.ds(c * (lead // cuts), lead // cuts)))
    loads, stores = [], []
    for at, (i, part) in enumerate(pieces):
        middle = held[i].at[part]
        loads.append(pltpu.make_async_copy(sources[i].at[part], middle, load_sem.at[at]))
        stores.append(pltpu.make_async_copy(middle, targets[i].at[part], store_sem.at[at]))
    for load in loads:
        load.start()
    for load, store in zip(loads, stores):
        load.wait()
        store.start()
    for store in stores:
        store.wait()


def local(query_in, key_in, value_in, short_weight, residue, log_rate, grad_out):
    n = lax.axis_size("seq")
    width, tokens = query_in.shape
    own, modes = residue.shape
    fits = width == SUB * LANE and tokens == LANE and modes == n == 2 * SUB
    if not (fits and own == LANE // 2):
        return local_fft(
            query_in, key_in, value_in, short_weight, residue, log_rate, grad_out
        )
    scale = 1.0 / math.sqrt(tokens * n)
    f32 = jnp.float32
    rows = (tokens + HALO) * SUB
    owners = (3 * TAPS + 1) // 2
    vmem = pl.BlockSpec(memory_space=pltpu.VMEM)
    hbm = pl.BlockSpec(memory_space=pltpu.MemorySpace.HBM)
    pair = pltpu.VMEM((n, 2 * SUB, LANE), f32)
    quad = pltpu.VMEM((n, 4 * SUB, LANE), f32)
    half_pair = pltpu.VMEM((n, 2 * SUB, LANE), jnp.bfloat16)
    half_quad = pltpu.VMEM((n, 4 * SUB, LANE), jnp.bfloat16)
    tail = pltpu.VMEM((3, HALO * SUB, LANE), jnp.bfloat16)
    head = pltpu.VMEM((4, HALO * SUB, LANE), jnp.bfloat16)
    flat = pltpu.VMEM((rows, LANE), f32)
    triple = pltpu.VMEM((3, rows, LANE), f32)
    small = pltpu.VMEM((modes * SUB, LANE), f32)
    shape = jax.ShapeDtypeStruct((width, tokens), jnp.bfloat16)
    modal = jax.ShapeDtypeStruct((modes, own), f32)
    results = pl.pallas_call(
        functools.partial(layer_kernel, n, modes, tokens, scale),
        out_shape=(
            shape, shape, shape, shape,
            jax.ShapeDtypeStruct(short_weight.shape, f32), modal, modal,
        ),
        in_specs=[hbm] * 4 + [vmem] * 3,
        out_specs=(hbm,) * 4 + (vmem,) * 3,
        scratch_shapes=[
            pltpu.VMEM((4, width, tokens), jnp.bfloat16),
            pltpu.VMEM((4, width, tokens), jnp.bfloat16),
            tail, head, tail, head,
            pltpu.VMEM((modes, LANE), f32),
            pltpu.VMEM((4, rows + HALO * SUB, LANE), f32),
            triple, flat, flat, flat, flat, flat, triple,
            pltpu.VMEM((3 * TAPS * SUB, LANE), f32),
            pltpu.VMEM((n * modes, LANE), f32),
            small, small, small,
            half_pair, half_pair, quad, half_quad, half_quad,
            pair, half_pair, half_pair,
            pltpu.VMEM((SUB, 2, LANE), f32),
            pltpu.VMEM((n, 2, LANE), f32),
            pltpu.VMEM((owners, 2 * SUB, LANE), jnp.bfloat16),
            half_pair,
            pltpu.VMEM((2 * SUB, LANE), jnp.bfloat16),
            pltpu.VMEM((owners, 2 * SUB, LANE), jnp.bfloat16),
            pltpu.VMEM((owners * 2 * SUB, LANE), f32),
            pltpu.SemaphoreType.DMA((8,)),
            pltpu.SemaphoreType.DMA((4,)),
            pltpu.SemaphoreType.DMA((7,)),
            pltpu.SemaphoreType.DMA((7,)),
            pltpu.SemaphoreType.DMA((2,)),
            pltpu.SemaphoreType.DMA((2,)),
        ],
        compiler_params=pltpu.CompilerParams(
            collective_id=0, has_side_effects=True, vmem_limit_bytes=56 * 2**20
        ),
    )(query_in, key_in, value_in, grad_out, short_weight, log_rate.T, residue.T)
    count = len(results)
    results = pl.pallas_call(
        functools.partial(hand_over, count),
        out_shape=[jax.ShapeDtypeStruct(r.shape, r.dtype) for r in results],
        in_specs=[hbm] * count,
        out_specs=[hbm] * count,
        scratch_shapes=[pltpu.VMEM(r.shape, r.dtype) for r in results]
        + [pltpu.SemaphoreType.DMA((4 * count,))] * 2,
        compiler_params=pltpu.CompilerParams(vmem_limit_bytes=60 * 2**20),
    )(*results)
    return (*results[:5], results[5].T, results[6].T)


def solution(mesh):
    return jax.shard_map(
        local,
        mesh=mesh,
        in_specs=(
            P("chan", "seq"),
            P("chan", "seq"),
            P("chan", "seq"),
            P(None, None, "chan"),
            P(("chan", "seq"), None),
            P(("chan", "seq"), None),
            P("chan", "seq"),
        ),
        out_specs=(
            P("chan", "seq"),
            P("chan", "seq"),
            P("chan", "seq"),
            P("chan", "seq"),
            P(None, None, "chan"),
            P(("chan", "seq"), None),
            P(("chan", "seq"), None),
        ),
        check_vma=False,
    )
```

```python
import functools
import math

import jax
import jax.numpy as jnp
from jax import lax
from jax.experimental import pallas as pl
from jax.experimental.pallas import tpu as pltpu
from jax.sharding import PartitionSpec as P


def shifted(shard, axis, by):
    count = lax.axis_size(axis)
    pairs = [(i, i + by) for i in range(count) if 0 <= i + by < count]
    return lax.ppermute(shard, axis, pairs)


def dft_table(length, sign):
    counter = jnp.arange(length, dtype=jnp.int32)
    product = counter[:, None] * counter[None, :] % length
    angle = product.astype(jnp.float32) * (sign * 2.0 * math.pi / length)
    return (jnp.cos(angle), jnp.sin(angle))


def complex_dot(real_part, imag_part, table_real, table_imag):
    highest = lax.Precision.HIGHEST
    out_real = jnp.matmul(real_part, table_real, precision=highest) - jnp.matmul(
        imag_part, table_imag, precision=highest
    )
    out_imag = jnp.matmul(real_part, table_imag, precision=highest) + jnp.matmul(
        imag_part, table_real, precision=highest
    )
    return (out_real, out_imag)


def transform(real_part, imag_part, sign):
    length = real_part.shape[-1]
    if length <= 256 or length % 128 != 0:
        table_real, table_imag = dft_table(length, sign)
        return complex_dot(real_part, imag_part, table_real, table_imag)
    outer = 128
    inner = length // outer
    leading = real_part.shape[:-1]
    split_real = jnp.swapaxes(real_part.reshape(leading + (inner, outer)), -1, -2)
    split_imag = jnp.swapaxes(imag_part.reshape(leading + (inner, outer)), -1, -2)
    part_real, part_imag = transform(split_real, split_imag, sign)
    first_index = jnp.arange(outer, dtype=jnp.int32)[:, None]
    second_index = jnp.arange(inner, dtype=jnp.int32)[None, :]
    angle = (first_index * second_index % length).astype(jnp.float32) * (
        sign * 2.0 * math.pi / length
    )
    twist_real = jnp.cos(angle)
    twist_imag = jnp.sin(angle)
    turned_real = part_real * twist_real - part_imag * twist_imag
    turned_imag = part_real * twist_imag + part_imag * twist_real
    table_real, table_imag = dft_table(outer, sign)
    highest = lax.Precision.HIGHEST
    out_real = jnp.einsum(
        "...nk,nl->...lk", turned_real, table_real, precision=highest
    ) - jnp.einsum("...nk,nl->...lk", turned_imag, table_imag, precision=highest)
    out_imag = jnp.einsum(
        "...nk,nl->...lk", turned_real, table_imag, precision=highest
    ) + jnp.einsum("...nk,nl->...lk", turned_imag, table_real, precision=highest)
    return (out_real.reshape(leading + (length,)), out_imag.reshape(leading + (length,)))


def spectrum(signal):
    length = signal.shape[1]
    padded = jnp.pad(signal.astype(jnp.float32), ((0, 0), (0, length)))
    return transform(padded, jnp.zeros_like(padded), -1.0)


def mirrored(values):
    return jnp.roll(jnp.flip(values, -1), 1, -1)


def paired_spectra(first, second):
    length = first.shape[1]
    first_pad = jnp.pad(first, ((0, 0), (0, length)))
    second_pad = jnp.pad(second.astype(jnp.float32), ((0, 0), (0, length)))
    joint_real, joint_imag = transform(first_pad, second_pad, -1.0)
    mirror_real = mirrored(joint_real)
    mirror_imag = mirrored(joint_imag)
    first_spec = (0.5 * (joint_real + mirror_real), 0.5 * (joint_imag - mirror_imag))
    second_spec = (0.5 * (joint_imag + mirror_imag), -0.5 * (joint_real - mirror_real))
    return (first_spec, second_spec)


def to_time(spec_pair, length):
    real_part, imag_part = spec_pair
    back_real, back_imag = transform(real_part, imag_part, 1.0)
    return back_real[:, :length] / real_part.shape[-1]


def paired_time(first_spec, second_spec, length):
    joint_real = first_spec[0] - second_spec[1]
    joint_imag = first_spec[1] + second_spec[0]
    back_real, back_imag = transform(joint_real, joint_imag, 1.0)
    total_len = joint_real.shape[-1]
    return (back_real[:, :length] / total_len, back_imag[:, :length] / total_len)


def spectral_product(first, second, conjugate):
    first_real, first_imag = first
    second_real, second_imag = second
    if conjugate:
        second_imag = -second_imag
    return (
        first_real * second_real - first_imag * second_imag,
        first_real * second_imag + first_imag * second_real,
    )


def modal_filter(residue, log_rate, length):
    decay_rate = jnp.exp(log_rate)
    offsets = jnp.arange(length).astype(jnp.float32)
    filt = jnp.zeros((residue.shape[0], length), jnp.float32)
    for mode_index in range(residue.shape[1]):
        factor = residue[:, mode_index] * jnp.sqrt(2.0 * decay_rate[:, mode_index])
        filt = filt + factor[:, None] * jnp.exp(-decay_rate[:, mode_index][:, None] * offsets)
    return filt


def modal_grads(filt_grad, residue, log_rate):
    decay_rate = jnp.exp(log_rate)
    offsets = jnp.arange(filt_grad.shape[1]).astype(jnp.float32)
    res_terms = []
    log_terms = []
    for mode_index in range(residue.shape[1]):
        rate_col = decay_rate[:, mode_index][:, None]
        basis = jnp.sqrt(2.0 * rate_col) * jnp.exp(-rate_col * offsets)
        weighted = filt_grad * basis
        res_terms.append(jnp.sum(weighted, axis=1))
        log_terms.append(
            residue[:, mode_index] * jnp.sum(weighted * (0.5 - rate_col * offsets), axis=1)
        )
    return (jnp.stack(res_terms, axis=1), jnp.stack(log_terms, axis=1))


def apply_taps(widened, taps, tok_rows):
    total = jnp.zeros((widened.shape[0], tok_rows), jnp.float32)
    for offset in range(7):
        total = total + taps[offset][:, None] * widened[:, 6 - offset : 6 - offset + tok_rows]
    return total


def taps_back(gradient, following, taps):
    tok_rows = gradient.shape[1]
    widened = jnp.concatenate([gradient, following], axis=1)
    total = jnp.zeros_like(gradient)
    for offset in range(7):
        total = total + taps[offset][:, None] * widened[:, offset : offset + tok_rows]
    return total


def taps_gradient(gradient, widened):
    tok_rows = gradient.shape[1]
    rows_out = [
        jnp.sum(gradient * widened[:, 6 - offset : 6 - offset + tok_rows], axis=1)
        for offset in range(7)
    ]
    return jnp.stack(rows_out, axis=0)


def to_channels(stream):
    return lax.all_to_all(stream, "seq", split_axis=0, concat_axis=1, tiled=True)


def to_tokens(stream):
    return lax.all_to_all(stream, "seq", split_axis=1, concat_axis=0, tiled=True)


def local_fft(query_in, key_in, value_in, short_weight, residue, log_rate, grad_out):
    tok_rows = query_in.shape[1]
    length = tok_rows * lax.axis_size("seq")
    scale = 1.0 / math.sqrt(length)
    tails = shifted((query_in[:, -6:], key_in[:, -6:], value_in[:, -6:]), "seq", 1)
    query_wide = jnp.concatenate([tails[0], query_in], axis=1).astype(jnp.float32)
    key_wide = jnp.concatenate([tails[1], key_in], axis=1).astype(jnp.float32)
    value_wide = jnp.concatenate([tails[2], value_in], axis=1).astype(jnp.float32)
    query_hat = apply_taps(query_wide, short_weight[0], tok_rows)
    key_hat = apply_taps(key_wide, short_weight[1], tok_rows)
    value_hat = apply_taps(value_wide, short_weight[2], tok_rows)
    mixed = (key_hat * value_hat).astype(jnp.bfloat16)
    grad_up = grad_out.astype(jnp.float32)
    grad_mixed = (grad_up * query_hat).astype(jnp.bfloat16)
    mixed_cols = to_channels(mixed)
    filt = modal_filter(residue, log_rate, length)
    spec_filter, spec_mixed = paired_spectra(filt, mixed_cols)
    long_out = to_time(spectral_product(spec_mixed, spec_filter, False), length).astype(
        jnp.bfloat16
    )
    conv_out = to_tokens(long_out)
    grad_cols = to_channels(grad_mixed)
    spec_grad = spectrum(grad_cols)
    long_grad, filt_grad = paired_time(
        spectral_product(spec_grad, spec_filter, True),
        spectral_product(spec_grad, spec_mixed, True),
        length,
    )
    conv_grad = to_tokens(long_grad.astype(jnp.bfloat16))
    grad_res, grad_log = modal_grads(filt_grad, residue, log_rate)
    conv_wide = conv_out.astype(jnp.float32)
    conv_grad_wide = conv_grad.astype(jnp.float32)
    output = (query_hat * conv_wide).astype(jnp.bfloat16)
    grad_q = grad_up * conv_wide
    grad_k = conv_grad_wide * value_hat
    grad_v = conv_grad_wide * key_hat
    heads = shifted((grad_q[:, :6], grad_k[:, :6], grad_v[:, :6]), "seq", -1)
    grad_query = taps_back(grad_q, heads[0], short_weight[0]).astype(jnp.bfloat16)
    grad_key = taps_back(grad_k, heads[1], short_weight[1]).astype(jnp.bfloat16)
    grad_value = taps_back(grad_v, heads[2], short_weight[2]).astype(jnp.bfloat16)
    local_terms = jnp.stack(
        [
            taps_gradient(grad_q, query_wide),
            taps_gradient(grad_k, key_wide),
            taps_gradient(grad_v, value_wide),
        ],
        axis=0,
    )
    grad_short = lax.psum(local_terms, "seq") * scale
    return (
        output,
        grad_query,
        grad_key,
        grad_value,
        grad_short,
        grad_res * scale,
        grad_log * scale,
    )


SUB = 8
LANE = 128
HALO = 6
TAPS = 7
GROUP = 8
MESH = pl.DeviceIdType.MESH


def slab(index):
    return pl.ds(pl.multiple_of(index * SUB, SUB), SUB)


def layer_kernel(
    n, modes, tokens, scale,
    query_ref, key_ref, value_ref, grad_ref, weight_ref, rate_ref, residue_ref,
    out_ref, gq_ref, gk_ref, gv_ref, short_ref, res_ref, log_ref,
    inputs, results, tails, heads, tails_in, heads_in, param_ref, streams, hats, mixed, gmixed, conv, conv_back, prod, cots,
    weights, params, decay, gain, rate,
    edge_send, edge_recv, acc_hold, acc_send, acc_recv,
    carry_hold, carry_send, carry_recv, modal_send, modal_recv, short_send, short_recv, total_send, total_recv, totals,
    load_sem, store_sem, send_sem, recv_sem, halo_send, halo_recv,
):
    me = lax.axis_index("seq")
    extent = tokens + HALO
    rows_all = 3 * TAPS
    owners = (rows_all + 1) // 2
    f32 = jnp.float32
    zero = jnp.zeros((SUB, LANE), f32)

    def rounded(value):
        return value.astype(jnp.bfloat16).astype(f32)

    def tree(parts):
        while len(parts) > 1:
            parts = [parts[i] + parts[i + 1] for i in range(0, len(parts), 2)]
        return parts[0]

    def per_mode(ref):
        return [ref[m * SUB : (m + 1) * SUB, :] for m in range(modes)]

    barrier = pltpu.get_barrier_semaphore()
    peers = [lax.rem(me + k, n) for k in range(1, n)]
    for peer in peers:
        pl.semaphore_signal(
            barrier, inc=1, device_id={"seq": peer}, device_id_type=MESH
        )

    half_width = SUB * LANE // 2
    loads = []
    for s, ref in enumerate((query_ref, key_ref, value_ref, grad_ref)):
        for half in range(2):
            part = pl.ds(half * half_width, half_width)
            loads.append(
                pltpu.make_async_copy(
                    ref.at[part], inputs.at[s, part], load_sem.at[2 * s + half]
                )
            )
            loads[-1].start()

    def send(phase, peer, source, target):
        pltpu.make_async_remote_copy(
            src_ref=source,
            dst_ref=target,
            send_sem=send_sem.at[phase],
            recv_sem=recv_sem.at[phase],
            device_id={"seq": peer},
            device_id_type=MESH,
        ).start()

    def sent(phase, like):
        pltpu.make_async_copy(like, like, send_sem.at[phase]).wait()

    def arrived(phase, like):
        pltpu.make_async_copy(like, like, recv_sem.at[phase]).wait()

    others = pl.ds(0, n - 1)
    param_ref[...] = jnp.concatenate([rate_ref[...], residue_ref[...]], axis=1)

    for s in range(3):
        for b in range(SUB):
            weights[pl.ds(s * TAPS * SUB + b, TAPS, stride=SUB), :] = weight_ref[
                s, :, b * LANE : (b + 1) * LANE
            ]

    eye = (
        lax.broadcasted_iota(jnp.int32, (LANE, LANE), 0)
        == lax.broadcasted_iota(jnp.int32, (LANE, LANE), 1)
    ).astype(jnp.bfloat16)

    def turned(block):
        return lax.dot_general(
            eye, block, (((1,), (1,)), ((), ())), preferred_element_type=f32
        )

    own_rows = pl.ds(pl.multiple_of(me * modes, modes), modes)
    for s in range(4):
        for b in range(0, SUB, 2):
            if b % (SUB // 2) == 0:
                loads[2 * s + b // (SUB // 2)].wait()
            block = turned(inputs[s, b * LANE : (b + 2) * LANE, :])
            for half in range(2):
                streams[s, pl.ds(HALO * SUB + b + half, tokens, stride=SUB), :] = block[
                    :, half * LANE : (half + 1) * LANE
                ]
        if s == 1:
            pl.semaphore_wait(barrier, n - 1)
            for peer in peers:
                send(0, peer, param_ref, params.at[own_rows])
            params[own_rows, :] = param_ref[...]

    edge = HALO * SUB
    last = tokens * SUB
    to_right = lambda: pltpu.make_async_remote_copy(
        src_ref=tails,
        dst_ref=tails_in,
        send_sem=halo_send.at[0],
        recv_sem=halo_recv.at[0],
        device_id={"seq": lax.rem(me + 1, n)},
        device_id_type=MESH,
    )
    to_left = lambda: pltpu.make_async_remote_copy(
        src_ref=heads,
        dst_ref=heads_in,
        send_sem=halo_send.at[1],
        recv_sem=halo_recv.at[1],
        device_id={"seq": lax.rem(me + n - 1, n)},
        device_id_type=MESH,
    )
    for s in range(3):
        tails[s] = streams[s, last : last + edge, :].astype(jnp.bfloat16)
    for s in range(4):
        heads[s] = streams[s, edge : 2 * edge, :].astype(jnp.bfloat16)

    @pl.when(me < n - 1)
    def _():
        to_right().start()

    @pl.when(me > 0)
    def _():
        to_left().start()

    taps = [
        [weights[(s * TAPS + j) * SUB : (s * TAPS + j + 1) * SUB, :] for j in range(TAPS)]
        for s in range(3)
    ]

    def filter_token(t):
        vals = []
        for s in range(3):
            total = taps[s][0] * streams[s, slab(t + HALO), :]
            for j in range(1, TAPS):
                total = total + taps[s][j] * streams[s, slab(t + HALO - j), :]
            hats[s, slab(t), :] = total
            vals.append(total)
        mixed[slab(t), :] = rounded(vals[1] * vals[2])
        gmixed[slab(t), :] = rounded(vals[0] * streams[3, slab(t + HALO), :])

    def token_loop(lo, hi, unroll, fn):
        def step(i, carry):
            for u in range(unroll):
                fn(lo + i * unroll + u)
            return carry

        lax.fori_loop(0, (hi - lo) // unroll, step, 0)

    token_loop(HALO, tokens, 2, filter_token)

    arrived(0, params.at[pl.ds(0, (n - 1) * modes)])
    low_half = lax.broadcasted_iota(jnp.int32, (SUB, LANE), 1) < LANE // 2
    for m in range(modes):
        even = params[pl.ds(m, SUB, stride=2 * modes), :]
        odd = params[pl.ds(modes + m, SUB, stride=2 * modes), :]
        log_rate = jnp.where(low_half, even, pltpu.roll(odd, LANE // 2, 1))
        residue = jnp.where(low_half, pltpu.roll(even, LANE // 2, 1), odd)
        r = jnp.exp(log_rate)
        rate[slab(m), :] = r
        decay[slab(m), :] = jnp.exp(-r)
        gain[slab(m), :] = residue * jnp.sqrt(2.0 * r)

    UN = 4
    decays = per_mode(decay)

    def edge_step(i, carry):
        x, z = [list(c) for c in carry]
        for u in range(2):
            t = i * 2 + u
            value = mixed[slab(t + HALO), :]
            cot = gmixed[slab(tokens - 1 - t), :]
            for m in range(modes):
                x[m] = decays[m] * x[m] + value
                z[m] = decays[m] * z[m] + cot
        return tuple(x), tuple(z)

    inner = tokens - HALO
    x, z = lax.fori_loop(0, inner // 2, edge_step, ((zero,) * modes,) * 2)
    @pl.when(me > 0)
    def _():
        to_left().wait_send()
        to_right().wait_recv()
        for s in range(3):
            streams[s, 0:edge, :] = tails_in[s].astype(f32)

    @pl.when(me == 0)
    def _():
        streams[0:3, 0:edge, :] = jnp.zeros((3, edge, LANE), f32)

    @pl.when(me < n - 1)
    def _():
        to_right().wait_send()
        to_left().wait_recv()
        for s in range(4):
            streams[s, edge + last : 2 * edge + last, :] = heads_in[s].astype(f32)

    @pl.when(me == n - 1)
    def _():
        streams[:, edge + last : 2 * edge + last, :] = jnp.zeros((4, edge, LANE), f32)

    token_loop(0, HALO, 2, filter_token)
    token_loop(tokens, extent, 2, filter_token)

    x, z = list(x), list(z)
    for m in range(modes):
        early = zero
        for t in range(HALO):
            back = HALO - 1 - t
            early = decays[m] * early + mixed[t * SUB : (t + 1) * SUB, :]
            z[m] = decays[m] * z[m] + gmixed[back * SUB : (back + 1) * SUB, :]
        x[m] = x[m] + jnp.exp(-float(inner) * rate[m * SUB : (m + 1) * SUB, :]) * early
    for m in range(modes):
        edge_send[m] = jnp.concatenate([x[m], z[m]], axis=0).astype(jnp.bfloat16)
    for peer in peers:
        send(1, peer, edge_send.at[peer], edge_recv.at[me])
    edge_recv[me] = edge_send[me]

    for first in range(0, modes, GROUP):
        group = range(first, first + GROUP)

        def fwd_step(i, carry, first=first, group=group):
            x, y, ax, ay = [list(c) for c in carry]
            for u in range(UN):
                t = i * UN + u
                value = mixed[slab(t), :]
                cot = gmixed[slab(t), :]
                parts = []
                for p, m in enumerate(group):
                    a = decay[m * SUB : (m + 1) * SUB, :]
                    y[p] = a * (y[p] + x[p])
                    x[p] = a * x[p] + value
                    parts.append(gain[m * SUB : (m + 1) * SUB, :] * x[p])
                    ax[p] = ax[p] + cot * x[p]
                    ay[p] = ay[p] + cot * y[p]
                total = tree(parts)
                conv[slab(t), :] = conv[slab(t), :] + total if first else total
            return tuple(tuple(c) for c in (x, y, ax, ay))

        zeros = tuple(zero for _ in group)
        x, y, ax, ay = lax.fori_loop(0, tokens // UN, fwd_step, (zeros,) * 4)
        for p, m in enumerate(group):
            acc_hold[m, 0:SUB, :] = y[p]
            acc_hold[m, 2 * SUB : 3 * SUB, :] = ax[p]
            acc_hold[m, 3 * SUB : 4 * SUB, :] = ay[p]
        x = list(x)
        for t in range(tokens, extent):
            value = mixed[t * SUB : (t + 1) * SUB, :]
            total = conv[t * SUB : (t + 1) * SUB, :] if first else zero
            for p, m in enumerate(group):
                x[p] = decay[m * SUB : (m + 1) * SUB, :] * x[p] + value
                total = total + gain[m * SUB : (m + 1) * SUB, :] * x[p]
            conv[t * SUB : (t + 1) * SUB, :] = total

    my_rate = rate[slab(me), :]
    my_decay = decay[slab(me), :]
    my_gain = gain[slab(me), :]
    whole = jnp.exp(-float(tokens) * my_rate)
    arrived(1, edge_recv.at[others])
    h, z = zero, zero
    for d in range(n):
        back = n - 1 - d
        carry_hold[d, 0:SUB, :] = h
        carry_hold[back, SUB : 2 * SUB, :] = z
        h = whole * h + edge_recv[d].astype(f32)[0:SUB]
        z = whole * z + edge_recv[back].astype(f32)[SUB : 2 * SUB]
    for d in range(n):
        carry_send[d] = carry_hold[d].astype(jnp.bfloat16)
    for peer in peers:
        send(2, peer, carry_send.at[peer], carry_recv.at[me])
    carry_recv[me] = carry_send[me]

    for first in range(0, modes, GROUP):
        group = range(first, first + GROUP)

        def bwd_step(i, carry, first=first, group=group):
            z, w = [list(c) for c in carry]
            for u in range(UN):
                t = tokens - 1 - (i * UN + u)
                cot = gmixed[slab(t), :]
                parts = []
                for p, m in enumerate(group):
                    a = decay[m * SUB : (m + 1) * SUB, :]
                    z[p] = a * z[p] + cot
                    w[p] = a * w[p] + z[p]
                    parts.append(gain[m * SUB : (m + 1) * SUB, :] * z[p])
                total = tree(parts)
                conv_back[slab(t), :] = conv_back[slab(t), :] + total if first else total
            return tuple(tuple(c) for c in (z, w))

        zeros = tuple(zero for _ in group)
        z, w = lax.fori_loop(0, tokens // UN, bwd_step, (zeros,) * 2)
        for p, m in enumerate(group):
            acc_hold[m, SUB : 2 * SUB, :] = w[p]

    for m in range(modes):
        acc_send[m] = acc_hold[m].astype(jnp.bfloat16)
    for peer in peers:
        send(3, peer, acc_send.at[peer], acc_recv.at[me])
    acc_recv[me] = acc_send[me]

    arrived(2, carry_recv.at[others])
    gains = per_mode(gain)
    carried = [carry_recv[m].astype(f32) for m in range(modes)]

    def fwd_two(i, c):
        c = list(c)
        for u in range(2):
            t = i * 2 + u
            c = [decays[m] * c[m] for m in range(modes)]
            total = rounded(conv[slab(t), :] + tree(c))
            prod[slab(t), :] = hats[0, slab(t), :] * total
            cots[0, slab(t), :] = streams[3, slab(t + HALO), :] * total
        return tuple(c)

    start = tuple(gains[m] * carried[m][0:SUB] for m in range(modes))
    lax.fori_loop(0, extent // 2, fwd_two, start)

    def store_back(t, total):
        total = rounded(total)
        cots[1, slab(t), :] = hats[2, slab(t), :] * total
        cots[2, slab(t), :] = hats[1, slab(t), :] * total

    def bwd_two(i, c):
        c = list(c)
        for u in range(2):
            t = tokens - 1 - (i * 2 + u)
            c = [decays[m] * c[m] for m in range(modes)]
            store_back(t, conv_back[slab(t), :] + tree(c))
        return tuple(c)

    start = tuple(gains[m] * carried[m][SUB : 2 * SUB] for m in range(modes))
    lax.fori_loop(0, tokens // 2, bwd_two, start)

    ahead = [zero] * HALO
    for m in range(modes):
        grow = jnp.exp(rate[m * SUB : (m + 1) * SUB, :])
        z = carry_recv[m].astype(f32)[SUB : 2 * SUB]
        for h in range(HALO):
            ahead[h] = ahead[h] + gains[m] * z
            z = grow * (z - gmixed[(tokens + h) * SUB : (tokens + h + 1) * SUB, :])
    for h in range(HALO):
        store_back(tokens + h, ahead[h])

    def short_step(i, accs):
        accs = list(accs)
        for u in range(2):
            t = i * 2 + u
            for s in range(3):
                cot = cots[s, slab(t), :]
                for j in range(TAPS):
                    at = s * TAPS + j
                    accs[at] = accs[at] + cot * streams[s, slab(t + HALO - j), :]
        return tuple(accs)

    accs = lax.fori_loop(0, tokens // 2, short_step, (zero,) * rows_all)
    accs = list(accs) + [zero] * (2 * owners - rows_all)
    for o in range(owners):
        both = jnp.concatenate(accs[2 * o : 2 * o + 2], axis=0)
        short_send[o] = both.astype(jnp.bfloat16)
    for peer in peers:

        @pl.when(peer < owners)
        def _(peer=peer):
            send(5, peer, short_send.at[peer], short_recv.at[me])

    @pl.when(me < owners)
    def _():
        short_recv[me] = short_send[me]

    arrived(3, acc_recv.at[others])
    hy, acc_x, acc_y = zero, zero, zero
    for d in range(n):
        h = carry_hold[d, 0:SUB, :]
        terms = acc_recv[d].astype(f32)
        z0 = my_decay * edge_recv[d].astype(f32)[SUB : 2 * SUB]
        z1 = my_decay * terms[SUB : 2 * SUB]
        acc_x = acc_x + (terms[2 * SUB : 3 * SUB] + h * z0)
        acc_y = acc_y + (terms[3 * SUB : 4 * SUB] + h * z1 + hy * z0)
        hy = whole * (hy + float(tokens) * h) + terms[0:SUB]
    grad_res = acc_x * jnp.sqrt(2.0 * my_rate) * scale
    grad_log = my_gain * (0.5 * acc_x - my_rate * acc_y) * scale
    for b in range(SUB):
        modal_send[b, 0:1, :] = grad_res[b : b + 1, :]
        modal_send[b, 1:2, :] = grad_log[b : b + 1, :]
    for peer in peers:
        send(4, peer, modal_send.at[lax.div(peer, 2)], modal_recv.at[me])
    modal_recv[me] = modal_send[lax.div(me, 2)]

    def taps_step(t):
        for s in range(3):
            total = taps[s][0] * cots[s, slab(t), :]
            for j in range(1, TAPS):
                total = total + taps[s][j] * cots[s, slab(t + j), :]
            hats[s, slab(t), :] = total

    token_loop(0, tokens, 2, taps_step)

    @pl.when(me < owners)
    def _():
        arrived(5, short_recv.at[others])
        total = short_recv[0].astype(f32)
        for d in range(1, n):
            total = total + short_recv[d].astype(f32)
        total_send[...] = (total * scale).astype(jnp.bfloat16)
        for peer in peers:
            send(6, peer, total_send, total_recv.at[me])
        total_recv[me] = total_send[...]

    stores = []
    outs = (out_ref, gq_ref, gk_ref, gv_ref)
    for first in (0, 2):
        for b in range(SUB):
            rows = pl.ds(b, tokens, stride=SUB)
            one = hats[first - 1, rows, :] if first else prod[rows, :]
            block = jnp.concatenate([one, hats[first, rows, :]], axis=0)
            block = turned(block.astype(jnp.bfloat16)).astype(jnp.bfloat16)
            for half in range(2):
                results[first + half, b * LANE : (b + 1) * LANE, :] = block[
                    :, half * LANE : (half + 1) * LANE
                ]
        for s in (first, first + 1):
            stores.append(pltpu.make_async_copy(results.at[s], outs[s], store_sem.at[s]))
            stores[-1].start()

    arrived(4, modal_recv.at[others])
    odd_owner = lax.rem(me, 2) == 1
    for at, ref in ((0, res_ref), (1, log_ref)):
        table = jnp.concatenate([modal_recv[m, at : at + 1, :] for m in range(modes)], axis=0)
        table = jnp.where(odd_owner, pltpu.roll(table, LANE // 2, 1), table)
        ref[...] = table[:, : LANE // 2]

    @pl.when(me < owners)
    def _():
        arrived(6, total_recv.at[pl.ds(0, owners - 1)])
        sent(5, short_recv.at[pl.ds(0, owners - 1)])
        sent(6, short_recv.at[others])

    @pl.when(me >= owners)
    def _():
        arrived(6, total_recv)
        sent(5, short_recv.at[pl.ds(0, owners)])

    for o in range(owners):
        totals[2 * o * SUB : 2 * (o + 1) * SUB, :] = total_recv[o].astype(f32)
    for s in range(3):
        for b in range(SUB):
            short_ref[s, :, b * LANE : (b + 1) * LANE] = totals[
                pl.ds(s * TAPS * SUB + b, TAPS, stride=SUB), :
            ]

    for store in stores:
        store.wait()
    sent(0, params.at[pl.ds(0, (n - 1) * modes)])
    sent(1, edge_recv.at[others])
    sent(2, carry_recv.at[others])
    sent(3, acc_recv.at[others])
    sent(4, modal_recv.at[others])


def hand_over(count, *refs):
    sources, targets, held = refs[:count], refs[count : 2 * count], refs[2 * count : -2]
    load_sem, store_sem = refs[-2:]
    loads = [
        pltpu.make_async_copy(sources[i], held[i], load_sem.at[i]) for i in range(count)
    ]
    stores = [
        pltpu.make_async_copy(held[i], targets[i], store_sem.at[i]) for i in range(count)
    ]
    for load in loads:
        load.start()
    for load, store in zip(loads, stores):
        load.wait()
        store.start()
    for store in stores:
        store.wait()


def local(query_in, key_in, value_in, short_weight, residue, log_rate, grad_out):
    n = lax.axis_size("seq")
    width, tokens = query_in.shape
    own, modes = residue.shape
    fits = width == SUB * LANE and tokens == LANE and modes == n == 2 * SUB
    if not (fits and own == LANE // 2):
        return local_fft(
            query_in, key_in, value_in, short_weight, residue, log_rate, grad_out
        )
    scale = 1.0 / math.sqrt(tokens * n)
    f32 = jnp.float32
    rows = (tokens + HALO) * SUB
    owners = (3 * TAPS + 1) // 2
    vmem = pl.BlockSpec(memory_space=pltpu.VMEM)
    hbm = pl.BlockSpec(memory_space=pltpu.MemorySpace.HBM)
    pair = pltpu.VMEM((n, 2 * SUB, LANE), f32)
    quad = pltpu.VMEM((n, 4 * SUB, LANE), f32)
    half_pair = pltpu.VMEM((n, 2 * SUB, LANE), jnp.bfloat16)
    half_quad = pltpu.VMEM((n, 4 * SUB, LANE), jnp.bfloat16)
    tail = pltpu.VMEM((3, HALO * SUB, LANE), jnp.bfloat16)
    head = pltpu.VMEM((4, HALO * SUB, LANE), jnp.bfloat16)
    flat = pltpu.VMEM((rows, LANE), f32)
    triple = pltpu.VMEM((3, rows, LANE), f32)
    small = pltpu.VMEM((modes * SUB, LANE), f32)
    shape = jax.ShapeDtypeStruct((width, tokens), jnp.bfloat16)
    modal = jax.ShapeDtypeStruct((modes, own), f32)
    results = pl.pallas_call(
        functools.partial(layer_kernel, n, modes, tokens, scale),
        out_shape=(
            shape, shape, shape, shape,
            jax.ShapeDtypeStruct(short_weight.shape, f32), modal, modal,
        ),
        in_specs=[hbm] * 4 + [vmem] * 3,
        out_specs=(hbm,) * 4 + (vmem,) * 3,
        scratch_shapes=[
            pltpu.VMEM((4, width, tokens), jnp.bfloat16),
            pltpu.VMEM((4, width, tokens), jnp.bfloat16),
            tail, head, tail, head,
            pltpu.VMEM((modes, LANE), f32),
            pltpu.VMEM((4, rows + HALO * SUB, LANE), f32),
            triple, flat, flat, flat, flat, flat, triple,
            pltpu.VMEM((3 * TAPS * SUB, LANE), f32),
            pltpu.VMEM((n * modes, LANE), f32),
            small, small, small,
            half_pair, half_pair, quad, half_quad, half_quad,
            pair, half_pair, half_pair,
            pltpu.VMEM((SUB, 2, LANE), f32),
            pltpu.VMEM((n, 2, LANE), f32),
            pltpu.VMEM((owners, 2 * SUB, LANE), jnp.bfloat16),
            half_pair,
            pltpu.VMEM((2 * SUB, LANE), jnp.bfloat16),
            pltpu.VMEM((owners, 2 * SUB, LANE), jnp.bfloat16),
            pltpu.VMEM((owners * 2 * SUB, LANE), f32),
            pltpu.SemaphoreType.DMA((8,)),
            pltpu.SemaphoreType.DMA((4,)),
            pltpu.SemaphoreType.DMA((7,)),
            pltpu.SemaphoreType.DMA((7,)),
            pltpu.SemaphoreType.DMA((2,)),
            pltpu.SemaphoreType.DMA((2,)),
        ],
        compiler_params=pltpu.CompilerParams(
            collective_id=0, has_side_effects=True, vmem_limit_bytes=56 * 2**20
        ),
    )(query_in, key_in, value_in, grad_out, short_weight, log_rate.T, residue.T)
    count = len(results)
    results = pl.pallas_call(
        functools.partial(hand_over, count),
        out_shape=[jax.ShapeDtypeStruct(r.shape, r.dtype) for r in results],
        in_specs=[hbm] * count,
        out_specs=[hbm] * count,
        scratch_shapes=[pltpu.VMEM(r.shape, r.dtype) for r in results]
        + [pltpu.SemaphoreType.DMA((count,))] * 2,
        compiler_params=pltpu.CompilerParams(vmem_limit_bytes=60 * 2**20),
    )(*results)
    return (*results[:5], results[5].T, results[6].T)


def solution(mesh):
    return jax.shard_map(
        local,
        mesh=mesh,
        in_specs=(
            P("chan", "seq"),
            P("chan", "seq"),
            P("chan", "seq"),
            P(None, None, "chan"),
            P(("chan", "seq"), None),
            P(("chan", "seq"), None),
            P("chan", "seq"),
        ),
        out_specs=(
            P("chan", "seq"),
            P("chan", "seq"),
            P("chan", "seq"),
            P("chan", "seq"),
            P(None, None, "chan"),
            P(("chan", "seq"), None),
            P(("chan", "seq"), None),
        ),
        check_vma=False,
    )
```
